512 devices in a mesh: gx: 16 (over z), gy: 16 (over y, x), gz: 2 (over core).
Axes of the slice: x: 4, y: 4, z: 16, core: 2. Of those that a mesh axis runs over, the one named last changes fastest.
Arguments:
- source: float32 [128, 512, 256], P('gx', 'gy', 'gz'), may hold values from -8 to 8, as said below
- beta_cells: float32 [128, 512, 256], P('gx', 'gy', 'gz'), may hold values from 0.25 to 4
- target: int32 [16, 16, 2], P('gx', 'gy', 'gz'), may hold values from 0 to 15
Outputs:
- solution: float32 [128, 512, 256], P('gx', 'gy', 'gz')
The draws below stay inside these ranges and needn't reach their ends.
Inputs may be any that keep to these rules, and one draw needn't show every extreme that they name: source is a real field of order one.
All inputs are finite; a program needn't handle non-finite values.
Results may differ from the reference program's by a relative error of at most 0.0001.
Values sent between devices are 32-bit elements; how exact they have to be, the bound alone decides.
A program may use at most 64 MiB of HBM per device.

```python
import math
import jax
import jax.numpy as jnp
from jax import lax

BOTTOM = 6
NX = 128
NY = 512
NZ = 256
N_GX = 16
N_GY = 16
N_GZ = 2


def draw_source(key, part):
    key = jax.random.fold_in(key, 11)
    values = 2.0 * jax.random.normal(key, (NX, NY, NZ), jnp.float32)
    return jnp.clip(values, -8.0, 8.0)


def touch_ends(values, key, low, top_value):
    spot = [jax.random.randint(jax.random.fold_in(key, axis), (), 0, length) for axis, length in enumerate(values.shape)]
    longest = values.shape.index(max(values.shape))
    next_to = spot[:longest] + [(spot[longest] + 1) % values.shape[longest]] + spot[longest + 1:]
    return values.at[tuple(spot)].set(low).at[tuple(next_to)].set(top_value)


def level_of(key, dims, cuts, low, top_value):
    loudness, own = 1.0, jax.random.fold_in(key, 6)
    for axis_at, shards_of in cuts:
        heights = jnp.exp(jax.random.uniform(jax.random.fold_in(own, axis_at), (shards_of,), jnp.float32, low / len(cuts), top_value / len(cuts)))
        loudness = loudness * jnp.repeat(heights, dims[axis_at] // shards_of).reshape([-1 if axis == axis_at else 1 for axis in range(len(dims))])
    return loudness


def setup_inputs(seed: int = 0) -> dict:
    splits = jax.random.split(jax.random.key(seed), 4)
    source = draw_source(jax.random.fold_in(splits[3], 71), 0)
    beta_cells = jnp.clip(jnp.exp(math.log(4.0) - 2.7725887 * jax.random.uniform(splits[1], (NX, NY, NZ), jnp.float32) ** level_of(splits[1], (NX, NY, NZ), ((0, 16), (1, 16), (2, 2)), -0.2, 0.2)), 0.25, 4.0)
    target = touch_ends(jax.random.randint(splits[2], (N_GX, N_GY, N_GZ), 0, N_GX), jax.random.fold_in(splits[2], 1), 0, N_GX - 1).astype(jnp.int32)
    return dict(source=source, beta_cells=beta_cells, target=target)


WEIGHT = 0.8


def pad_cells(field):
    widths = [(0, 0)] * (field.ndim - 3) + [(1, 1)] * 3
    return jnp.pad(field, widths)


def face_terms(padded_val, padded_coef):
    center_val = padded_val[..., 1:-1, 1:-1, 1:-1]
    center_coef = padded_coef[..., 1:-1, 1:-1, 1:-1]
    neighbours = [
        (padded_val[..., :-2, 1:-1, 1:-1], padded_coef[..., :-2, 1:-1, 1:-1]),
        (padded_val[..., 2:, 1:-1, 1:-1], padded_coef[..., 2:, 1:-1, 1:-1]),
        (padded_val[..., 1:-1, :-2, 1:-1], padded_coef[..., 1:-1, :-2, 1:-1]),
        (padded_val[..., 1:-1, 2:, 1:-1], padded_coef[..., 1:-1, 2:, 1:-1]),
        (padded_val[..., 1:-1, 1:-1, :-2], padded_coef[..., 1:-1, 1:-1, :-2]),
        (padded_val[..., 1:-1, 1:-1, 2:], padded_coef[..., 1:-1, 1:-1, 2:]),
    ]
    weight_sum = jnp.zeros_like(center_coef)
    flux_sum = jnp.zeros_like(center_val)
    for near_val, near_coef in neighbours:
        face_value = 0.5 * (center_coef + near_coef)
        weight_sum = weight_sum + face_value
        flux_sum = flux_sum + face_value * (center_val - near_val)
    return center_val, weight_sum, flux_sum


def relax_cells(padded_val, padded_coef, rhs_field, factor, spare_term):
    center_val, weight_sum, flux_sum = face_terms(padded_val, padded_coef)
    return center_val + WEIGHT * (rhs_field - factor * flux_sum) / (factor * weight_sum + spare_term)


def residual(padded_val, padded_coef, rhs_field, factor):
    center_val, weight_sum, flux_sum = face_terms(padded_val, padded_coef)
    return rhs_field - factor * flux_sum


def restrict(field):
    size_a, size_b, size_c = field.shape
    return field.reshape(size_a // 2, 2, size_b // 2, 2, size_c // 2, 2).mean(axis=(1, 3, 5))


def prolong(field):
    size_a, size_b, size_c = field.shape
    spread = jnp.broadcast_to(field[:, None, :, None, :, None], (size_a, 2, size_b, 2, size_c, 2))
    return spread.reshape(2 * size_a, 2 * size_b, 2 * size_c)


def bottom_solve(rhs_field, coefficient, inside):
    spare_term = 1.0 - inside
    padded_coef = pad_cells(coefficient)
    total = jnp.sum(rhs_field, axis=(-3, -2, -1), keepdims=True)
    count = jnp.sum(inside, axis=(-3, -2, -1), keepdims=True)
    mean_src = total / jnp.maximum(count, 1.0)
    approx = inside * (4.0 * mean_src)
    for number in range(BOTTOM):
        approx = inside * relax_cells(pad_cells(approx), padded_coef, rhs_field, 0.0625, spare_term)
    return approx


def coarse_rows(low_src, low_coef, target):
    boxes_x, boxes_y, boxes_z = target.shape
    cells_x = low_src.shape[0] // boxes_x
    cells_y = low_src.shape[1] // boxes_y
    cells_z = low_src.shape[2] // boxes_z

    def to_rows(field):
        return field.reshape(boxes_x * cells_x, boxes_y, cells_y, boxes_z, cells_z).transpose(1, 3, 0, 2, 4)

    owner_map = jnp.repeat(target.transpose(1, 2, 0), cells_x, axis=2)[..., None, None]
    src_rows = to_rows(low_src)
    coef_rows = to_rows(low_coef)

    def add_target(target_value, summed):
        inside = jnp.broadcast_to((owner_map == target_value).astype(jnp.float32), src_rows.shape)
        return summed + bottom_solve(src_rows * inside, coef_rows * inside, inside)

    summed = lax.fori_loop(0, boxes_x, add_target, jnp.zeros_like(src_rows))
    return summed.transpose(2, 0, 3, 1, 4).reshape(boxes_x * cells_x, boxes_y * cells_y, boxes_z * cells_z)


def reference(source, beta_cells, target):
    fine_pad = pad_cells(beta_cells)
    fine_sol = relax_cells(pad_cells(jnp.zeros_like(source)), fine_pad, source, 1.0, 0.0)
    fine_sol = relax_cells(pad_cells(fine_sol), fine_pad, source, 1.0, 0.0)
    fine_res = residual(pad_cells(fine_sol), fine_pad, source, 1.0)
    mid_src = restrict(fine_res)
    mid_coef = restrict(beta_cells)
    mid_pad = pad_cells(mid_coef)
    mid_sol = relax_cells(pad_cells(jnp.zeros_like(mid_src)), mid_pad, mid_src, 0.25, 0.0)
    mid_sol = relax_cells(pad_cells(mid_sol), mid_pad, mid_src, 0.25, 0.0)
    mid_res = residual(pad_cells(mid_sol), mid_pad, mid_src, 0.25)
    low_src = restrict(mid_res)
    low_coef = restrict(mid_coef)
    bottom_corr = coarse_rows(low_src, low_coef, target)
    mid_sol = mid_sol + prolong(bottom_corr)
    mid_sol = relax_cells(pad_cells(mid_sol), mid_pad, mid_src, 0.25, 0.0)
    mid_sol = relax_cells(pad_cells(mid_sol), mid_pad, mid_src, 0.25, 0.0)
    fine_sol = fine_sol + prolong(mid_sol)
    fine_sol = relax_cells(pad_cells(fine_sol), fine_pad, source, 1.0, 0.0)
    fine_sol = relax_cells(pad_cells(fine_sol), fine_pad, source, 1.0, 0.0)
    return fine_sol
```

```python
import jax
import jax.numpy as jnp
from jax import lax
from jax.experimental import pallas as pl
from jax.experimental.pallas import tpu as pltpu
from jax.sharding import PartitionSpec as P


BOTTOM = 6
RELAX = 0.8
F32 = jnp.float32
MESH = pl.DeviceIdType.MESH
NEAR = 4


def lanes_of(rows):
    return lax.broadcasted_iota(jnp.int32, (rows, 128), 1)


def beside(left_tile, right_tile, step):
    lane = lanes_of(left_tile.shape[0])
    low0, low1 = pltpu.roll(left_tile, step, 1), pltpu.roll(right_tile, step, 1)
    high0, high1 = pltpu.roll(left_tile, 128 - step, 1), pltpu.roll(right_tile, 128 - step, 1)
    below = (low0, jnp.where(lane < step, low0, low1))
    above = (jnp.where(lane >= 128 - step, high1, high0), high1)
    return below, above


def make_faces(x, coef, faces, row, rows, step):
    fx, fy, fl, fr, weight, ease = faces
    at = pl.ds(row, rows)
    own = [coef[x, t, at, :] for t in range(2)]
    below, above = beside(*own, step)
    lane = lanes_of(rows)
    for t in range(2):
        c = own[t]
        low = jnp.where(lane < step, 0.0, below[0]) if t == 0 else below[1]
        high = jnp.where(lane >= 128 - step, 0.0, above[1]) if t == 1 else above[0]
        x_low = c + coef[x - 1, t, at, :]
        y_low = c + coef[x, t, pl.ds(row - 1, rows), :]
        z_low, z_high = c + low, c + high
        total = (
            x_low
            + (c + coef[x + 1, t, at, :])
            + y_low
            + (c + coef[x, t, pl.ds(row + 1, rows), :])
            + z_low
            + z_high
        )
        fx[x, t, at, :] = x_low
        fy[x, t, at, :] = y_low
        fl[x, t, at, :] = jnp.where(lane < step, 0.0, z_low) if t == 0 else z_low
        fr[x, t, at, :] = jnp.where(lane >= 128 - step, 0.0, z_high) if t == 1 else z_high
        weight[x, t, at, :] = total
        ease[x, t, at, :] = jnp.where(c > 0.0, RELAX / total, 0.0)


def last_face(x, coef, faces, row, rows):
    at = pl.ds(row, rows)
    for t in range(2):
        faces[0][x, t, at, :] = coef[x, t, at, :] + coef[x - 1, t, at, :]


def pull(x, field, faces, row, rows, step):
    fx, fy, fl, fr = faces[:4]
    at = pl.ds(row, rows)
    own = [field[x, t, at, :] for t in range(2)]
    below, above = beside(*own, step)
    sums = []
    for t in range(2):
        sums.append(
            fx[x, t, at, :] * field[x - 1, t, at, :]
            + fx[x + 1, t, at, :] * field[x + 1, t, at, :]
            + fy[x, t, at, :] * field[x, t, pl.ds(row - 1, rows), :]
            + fy[x, t, pl.ds(row + 1, rows), :] * field[x, t, pl.ds(row + 1, rows), :]
            + fl[x, t, at, :] * below[t]
            + fr[x, t, at, :] * above[t]
        )
    return sums, own


def sweep(x, field, out, faces, source, gain, row, rows, step):
    at = pl.ds(row, rows)
    sums, own = pull(x, field, faces, row, rows, step)
    for t in range(2):
        out[x, t, at, :] = 0.2 * own[t] + faces[5][x, t, at, :] * (gain * source[x, t, at, :] + sums[t])


def left_over(x, field, faces, source, half, row, rows, step):
    at = pl.ds(row, rows)
    sums, own = pull(x, field, faces, row, rows, step)
    return [source[x, t, at, :] - half * (faces[4][x, t, at, :] * own[t] - sums[t]) for t in range(2)]


def pair_sum(value, step):
    lane = lanes_of(value.shape[0])
    other = jnp.where((lane // step) % 2 == 0, pltpu.roll(value, 128 - step, 1), pltpu.roll(value, step, 1))
    return value + other


def exact_dot(a, b):
    return jnp.dot(a, b, precision=lax.Precision.HIGHEST, preferred_element_type=F32)


def squeeze_matrix(part):
    src = lax.broadcasted_iota(jnp.int32, (128, 128), 0)
    dst = lax.broadcasted_iota(jnp.int32, (128, 128), 1)
    return jnp.where((src == 4 * (dst % 32)) & (dst // 32 == part), 1.0, 0.0).astype(F32)


def spread_matrix(part):
    src = lax.broadcasted_iota(jnp.int32, (128, 128), 0)
    dst = lax.broadcasted_iota(jnp.int32, (128, 128), 1)
    return jnp.where(src == 32 * part + dst // 4, 1.0, 0.0).astype(F32)


def cycle(n_gx, n_gy, src, beta, tgt, out, *scratch):
    (C, S, FX, FY, FL, FR, W, E, V1, V2, V3,
     MC, MS, MFX, MFY, MFL, MFR, MW, ME, M1, M2, M2P, M3, M4,
     RS, RC, R2, SY, Y2, SX, EB, ES, GB, GS, FB, FS, Q, SQ, PK, PF, FO,
     local, e1s, e1r, mcs, mcr, mss, msr, ebs, ebr, gs, gr, fs, fr, ys, yr, xs, xr, qs, qr, os_, or_) = scratch
    i, j, g = lax.axis_index("gx"), lax.axis_index("gy"), lax.axis_index("gz")
    fine = (FX, FY, FL, FR, W, E)
    mid = (MFX, MFY, MFL, MFR, MW, ME)

    def near_x(d):
        return lax.rem(i + d + n_gx, n_gx)

    def near_y(d):
        return lax.rem(j + d + n_gy, n_gy)

    def send(source, target, send_sem, recv_sem, where):
        pltpu.make_async_remote_copy(
            src_ref=source, dst_ref=target, send_sem=send_sem, recv_sem=recv_sem,
            device_id=where, device_id_type=MESH,
        ).start()

    def wait(ref, sem):
        pltpu.make_async_copy(ref, ref, sem).wait()

    own_rows = pl.ds(pl.multiple_of(8 * g, 8), 24)
    own_at = pl.ds(pl.multiple_of(16 - 8 * g, 8), 24)
    pltpu.make_async_copy(beta.at[:, own_rows, :], C.at[pl.ds(4, 8), g, own_at, :], local.at[0]).start()
    pltpu.make_async_copy(src.at[:, own_rows, :], S.at[pl.ds(4, 8), g, own_at, :], local.at[1]).start()

    barrier = pltpu.get_barrier_semaphore()
    side = 2 * g - 1
    count = 0
    for d in range(1, n_gx):
        for core in range(2):
            pl.semaphore_signal(barrier, inc=1, device_id=(near_x(d), j, core), device_id_type=MESH)
            count += 1
    for dx in (-1, 0, 1):
        for core in range(2):
            pl.semaphore_signal(barrier, inc=1, device_id=(near_x(dx), near_y(side), core), device_id_type=MESH)
            count += 1
    pl.semaphore_signal(barrier, inc=1, device_id=(i, j, 1 - g), device_id_type=MESH)
    pl.semaphore_wait(barrier, count + 1)

    for index, (field, target, deep) in enumerate(((beta, C, 4), (src, S, 3))):
        ss, rs = e1s.at[index], e1r.at[index]
        for dx in (1, -1):
            part = pl.ds(8 - deep, deep) if dx == 1 else pl.ds(0, deep)
            place = pl.ds(4 - deep, deep) if dx == 1 else pl.ds(12, deep)
            for core in range(2):
                dy = 1 if core == 0 else -1
                send(field.at[part, pl.ds(24 if core == 0 else 0, 8), :],
                     target.at[place, g, pl.ds(8 if core == 0 else 32, 8), :], ss, rs,
                     (near_x(dx), near_y(dy), core))
                send(field.at[part, pl.ds(8 * core, 24), :],
                     target.at[place, g, pl.ds(16 - 8 * core, 24), :], ss, rs, (near_x(dx), j, core))
        for core in range(2):
            dy = 1 if core == 0 else -1
            send(field.at[:, pl.ds(24 if core == 0 else 0, 8), :],
                 target.at[pl.ds(4, 8), g, pl.ds(8 if core == 0 else 32, 8), :], ss, rs, (i, near_y(dy), core))
        send(field.at[:, pl.ds(pl.multiple_of(8 - 8 * g, 8), 24), :],
             target.at[pl.ds(4, 8), g, pl.ds(pl.multiple_of(8 + 8 * g, 8), 24), :], ss, rs, (i, j, 1 - g))

    c_bytes = C.at[pl.ds(0, 13), :, pl.ds(0, 32), :]
    s_bytes = S.at[pl.ds(0, 11), :, pl.ds(0, 32), :]
    wait(beta.at[:, pl.ds(0, 24), :], local.at[0])
    wait(c_bytes, e1r.at[0])

    @pl.when(i == 0)
    def _():
        C[pl.ds(0, 4)] = jnp.zeros((4, *C.shape[1:]), F32)

    @pl.when(i == n_gx - 1)
    def _():
        C[pl.ds(12, 4)] = jnp.zeros((4, *C.shape[1:]), F32)

    @pl.when((j == 0) & (g == 0))
    def _():
        C[:, :, pl.ds(8, 8), :] = jnp.zeros((16, 2, 8, 128), F32)

    @pl.when((j == n_gy - 1) & (g == 1))
    def _():
        C[:, :, pl.ds(32, 8), :] = jnp.zeros((16, 2, 8, 128), F32)

    def mid_coefficient(m, _):
        for t in range(2):
            RC[m, t] = C[4 + 2 * m, t, pl.ds(8, 32), :] + C[5 + 2 * m, t, pl.ds(8, 32), :]
            two = RC[m, t, pl.ds(0, 16, stride=2), :] + RC[m, t, pl.ds(1, 16, stride=2), :]
            MC[m + 3, t, pl.ds(8, 16), :] = 0.125 * pair_sum(two, 1)
        return 0

    lax.fori_loop(0, 4, mid_coefficient, 0)
    mid_rows = pl.ds(8, 16)
    send(MC.at[pl.ds(4, 3), :, mid_rows, :], MC.at[pl.ds(0, 3), :, mid_rows, :], mcs, mcr, (near_x(1), j, g))
    send(MC.at[pl.ds(3, 3), :, mid_rows, :], MC.at[pl.ds(7, 3), :, mid_rows, :], mcs, mcr, (near_x(-1), j, g))

    wait(src.at[:, pl.ds(0, 24), :], local.at[1])
    wait(s_bytes, e1r.at[1])

    def fine_first(x, _):
        make_faces(x, C, fine, 8, 32, 1)
        for t in range(2):
            V1[x, t, pl.ds(8, 32), :] = E[x, t, pl.ds(8, 32), :] * (2.0 * S[x, t, pl.ds(8, 32), :])
        return 0

    lax.fori_loop(1, 15, fine_first, 0)
    last_face(15, C, fine, 8, 32)

    def fine_second(x, _):
        sweep(x, V1, V2, fine, S, 2.0, 8, 32, 1)
        return 0

    lax.fori_loop(2, 14, fine_second, 0)

    def fine_residual(m, _):
        lower = left_over(4 + 2 * m, V2, fine, S, 0.5, 8, 32, 1)
        upper = left_over(5 + 2 * m, V2, fine, S, 0.5, 8, 32, 1)
        for t in range(2):
            RS[m, t] = lower[t] + upper[t]
            two = RS[m, t, pl.ds(0, 16, stride=2), :] + RS[m, t, pl.ds(1, 16, stride=2), :]
            MS[m + 3, t, mid_rows, :] = 0.125 * pair_sum(two, 1)
        return 0

    lax.fori_loop(0, 4, fine_residual, 0)
    send(MS.at[pl.ds(5, 2), :, mid_rows, :], MS.at[pl.ds(1, 2), :, mid_rows, :], mss, msr, (near_x(1), j, g))
    send(MS.at[pl.ds(3, 2), :, mid_rows, :], MS.at[pl.ds(7, 2), :, mid_rows, :], mss, msr, (near_x(-1), j, g))

    def squeeze(parts):
        total = None
        for part, value in enumerate(parts):
            term = exact_dot(value, squeeze_matrix(part))
            total = term if total is None else total + term
        return total

    def coarsest(field, scale):
        parts = []
        for layer in range(2):
            for t in range(2):
                R2[layer, t] = field(2 * layer, t) + field(2 * layer + 1, t)
                two = R2[layer, t, pl.ds(4, 4, stride=2), :] + R2[layer, t, pl.ds(5, 4, stride=2), :]
                parts.append(scale * pair_sum(two, 2))
        return squeeze(parts)

    own_target = jnp.full((4, 128), tgt[0, 0, 0].astype(F32), F32)
    ES[pl.ds(0, 4), :] = coarsest(lambda m, t: MC[3 + m, t, mid_rows, :], 0.125)
    ES[pl.ds(4, 4), :] = own_target
    EB[2 * NEAR + g] = ES[...]
    for d in (4, 3, 2, 1):
        for sign in (1, -1):
            for core in range(2):
                send(ES, EB.at[2 * (NEAR - sign * d) + g], ebs, ebr, (near_x(sign * d), j, core))
    send(ES, EB.at[2 * NEAR + g], ebs, ebr, (i, j, 1 - g))

    wait(MC.at[pl.ds(0, 6), :, mid_rows, :], mcr)

    @pl.when(i == 0)
    def _():
        MC[pl.ds(0, 3)] = jnp.zeros((3, *MC.shape[1:]), F32)

    @pl.when(i == n_gx - 1)
    def _():
        MC[pl.ds(7, 3)] = jnp.zeros((3, *MC.shape[1:]), F32)

    def mid_first(x, _):
        make_faces(x, MC, mid, 8, 16, 2)
        return 0

    lax.fori_loop(1, 9, mid_first, 0)
    last_face(9, MC, mid, 8, 16)
    wait(MS.at[pl.ds(0, 4), :, mid_rows, :], msr)

    def mid_start(x, _):
        for t in range(2):
            M1[x, t, mid_rows, :] = ME[x, t, mid_rows, :] * (8.0 * MS[x, t, mid_rows, :])
        return 0

    lax.fori_loop(1, 9, mid_start, 0)

    def mid_second(x, _):
        sweep(x, M1, M2, mid, MS, 8.0, 8, 16, 2)
        return 0

    lax.fori_loop(2, 8, mid_second, 0)
    mid_res = [left_over(3 + m, M2, mid, MS, 0.125, 8, 16, 2) for m in range(4)]
    low_src = coarsest(lambda m, t: mid_res[m][t], 0.125)

    GS[...] = low_src
    FS[pl.ds(0, 1), :] = jnp.sum(low_src, axis=0, keepdims=True)
    FS[pl.ds(1, 1), :] = own_target[:1]
    GB[2 * NEAR + g] = low_src
    for d in sorted(range(NEAR + 1, n_gx - NEAR), key=lambda d: -min(d, n_gx - d)):
        for core in range(2):
            send(FS, FB.at[2 * (n_gx - d - NEAR - 1) + g], fs, fr, (near_x(d), j, core))
    for d in (4, 3, 2, 1):
        for sign in (1, -1):
            for core in range(2):
                send(GS, GB.at[2 * (NEAR - sign * d) + g], gs, gr, (near_x(sign * d), j, core))
    send(GS, GB.at[2 * NEAR + g], gs, gr, (i, j, 1 - g))

    for m in range(4):
        for t in range(2):
            SY[m, t] = M2[3 + m, t, pl.ds(12, 8), :]
    send(SY, Y2.at[g], ys, yr, (i, j, 1 - g))
    send(SY, Y2.at[1 - g], ys, yr, (i, near_y(side), 1 - g))
    for m in range(4):
        for t in range(2):
            M2P[3 + m, t, mid_rows, :] = M2[3 + m, t, mid_rows, :]
    wait(Y2, yr)
    for m in range(4):
        for t in range(2):
            M2P[3 + m, t, pl.ds(9, 1), :] = Y2[0, m, t, pl.ds(5, 1), :]
            M2P[3 + m, t, pl.ds(22, 1), :] = Y2[1, m, t, pl.ds(2, 1), :]
    send(M2P.at[pl.ds(4, 3), :, mid_rows, :], M2P.at[pl.ds(0, 3), :, mid_rows, :], xs, xr, (near_x(1), j, g))
    send(M2P.at[pl.ds(3, 3), :, mid_rows, :], M2P.at[pl.ds(7, 3), :, mid_rows, :], xs, xr, (near_x(-1), j, g))

    wait(EB.at[pl.ds(0, 17)], ebr)
    lane = lanes_of(8)
    row = lax.broadcasted_iota(jnp.int32, (8, 128), 0)
    layer, tile, cell = lane // 64, (lane // 32) % 2, lane % 32
    boxes = 2 * NEAR + 1
    zero = jnp.zeros((8, 128), F32)
    coefs, marks = [], []
    for b in range(boxes):
        first, second = EB[2 * b], EB[2 * b + 1]
        coefs.append(jnp.concatenate([first[:4], second[:4]], axis=0))
        marks.append(jnp.where(tile == 0, jnp.broadcast_to(first[4:5], (8, 128)), jnp.broadcast_to(second[4:5], (8, 128))))
    joined = []
    for b in range(boxes - 1):
        touch = lax.rem(i + b - NEAR + n_gx, n_gx) != n_gx - 1
        joined.append(jnp.where((marks[b] == marks[b + 1]) & touch, 1.0, 0.0))

    def along_x(values, ends=None):
        turned = [pltpu.roll(v, 64, 1) for v in values]
        below, above = [], []
        for b in range(boxes):
            before = turned[b - 1] * joined[b - 1] if b else zero
            after = turned[b + 1] * joined[b] if b < boxes - 1 else zero
            below.append(jnp.where(layer == 0, before, turned[b]))
            above.append(jnp.where(layer == 0, turned[b], after))
        return below, above

    def along_yz(v):
        return (pltpu.roll(v, 1, 0), pltpu.roll(v, 7, 0), pltpu.roll(v, 1, 1), pltpu.roll(v, 127, 1))

    keeps = (row > 0, row < 7, cell > 0, cell < 31)
    c_below, c_above = along_x(coefs)
    low_faces, low_ease = [], []
    for b in range(boxes):
        c = coefs[b]
        around = [jnp.where(keep, v, 0.0) for keep, v in zip(keeps, along_yz(c))]
        faces = [c + c_below[b], c + c_above[b]] + [c + v for v in around]
        total = faces[0] + faces[1] + faces[2] + faces[3] + faces[4] + faces[5]
        low_faces.append(faces[:2] + [jnp.where(keep, f, 0.0) for keep, f in zip(keeps, faces[2:])])
        low_ease.append(RELAX / total)

    wait(GB.at[pl.ds(0, 17)], gr)
    wait(FB, fr)
    rhs = [jnp.concatenate([GB[2 * b], GB[2 * b + 1]], axis=0) for b in range(boxes)]
    sums = [jnp.sum(v, axis=0, keepdims=True) for v in rhs]
    names = [m[:1] for m in marks]
    top_tile = tile[:1]
    for d in range(n_gx - boxes):
        first, second = FB[2 * d], FB[2 * d + 1]
        sums.append(first[:1] + second[:1])
        names.append(jnp.where(top_tile == 0, first[1:], second[1:]))
    sums = jnp.concatenate(sums, axis=0)
    names = jnp.concatenate(names, axis=0)
    src_lane = lax.broadcasted_iota(jnp.int32, (128, 128), 0)
    dst_lane = lax.broadcasted_iota(jnp.int32, (128, 128), 1)
    same_tile = jnp.where((src_lane // 32) % 2 == (dst_lane // 32) % 2, 1.0, 0.0).astype(F32)
    sums = exact_dot(sums, same_tile)
    low = []
    for b in range(boxes):
        same = names == names[b:b + 1]
        total = jnp.sum(jnp.where(same, sums, 0.0), axis=0, keepdims=True)
        number = jnp.sum(jnp.where(same, 512.0, 0.0), axis=0, keepdims=True)
        low.append(jnp.broadcast_to(4.0 * total / jnp.maximum(number, 1.0), (8, 128)))

    for number in range(BOTTOM):
        below, above = along_x(low)
        fresh = []
        for b in range(boxes):
            around = [below[b], above[b], *along_yz(low[b])]
            total = 32.0 * rhs[b]
            for face, value in zip(low_faces[b], around):
                total = total + face * value
            fresh.append(0.2 * low[b] + low_ease[b] * total)
        low = fresh

    for b in range(3):
        SQ[b] = low[NEAR - 1 + b]
    send(SQ, Q.at[:, pl.ds(pl.multiple_of(16 - 16 * g, 8), 8), :], qs, qr, (i, near_y(side), 1 - g))
    for b in range(3):
        Q[b, pl.ds(8, 8), :] = low[NEAR - 1 + b]
    wait(M2P.at[pl.ds(0, 6), :, mid_rows, :], xr)
    wait(SQ, qr)
    fix = jnp.concatenate(
        [jnp.where(g == 0, Q[b, pl.ds(6, 8), :], Q[b, pl.ds(10, 8), :]) for b in range(3)], axis=0
    )
    for part in range(4):
        wide = exact_dot(fix, spread_matrix(part))
        for b in range(3):
            PK[2 * b + part // 2, part % 2, pl.ds(0, 8, stride=2), :] = wide[8 * b:8 * b + 8]
            PK[2 * b + part // 2, part % 2, pl.ds(1, 8, stride=2), :] = wide[8 * b:8 * b + 8]

    def corrected(x, _):
        for t in range(2):
            better = M2P[x, t, mid_rows, :] + PK[(x + 1) // 2, t]
            M3[x, t, mid_rows, :] = jnp.where(MC[x, t, mid_rows, :] > 0.0, better, 0.0)
        return 0

    lax.fori_loop(0, 10, corrected, 0)

    def mid_third(x, _):
        sweep(x, M3, M4, mid, MS, 8.0, 8, 16, 2)
        return 0

    lax.fori_loop(1, 9, mid_third, 0)

    def mid_fourth(x, _):
        sweep(x, M4, M1, mid, MS, 8.0, 8, 16, 2)
        for t in range(2):
            PF[pl.ds(0, 16, stride=2), :] = M1[x, t, mid_rows, :]
            PF[pl.ds(1, 16, stride=2), :] = M1[x, t, mid_rows, :]
            for half in range(2):
                V3[2 * x - 2 + half, t, pl.ds(8, 32), :] = V2[2 * x - 2 + half, t, pl.ds(8, 32), :] + PF[...]
        return 0

    lax.fori_loop(2, 8, mid_fourth, 0)

    def fine_third(x, _):
        sweep(x, V3, V1, fine, S, 2.0, 8, 32, 1)
        return 0

    lax.fori_loop(3, 13, fine_third, 0)

    def fine_fourth(x, _):
        at = pl.ds(16, 16)
        sums, own = pull(x, V1, fine, 16, 16, 1)
        for t in range(2):
            FO[x - 4, t] = 0.2 * own[t] + E[x, t, at, :] * (2.0 * S[x, t, at, :] + sums[t])
        return 0

    lax.fori_loop(4, 12, fine_fourth, 0)

    out_rows = pl.ds(pl.multiple_of(16 * g, 8), 16)
    send(FO.at[:, 1 - g], out.at[:, out_rows, :], os_, or_, (i, j, 1 - g))
    keep = pltpu.make_async_copy(FO.at[:, g], out.at[:, out_rows, :], local.at[2])
    keep.start()

    wait(c_bytes, e1s.at[0])
    wait(s_bytes, e1s.at[1])
    wait(MC.at[pl.ds(0, 6), :, mid_rows, :], mcs)
    wait(MS.at[pl.ds(0, 4), :, mid_rows, :], mss)
    wait(EB.at[pl.ds(0, 17)], ebs)
    wait(GB.at[pl.ds(0, 17)], gs)
    wait(FB, fs)
    wait(Y2, ys)
    wait(M2P.at[pl.ds(0, 6), :, mid_rows, :], xs)
    wait(SQ, qs)
    keep.wait()
    wait(FO.at[:, 0], os_)
    wait(out.at[:, pl.ds(0, 16), :], or_)


def solution(mesh):
    n_gx, n_gy = mesh.shape["gx"], mesh.shape["gy"]

    def kernel(*refs):
        cycle(n_gx, n_gy, *refs)

    def per_device(source, beta_cells, target):
        fine = pltpu.VMEM((16, 2, 48, 128), F32)
        mid = pltpu.VMEM((10, 2, 32, 128), F32)
        far = n_gx - 2 * NEAR - 1
        dma = pltpu.SemaphoreType.DMA
        return pl.pallas_call(
            kernel,
            out_shape=jax.ShapeDtypeStruct(source.shape, F32),
            in_specs=[
                pl.BlockSpec(memory_space=pl.ANY),
                pl.BlockSpec(memory_space=pl.ANY),
                pl.BlockSpec(memory_space=pltpu.SMEM),
            ],
            out_specs=pl.BlockSpec(memory_space=pl.ANY),
            scratch_shapes=[
                *[fine] * 11,
                *[mid] * 13,
                pltpu.VMEM((4, 2, 32, 128), F32),
                pltpu.VMEM((4, 2, 32, 128), F32),
                pltpu.VMEM((2, 2, 16, 128), F32),
                pltpu.VMEM((4, 2, 8, 128), F32),
                pltpu.VMEM((2, 4, 2, 8, 128), F32),
                pltpu.VMEM((8, 128), F32),
                pltpu.VMEM((4 * NEAR + 2, 8, 128), F32),
                pltpu.VMEM((8, 128), F32),
                pltpu.VMEM((4 * NEAR + 2, 4, 128), F32),
                pltpu.VMEM((4, 128), F32),
                pltpu.VMEM((2 * far, 2, 128), F32),
                pltpu.VMEM((2, 128), F32),
                pltpu.VMEM((3, 24, 128), F32),
                pltpu.VMEM((3, 8, 128), F32),
                pltpu.VMEM((6, 2, 16, 128), F32),
                pltpu.VMEM((32, 128), F32),
                pltpu.VMEM((8, 2, 16, 128), F32),
                dma((3,)),
                dma((2,)),
                dma((2,)),
                *[dma] * 18,
            ],
            compiler_params=pltpu.CompilerParams(
                collective_id=0, has_side_effects=True, vmem_limit_bytes=32 * 2**20
            ),
            name="cycle",
        )(source, beta_cells, target)

    spec = P("gx", "gy", "gz")
    return jax.shard_map(
        per_device, mesh=mesh, in_specs=(spec, spec, spec), out_specs=spec, check_vma=False
    )
```

```python
import jax
import jax.numpy as jnp
from jax import lax
from jax.experimental import pallas as pl
from jax.experimental.pallas import tpu as pltpu
from jax.sharding import PartitionSpec as P


BOTTOM = 6
RELAX = 0.8
F32 = jnp.float32
MESH = pl.DeviceIdType.MESH
NEAR = 4


def lanes_of(rows):
    return lax.broadcasted_iota(jnp.int32, (rows, 128), 1)


def beside(left_tile, right_tile, step):
    lane = lanes_of(left_tile.shape[0])
    low0, low1 = pltpu.roll(left_tile, step, 1), pltpu.roll(right_tile, step, 1)
    high0, high1 = pltpu.roll(left_tile, 128 - step, 1), pltpu.roll(right_tile, 128 - step, 1)
    below = (low0, jnp.where(lane < step, low0, low1))
    above = (jnp.where(lane >= 128 - step, high1, high0), high1)
    return below, above


def make_faces(x, coef, faces, row, rows, step):
    fx, fy, fl, fr, weight, ease = faces
    at = pl.ds(row, rows)
    own = [coef[x, t, at, :] for t in range(2)]
    below, above = beside(*own, step)
    lane = lanes_of(rows)
    for t in range(2):
        c = own[t]
        low = jnp.where(lane < step, 0.0, below[0]) if t == 0 else below[1]
        high = jnp.where(lane >= 128 - step, 0.0, above[1]) if t == 1 else above[0]
        x_low = c + coef[x - 1, t, at, :]
        y_low = c + coef[x, t, pl.ds(row - 1, rows), :]
        z_low, z_high = c + low, c + high
        total = (
            x_low
            + (c + coef[x + 1, t, at, :])
            + y_low
            + (c + coef[x, t, pl.ds(row + 1, rows), :])
            + z_low
            + z_high
        )
        fx[x, t, at, :] = x_low
        fy[x, t, at, :] = y_low
        fl[x, t, at, :] = jnp.where(lane < step, 0.0, z_low) if t == 0 else z_low
        fr[x, t, at, :] = jnp.where(lane >= 128 - step, 0.0, z_high) if t == 1 else z_high
        weight[x, t, at, :] = total
        ease[x, t, at, :] = jnp.where(c > 0.0, RELAX / total, 0.0)


def last_face(x, coef, faces, row, rows):
    at = pl.ds(row, rows)
    for t in range(2):
        faces[0][x, t, at, :] = coef[x, t, at, :] + coef[x - 1, t, at, :]


def pull(x, field, faces, row, rows, step):
    fx, fy, fl, fr = faces[:4]
    at = pl.ds(row, rows)
    own = [field[x, t, at, :] for t in range(2)]
    below, above = beside(*own, step)
    sums = []
    for t in range(2):
        sums.append(
            fx[x, t, at, :] * field[x - 1, t, at, :]
            + fx[x + 1, t, at, :] * field[x + 1, t, at, :]
            + fy[x, t, at, :] * field[x, t, pl.ds(row - 1, rows), :]
            + fy[x, t, pl.ds(row + 1, rows), :] * field[x, t, pl.ds(row + 1, rows), :]
            + fl[x, t, at, :] * below[t]
            + fr[x, t, at, :] * above[t]
        )
    return sums, own


def sweep(x, field, out, faces, source, gain, row, rows, step):
    at = pl.ds(row, rows)
    sums, own = pull(x, field, faces, row, rows, step)
    for t in range(2):
        out[x, t, at, :] = 0.2 * own[t] + faces[5][x, t, at, :] * (gain * source[x, t, at, :] + sums[t])


def left_over(x, field, faces, source, half, row, rows, step):
    at = pl.ds(row, rows)
    sums, own = pull(x, field, faces, row, rows, step)
    return [source[x, t, at, :] - half * (faces[4][x, t, at, :] * own[t] - sums[t]) for t in range(2)]


def pair_sum(value, step):
    lane = lanes_of(value.shape[0])
    other = jnp.where((lane // step) % 2 == 0, pltpu.roll(value, 128 - step, 1), pltpu.roll(value, step, 1))
    return value + other


def exact_dot(a, b):
    return jnp.dot(a, b, precision=lax.Precision.HIGHEST, preferred_element_type=F32)


def squeeze_matrix(part):
    src = lax.broadcasted_iota(jnp.int32, (128, 128), 0)
    dst = lax.broadcasted_iota(jnp.int32, (128, 128), 1)
    return jnp.where((src == 4 * (dst % 32)) & (dst // 32 == part), 1.0, 0.0).astype(F32)


def spread_matrix(part):
    src = lax.broadcasted_iota(jnp.int32, (128, 128), 0)
    dst = lax.broadcasted_iota(jnp.int32, (128, 128), 1)
    return jnp.where(src == 32 * part + dst // 4, 1.0, 0.0).astype(F32)


def cycle(n_gx, n_gy, src, beta, tgt, out, *scratch):
    (C, S, FX, FY, FL, FR, W, E, V1, V2, V3,
     MC, MS, MFX, MFY, MFL, MFR, MW, ME, M1, M2, M2P, M3, M4,
     RS, RC, R2, SY, Y2, SX, EB, ES, GB, GS, FB, FS, Q, SQ, PK, PF, FO,
     local, e1s, e1r, mcs, mcr, mss, msr, ebs, ebr, gs, gr, fs, fr, ys, yr, xs, xr, qs, qr, os_, or_, known) = scratch
    i, j, g = lax.axis_index("gx"), lax.axis_index("gy"), lax.axis_index("gz")
    fine = (FX, FY, FL, FR, W, E)
    mid = (MFX, MFY, MFL, MFR, MW, ME)

    def near_x(d):
        return lax.rem(i + d + n_gx, n_gx)

    def near_y(d):
        return lax.rem(j + d + n_gy, n_gy)

    def send(source, target, send_sem, recv_sem, where):
        pltpu.make_async_remote_copy(
            src_ref=source, dst_ref=target, send_sem=send_sem, recv_sem=recv_sem,
            device_id=where, device_id_type=MESH,
        ).start()

    def tell(step):
        for sign in (1, -1):
            pl.semaphore_signal(known.at[step], inc=1, device_id=(near_x(sign * 3), j, g), device_id_type=MESH)

    def wait(ref, sem):
        pltpu.make_async_copy(ref, ref, sem).wait()

    own_rows = pl.ds(pl.multiple_of(8 * g, 8), 24)
    own_at = pl.ds(pl.multiple_of(16 - 8 * g, 8), 24)
    pltpu.make_async_copy(beta.at[:, own_rows, :], C.at[pl.ds(4, 8), g, own_at, :], local.at[0]).start()
    pltpu.make_async_copy(src.at[:, own_rows, :], S.at[pl.ds(4, 8), g, own_at, :], local.at[1]).start()

    barrier = pltpu.get_barrier_semaphore()
    side = 2 * g - 1

    def greet(where):
        pl.semaphore_signal(barrier, inc=1, device_id=where, device_id_type=MESH)

    for dx in (-1, 0, 1):
        for core in range(2):
            greet((near_x(dx), near_y(side), core))
    for dx in (3, 2, 1):
        for sign in (1, -1):
            for core in range(2 if dx < 3 else 1):
                greet((near_x(sign * dx), j, core if dx < 3 else g))
    greet((i, j, 1 - g))
    pl.semaphore_wait(barrier, 17)
    tell(0)

    for index, (field, target, deep) in enumerate(((beta, C, 4), (src, S, 3))):
        ss, rs = e1s.at[index], e1r.at[index]
        for dx in (1, -1):
            part = pl.ds(8 - deep, deep) if dx == 1 else pl.ds(0, deep)
            place = pl.ds(4 - deep, deep) if dx == 1 else pl.ds(12, deep)
            for core in range(2):
                dy = 1 if core == 0 else -1
                send(field.at[part, pl.ds(24 if core == 0 else 0, 8), :],
                     target.at[place, g, pl.ds(8 if core == 0 else 32, 8), :], ss, rs,
                     (near_x(dx), near_y(dy), core))
                send(field.at[part, pl.ds(8 * core, 24), :],
                     target.at[place, g, pl.ds(16 - 8 * core, 24), :], ss, rs, (near_x(dx), j, core))
        for core in range(2):
            dy = 1 if core == 0 else -1
            send(field.at[:, pl.ds(24 if core == 0 else 0, 8), :],
                 target.at[pl.ds(4, 8), g, pl.ds(8 if core == 0 else 32, 8), :], ss, rs, (i, near_y(dy), core))
        send(field.at[:, pl.ds(pl.multiple_of(8 - 8 * g, 8), 24), :],
             target.at[pl.ds(4, 8), g, pl.ds(pl.multiple_of(8 + 8 * g, 8), 24), :], ss, rs, (i, j, 1 - g))

    c_bytes = C.at[pl.ds(0, 13), :, pl.ds(0, 32), :]
    s_bytes = S.at[pl.ds(0, 11), :, pl.ds(0, 32), :]
    wait(beta.at[:, pl.ds(0, 24), :], local.at[0])
    wait(c_bytes, e1r.at[0])

    @pl.when(i == 0)
    def _():
        C[pl.ds(0, 4)] = jnp.zeros((4, *C.shape[1:]), F32)

    @pl.when(i == n_gx - 1)
    def _():
        C[pl.ds(12, 4)] = jnp.zeros((4, *C.shape[1:]), F32)

    @pl.when((j == 0) & (g == 0))
    def _():
        C[:, :, pl.ds(8, 8), :] = jnp.zeros((16, 2, 8, 128), F32)

    @pl.when((j == n_gy - 1) & (g == 1))
    def _():
        C[:, :, pl.ds(32, 8), :] = jnp.zeros((16, 2, 8, 128), F32)

    def mid_coefficient(m, _):
        for t in range(2):
            RC[m, t] = C[4 + 2 * m, t, pl.ds(8, 32), :] + C[5 + 2 * m, t, pl.ds(8, 32), :]
            two = RC[m, t, pl.ds(0, 16, stride=2), :] + RC[m, t, pl.ds(1, 16, stride=2), :]
            MC[m + 3, t, pl.ds(8, 16), :] = 0.125 * pair_sum(two, 1)
        return 0

    lax.fori_loop(0, 4, mid_coefficient, 0)
    mid_rows = pl.ds(8, 16)
    send(MC.at[pl.ds(4, 3), :, mid_rows, :], MC.at[pl.ds(0, 3), :, mid_rows, :], mcs, mcr, (near_x(1), j, g))
    send(MC.at[pl.ds(3, 3), :, mid_rows, :], MC.at[pl.ds(7, 3), :, mid_rows, :], mcs, mcr, (near_x(-1), j, g))

    pl.semaphore_wait(known.at[0], 2)
    tell(1)

    wait(src.at[:, pl.ds(0, 24), :], local.at[1])
    wait(s_bytes, e1r.at[1])

    def fine_first(x, _):
        make_faces(x, C, fine, 8, 32, 1)
        for t in range(2):
            V1[x, t, pl.ds(8, 32), :] = E[x, t, pl.ds(8, 32), :] * (2.0 * S[x, t, pl.ds(8, 32), :])
        return 0

    lax.fori_loop(1, 15, fine_first, 0)
    last_face(15, C, fine, 8, 32)

    def fine_second(x, _):
        sweep(x, V1, V2, fine, S, 2.0, 8, 32, 1)
        return 0

    lax.fori_loop(2, 14, fine_second, 0)

    def fine_residual(m, _):
        lower = left_over(4 + 2 * m, V2, fine, S, 0.5, 8, 32, 1)
        upper = left_over(5 + 2 * m, V2, fine, S, 0.5, 8, 32, 1)
        for t in range(2):
            RS[m, t] = lower[t] + upper[t]
            two = RS[m, t, pl.ds(0, 16, stride=2), :] + RS[m, t, pl.ds(1, 16, stride=2), :]
            MS[m + 3, t, mid_rows, :] = 0.125 * pair_sum(two, 1)
        return 0

    lax.fori_loop(0, 4, fine_residual, 0)
    send(MS.at[pl.ds(5, 2), :, mid_rows, :], MS.at[pl.ds(1, 2), :, mid_rows, :], mss, msr, (near_x(1), j, g))
    send(MS.at[pl.ds(3, 2), :, mid_rows, :], MS.at[pl.ds(7, 2), :, mid_rows, :], mss, msr, (near_x(-1), j, g))

    def squeeze(parts):
        total = None
        for part, value in enumerate(parts):
            term = exact_dot(value, squeeze_matrix(part))
            total = term if total is None else total + term
        return total

    def coarsest(field, scale):
        parts = []
        for layer in range(2):
            for t in range(2):
                R2[layer, t] = field(2 * layer, t) + field(2 * layer + 1, t)
                two = R2[layer, t, pl.ds(4, 4, stride=2), :] + R2[layer, t, pl.ds(5, 4, stride=2), :]
                parts.append(scale * pair_sum(two, 2))
        return squeeze(parts)

    own_target = jnp.full((4, 128), tgt[0, 0, 0].astype(F32), F32)
    ES[pl.ds(0, 4), :] = coarsest(lambda m, t: MC[3 + m, t, mid_rows, :], 0.125)
    ES[pl.ds(4, 4), :] = own_target
    EB[2 * NEAR + g] = ES[...]
    for d in (4, 3, 2, 1):
        for sign in (1, -1):
            for core in range(2):
                send(ES, EB.at[2 * (NEAR - sign * d) + g], ebs, ebr, (near_x(sign * d), j, core))
    send(ES, EB.at[2 * NEAR + g], ebs, ebr, (i, j, 1 - g))

    wait(MC.at[pl.ds(0, 6), :, mid_rows, :], mcr)

    @pl.when(i == 0)
    def _():
        MC[pl.ds(0, 3)] = jnp.zeros((3, *MC.shape[1:]), F32)

    @pl.when(i == n_gx - 1)
    def _():
        MC[pl.ds(7, 3)] = jnp.zeros((3, *MC.shape[1:]), F32)

    def mid_first(x, _):
        make_faces(x, MC, mid, 8, 16, 2)
        return 0

    lax.fori_loop(1, 9, mid_first, 0)
    last_face(9, MC, mid, 8, 16)
    wait(MS.at[pl.ds(0, 4), :, mid_rows, :], msr)

    def mid_start(x, _):
        for t in range(2):
            M1[x, t, mid_rows, :] = ME[x, t, mid_rows, :] * (8.0 * MS[x, t, mid_rows, :])
        return 0

    lax.fori_loop(1, 9, mid_start, 0)

    def mid_second(x, _):
        sweep(x, M1, M2, mid, MS, 8.0, 8, 16, 2)
        return 0

    lax.fori_loop(2, 8, mid_second, 0)
    mid_res = [left_over(3 + m, M2, mid, MS, 0.125, 8, 16, 2) for m in range(4)]
    low_src = coarsest(lambda m, t: mid_res[m][t], 0.125)

    pl.semaphore_wait(known.at[1], 2)
    GS[...] = low_src
    FS[pl.ds(0, 1), :] = jnp.sum(low_src, axis=0, keepdims=True)
    FS[pl.ds(1, 1), :] = own_target[:1]
    GB[2 * NEAR + g] = low_src
    for d in sorted(range(NEAR + 1, n_gx - NEAR), key=lambda d: -min(d, n_gx - d)):
        for core in range(2):
            send(FS, FB.at[2 * (n_gx - d - NEAR - 1) + g], fs, fr, (near_x(d), j, core))
    for d in (4, 3, 2, 1):
        for sign in (1, -1):
            for core in range(2):
                send(GS, GB.at[2 * (NEAR - sign * d) + g], gs, gr, (near_x(sign * d), j, core))
    send(GS, GB.at[2 * NEAR + g], gs, gr, (i, j, 1 - g))

    for m in range(4):
        for t in range(2):
            SY[m, t] = M2[3 + m, t, pl.ds(12, 8), :]
    send(SY, Y2.at[g], ys, yr, (i, j, 1 - g))
    send(SY, Y2.at[1 - g], ys, yr, (i, near_y(side), 1 - g))
    for m in range(4):
        for t in range(2):
            M2P[3 + m, t, mid_rows, :] = M2[3 + m, t, mid_rows, :]
    wait(Y2, yr)
    for m in range(4):
        for t in range(2):
            M2P[3 + m, t, pl.ds(9, 1), :] = Y2[0, m, t, pl.ds(5, 1), :]
            M2P[3 + m, t, pl.ds(22, 1), :] = Y2[1, m, t, pl.ds(2, 1), :]
    send(M2P.at[pl.ds(4, 3), :, mid_rows, :], M2P.at[pl.ds(0, 3), :, mid_rows, :], xs, xr, (near_x(1), j, g))
    send(M2P.at[pl.ds(3, 3), :, mid_rows, :], M2P.at[pl.ds(7, 3), :, mid_rows, :], xs, xr, (near_x(-1), j, g))

    wait(EB.at[pl.ds(0, 17)], ebr)
    lane = lanes_of(8)
    row = lax.broadcasted_iota(jnp.int32, (8, 128), 0)
    layer, tile, cell = lane // 64, (lane // 32) % 2, lane % 32
    boxes = 2 * NEAR + 1
    zero = jnp.zeros((8, 128), F32)
    coefs, marks = [], []
    for b in range(boxes):
        first, second = EB[2 * b], EB[2 * b + 1]
        coefs.append(jnp.concatenate([first[:4], second[:4]], axis=0))
        marks.append(jnp.where(tile == 0, jnp.broadcast_to(first[4:5], (8, 128)), jnp.broadcast_to(second[4:5], (8, 128))))
    joined = []
    for b in range(boxes - 1):
        touch = lax.rem(i + b - NEAR + n_gx, n_gx) != n_gx - 1
        joined.append(jnp.where((marks[b] == marks[b + 1]) & touch, 1.0, 0.0))

    def along_x(values, ends=None):
        turned = [pltpu.roll(v, 64, 1) for v in values]
        below, above = [], []
        for b in range(boxes):
            before = turned[b - 1] * joined[b - 1] if b else zero
            after = turned[b + 1] * joined[b] if b < boxes - 1 else zero
            below.append(jnp.where(layer == 0, before, turned[b]))
            above.append(jnp.where(layer == 0, turned[b], after))
        return below, above

    def along_yz(v):
        return (pltpu.roll(v, 1, 0), pltpu.roll(v, 7, 0), pltpu.roll(v, 1, 1), pltpu.roll(v, 127, 1))

    keeps = (row > 0, row < 7, cell > 0, cell < 31)
    c_below, c_above = along_x(coefs)
    low_faces, low_ease = [], []
    for b in range(boxes):
        c = coefs[b]
        around = [jnp.where(keep, v, 0.0) for keep, v in zip(keeps, along_yz(c))]
        faces = [c + c_below[b], c + c_above[b]] + [c + v for v in around]
        total = faces[0] + faces[1] + faces[2] + faces[3] + faces[4] + faces[5]
        low_faces.append(faces[:2] + [jnp.where(keep, f, 0.0) for keep, f in zip(keeps, faces[2:])])
        low_ease.append(RELAX / total)

    wait(GB.at[pl.ds(0, 17)], gr)
    wait(FB, fr)
    rhs = [jnp.concatenate([GB[2 * b], GB[2 * b + 1]], axis=0) for b in range(boxes)]
    sums = [jnp.sum(v, axis=0, keepdims=True) for v in rhs]
    names = [m[:1] for m in marks]
    top_tile = tile[:1]
    for d in range(n_gx - boxes):
        first, second = FB[2 * d], FB[2 * d + 1]
        sums.append(first[:1] + second[:1])
        names.append(jnp.where(top_tile == 0, first[1:], second[1:]))
    sums = jnp.concatenate(sums, axis=0)
    names = jnp.concatenate(names, axis=0)
    src_lane = lax.broadcasted_iota(jnp.int32, (128, 128), 0)
    dst_lane = lax.broadcasted_iota(jnp.int32, (128, 128), 1)
    same_tile = jnp.where((src_lane // 32) % 2 == (dst_lane // 32) % 2, 1.0, 0.0).astype(F32)
    sums = exact_dot(sums, same_tile)
    low = []
    for b in range(boxes):
        same = names == names[b:b + 1]
        total = jnp.sum(jnp.where(same, sums, 0.0), axis=0, keepdims=True)
        number = jnp.sum(jnp.where(same, 512.0, 0.0), axis=0, keepdims=True)
        low.append(jnp.broadcast_to(4.0 * total / jnp.maximum(number, 1.0), (8, 128)))

    for number in range(BOTTOM):
        below, above = along_x(low)
        fresh = []
        for b in range(boxes):
            around = [below[b], above[b], *along_yz(low[b])]
            total = 32.0 * rhs[b]
            for face, value in zip(low_faces[b], around):
                total = total + face * value
            fresh.append(0.2 * low[b] + low_ease[b] * total)
        low = fresh

    for b in range(3):
        SQ[b] = low[NEAR - 1 + b]
    send(SQ, Q.at[:, pl.ds(pl.multiple_of(16 - 16 * g, 8), 8), :], qs, qr, (i, near_y(side), 1 - g))
    for b in range(3):
        Q[b, pl.ds(8, 8), :] = low[NEAR - 1 + b]
    wait(M2P.at[pl.ds(0, 6), :, mid_rows, :], xr)
    wait(SQ, qr)
    fix = jnp.concatenate(
        [jnp.where(g == 0, Q[b, pl.ds(6, 8), :], Q[b, pl.ds(10, 8), :]) for b in range(3)], axis=0
    )
    for part in range(4):
        wide = exact_dot(fix, spread_matrix(part))
        for b in range(3):
            PK[2 * b + part // 2, part % 2, pl.ds(0, 8, stride=2), :] = wide[8 * b:8 * b + 8]
            PK[2 * b + part // 2, part % 2, pl.ds(1, 8, stride=2), :] = wide[8 * b:8 * b + 8]

    def corrected(x, _):
        for t in range(2):
            better = M2P[x, t, mid_rows, :] + PK[(x + 1) // 2, t]
            M3[x, t, mid_rows, :] = jnp.where(MC[x, t, mid_rows, :] > 0.0, better, 0.0)
        return 0

    lax.fori_loop(0, 10, corrected, 0)

    def mid_third(x, _):
        sweep(x, M3, M4, mid, MS, 8.0, 8, 16, 2)
        return 0

    lax.fori_loop(1, 9, mid_third, 0)

    def mid_fourth(x, _):
        sweep(x, M4, M1, mid, MS, 8.0, 8, 16, 2)
        for t in range(2):
            PF[pl.ds(0, 16, stride=2), :] = M1[x, t, mid_rows, :]
            PF[pl.ds(1, 16, stride=2), :] = M1[x, t, mid_rows, :]
            for half in range(2):
                V3[2 * x - 2 + half, t, pl.ds(8, 32), :] = V2[2 * x - 2 + half, t, pl.ds(8, 32), :] + PF[...]
        return 0

    lax.fori_loop(2, 8, mid_fourth, 0)

    def fine_third(x, _):
        sweep(x, V3, V1, fine, S, 2.0, 8, 32, 1)
        return 0

    lax.fori_loop(3, 13, fine_third, 0)

    def fine_fourth(x, _):
        at = pl.ds(16, 16)
        sums, own = pull(x, V1, fine, 16, 16, 1)
        for t in range(2):
            FO[x - 4, t] = 0.2 * own[t] + E[x, t, at, :] * (2.0 * S[x, t, at, :] + sums[t])
        return 0

    lax.fori_loop(4, 12, fine_fourth, 0)

    out_rows = pl.ds(pl.multiple_of(16 * g, 8), 16)
    send(FO.at[:, 1 - g], out.at[:, out_rows, :], os_, or_, (i, j, 1 - g))
    keep = pltpu.make_async_copy(FO.at[:, g], out.at[:, out_rows, :], local.at[2])
    keep.start()

    wait(c_bytes, e1s.at[0])
    wait(s_bytes, e1s.at[1])
    wait(MC.at[pl.ds(0, 6), :, mid_rows, :], mcs)
    wait(MS.at[pl.ds(0, 4), :, mid_rows, :], mss)
    wait(EB.at[pl.ds(0, 17)], ebs)
    wait(GB.at[pl.ds(0, 17)], gs)
    wait(FB, fs)
    wait(Y2, ys)
    wait(M2P.at[pl.ds(0, 6), :, mid_rows, :], xs)
    wait(SQ, qs)
    keep.wait()
    wait(FO.at[:, 0], os_)
    wait(out.at[:, pl.ds(0, 16), :], or_)


def solution(mesh):
    n_gx, n_gy = mesh.shape["gx"], mesh.shape["gy"]

    def kernel(*refs):
        cycle(n_gx, n_gy, *refs)

    def per_device(source, beta_cells, target):
        fine = pltpu.VMEM((16, 2, 48, 128), F32)
        mid = pltpu.VMEM((10, 2, 32, 128), F32)
        far = n_gx - 2 * NEAR - 1
        dma = pltpu.SemaphoreType.DMA
        return pl.pallas_call(
            kernel,
            out_shape=jax.ShapeDtypeStruct(source.shape, F32),
            in_specs=[
                pl.BlockSpec(memory_space=pltpu.HBM),
                pl.BlockSpec(memory_space=pltpu.HBM),
                pl.BlockSpec(memory_space=pltpu.SMEM),
            ],
            out_specs=pl.BlockSpec(memory_space=pl.ANY),
            scratch_shapes=[
                *[fine] * 11,
                *[mid] * 13,
                pltpu.VMEM((4, 2, 32, 128), F32),
                pltpu.VMEM((4, 2, 32, 128), F32),
                pltpu.VMEM((2, 2, 16, 128), F32),
                pltpu.VMEM((4, 2, 8, 128), F32),
                pltpu.VMEM((2, 4, 2, 8, 128), F32),
                pltpu.VMEM((8, 128), F32),
                pltpu.VMEM((4 * NEAR + 2, 8, 128), F32),
                pltpu.VMEM((8, 128), F32),
                pltpu.VMEM((4 * NEAR + 2, 4, 128), F32),
                pltpu.VMEM((4, 128), F32),
                pltpu.VMEM((2 * far, 2, 128), F32),
                pltpu.VMEM((2, 128), F32),
                pltpu.VMEM((3, 24, 128), F32),
                pltpu.VMEM((3, 8, 128), F32),
                pltpu.VMEM((6, 2, 16, 128), F32),
                pltpu.VMEM((32, 128), F32),
                pltpu.VMEM((8, 2, 16, 128), F32),
                dma((3,)),
                dma((2,)),
                dma((2,)),
                *[dma] * 18,
                pltpu.SemaphoreType.REGULAR((2,)),
            ],
            compiler_params=pltpu.CompilerParams(
                collective_id=0, has_side_effects=True, vmem_limit_bytes=32 * 2**20
            ),
            name="cycle",
        )(source, beta_cells, target)

    spec = P("gx", "gy", "gz")
    return jax.shard_map(
        per_device, mesh=mesh, in_specs=(spec, spec, spec), out_specs=spec, check_vma=False
    )
```

```python
import jax
import jax.numpy as jnp
from jax import lax
from jax.experimental import pallas as pl
from jax.experimental.pallas import tpu as pltpu
from jax.sharding import PartitionSpec as P


BOTTOM = 6
RELAX = 0.8
F32 = jnp.float32
MESH = pl.DeviceIdType.MESH
NEAR = 4


def layers(low, high, work):
    for x in range(low, high):
        work(x, 0)


def lanes_of(rows):
    return lax.broadcasted_iota(jnp.int32, (rows, 128), 1)


def beside(left_tile, right_tile, step):
    lane = lanes_of(left_tile.shape[0])
    low0, low1 = pltpu.roll(left_tile, step, 1), pltpu.roll(right_tile, step, 1)
    high0, high1 = pltpu.roll(left_tile, 128 - step, 1), pltpu.roll(right_tile, 128 - step, 1)
    below = (low0, jnp.where(lane < step, low0, low1))
    above = (jnp.where(lane >= 128 - step, high1, high0), high1)
    return below, above


def make_faces(x, coef, faces, row, rows, step):
    fx, fy, fl, fr, weight, ease = faces
    at = pl.ds(row, rows)
    own = [coef[x, t, at, :] for t in range(2)]
    below, above = beside(*own, step)
    lane = lanes_of(rows)
    for t in range(2):
        c = own[t]
        low = jnp.where(lane < step, 0.0, below[0]) if t == 0 else below[1]
        high = jnp.where(lane >= 128 - step, 0.0, above[1]) if t == 1 else above[0]
        x_low = c + coef[x - 1, t, at, :]
        y_low = c + coef[x, t, pl.ds(row - 1, rows), :]
        z_low, z_high = c + low, c + high
        total = (
            x_low
            + (c + coef[x + 1, t, at, :])
            + y_low
            + (c + coef[x, t, pl.ds(row + 1, rows), :])
            + z_low
            + z_high
        )
        fx[x, t, at, :] = x_low
        fy[x, t, at, :] = y_low
        fl[x, t, at, :] = jnp.where(lane < step, 0.0, z_low) if t == 0 else z_low
        fr[x, t, at, :] = jnp.where(lane >= 128 - step, 0.0, z_high) if t == 1 else z_high
        weight[x, t, at, :] = total
        ease[x, t, at, :] = jnp.where(c > 0.0, RELAX / total, 0.0)


def last_face(x, coef, faces, row, rows):
    at = pl.ds(row, rows)
    for t in range(2):
        faces[0][x, t, at, :] = coef[x, t, at, :] + coef[x - 1, t, at, :]


def pull(x, field, faces, row, rows, step):
    fx, fy, fl, fr = faces[:4]
    at = pl.ds(row, rows)
    own = [field[x, t, at, :] for t in range(2)]
    below, above = beside(*own, step)
    sums = []
    for t in range(2):
        sums.append(
            fx[x, t, at, :] * field[x - 1, t, at, :]
            + fx[x + 1, t, at, :] * field[x + 1, t, at, :]
            + fy[x, t, at, :] * field[x, t, pl.ds(row - 1, rows), :]
            + fy[x, t, pl.ds(row + 1, rows), :] * field[x, t, pl.ds(row + 1, rows), :]
            + fl[x, t, at, :] * below[t]
            + fr[x, t, at, :] * above[t]
        )
    return sums, own


def sweep(x, field, out, faces, source, gain, row, rows, step):
    at = pl.ds(row, rows)
    sums, own = pull(x, field, faces, row, rows, step)
    for t in range(2):
        out[x, t, at, :] = 0.2 * own[t] + faces[5][x, t, at, :] * (gain * source[x, t, at, :] + sums[t])


def left_over(x, field, faces, source, half, row, rows, step):
    at = pl.ds(row, rows)
    sums, own = pull(x, field, faces, row, rows, step)
    return [source[x, t, at, :] - half * (faces[4][x, t, at, :] * own[t] - sums[t]) for t in range(2)]


def pair_sum(value, step):
    lane = lanes_of(value.shape[0])
    other = jnp.where((lane // step) % 2 == 0, pltpu.roll(value, 128 - step, 1), pltpu.roll(value, step, 1))
    return value + other


def exact_dot(a, b):
    return jnp.dot(a, b, precision=lax.Precision.HIGHEST, preferred_element_type=F32)


def braid(parts):
    kind = lanes_of(parts[0].shape[0]) % 4
    return jnp.where(kind < 2, jnp.where(kind == 0, parts[0], parts[1]), jnp.where(kind == 2, parts[2], parts[3]))


def unbraid(value):
    lane = lanes_of(value.shape[0])
    even, upper = lane % 2 == 0, lane % 4 >= 2
    pairs = (jnp.where(even, value, pltpu.roll(value, 1, 1)), jnp.where(even, pltpu.roll(value, 127, 1), value))
    return [
        jnp.where(upper, pltpu.roll(pair, 2, 1), pair) if half == 0 else jnp.where(upper, pair, pltpu.roll(pair, 126, 1))
        for half in range(2)
        for pair in pairs
    ]


def cycle(n_gx, n_gy, src, beta, tgt, out, *scratch):
    (C, S, FX, FY, FL, FR, W, E, V1, V2, V3,
     MC, MS, MFX, MFY, MFL, MFR, MW, ME, M1, M2, M2P, M3, M4,
     RS, RC, R2, SY, Y2, SX, EB, ES, GB, GS, FB, FS, Q, SQ, PK, PF, FO,
     local, e1s, e1r, mcs, mcr, mss, msr, ebs, ebr, gs, gr, fs, fr, ys, yr, xs, xr, qs, qr, os_, or_, vs, vr, known) = scratch
    i, j, g = lax.axis_index("gx"), lax.axis_index("gy"), lax.axis_index("gz")
    fine = (FX, FY, FL, FR, W, E)
    mid = (MFX, MFY, MFL, MFR, MW, ME)

    def near_x(d):
        return lax.rem(i + d + n_gx, n_gx)

    def near_y(d):
        return lax.rem(j + d + n_gy, n_gy)

    def send(source, target, send_sem, recv_sem, where):
        pltpu.make_async_remote_copy(
            src_ref=source, dst_ref=target, send_sem=send_sem, recv_sem=recv_sem,
            device_id=where, device_id_type=MESH,
        ).start()

    def tell(step):
        for sign in (1, -1):
            pl.semaphore_signal(known.at[step], inc=1, device_id=(near_x(sign * 3), j, g), device_id_type=MESH)

    def wait(ref, sem):
        pltpu.make_async_copy(ref, ref, sem).wait()

    own_rows = pl.ds(pl.multiple_of(8 * g, 8), 24)
    own_at = pl.ds(pl.multiple_of(16 - 8 * g, 8), 24)
    pltpu.make_async_copy(beta.at[:, own_rows, :], C.at[pl.ds(4, 8), g, own_at, :], local.at[0]).start()
    pltpu.make_async_copy(src.at[:, own_rows, :], S.at[pl.ds(4, 8), g, own_at, :], local.at[1]).start()

    barrier = pltpu.get_barrier_semaphore()
    side = 2 * g - 1

    def greet(where):
        pl.semaphore_signal(barrier, inc=1, device_id=where, device_id_type=MESH)

    for dx in (-1, 0, 1):
        for core in range(2):
            greet((near_x(dx), near_y(side), core))
    for dx in (3, 2, 1):
        for sign in (1, -1):
            for core in range(2 if dx < 3 else 1):
                greet((near_x(sign * dx), j, core if dx < 3 else g))
    greet((i, j, 1 - g))
    pl.semaphore_wait(barrier, 17)
    tell(0)

    for index, (field, target, deep) in enumerate(((beta, C, 3), (src, S, 2))):
        ss, rs = e1s.at[index], e1r.at[2 * index + 1]
        for dx in (1, -1):
            part = pl.ds(8 - deep, deep) if dx == 1 else pl.ds(0, deep)
            place = pl.ds(4 - deep, deep) if dx == 1 else pl.ds(12, deep)
            for core in range(2):
                send(field.at[part, pl.ds(24 if core == 0 else 0, 8), :],
                     target.at[place, g, pl.ds(8 if core == 0 else 32, 8), :], ss, rs,
                     (near_x(dx), near_y(1 if core == 0 else -1), core))
                send(field.at[part, pl.ds(8 * core, 24), :],
                     target.at[place, g, pl.ds(16 - 8 * core, 24), :], ss, rs, (near_x(dx), j, core))
    for index, (field, target) in enumerate(((beta, C), (src, S))):
        ss, rs = e1s.at[index], e1r.at[2 * index]
        for core in range(2):
            send(field.at[:, pl.ds(24 if core == 0 else 0, 8), :],
                 target.at[pl.ds(4, 8), g, pl.ds(8 if core == 0 else 32, 8), :], ss, rs,
                 (i, near_y(1 if core == 0 else -1), core))
        send(field.at[:, pl.ds(pl.multiple_of(8 - 8 * g, 8), 24), :],
             target.at[pl.ds(4, 8), g, pl.ds(pl.multiple_of(8 + 8 * g, 8), 24), :], ss, rs, (i, j, 1 - g))

    def cells(count):
        return C.at[pl.ds(0, count), :, pl.ds(0, 32), :]

    wait(beta.at[:, pl.ds(0, 24), :], local.at[0])
    wait(cells(5), e1r.at[0])

    @pl.when((j == 0) & (g == 0))
    def _():
        C[pl.ds(4, 8), :, pl.ds(8, 8), :] = jnp.zeros((8, 2, 8, 128), F32)

    @pl.when((j == n_gy - 1) & (g == 1))
    def _():
        C[pl.ds(4, 8), :, pl.ds(32, 8), :] = jnp.zeros((8, 2, 8, 128), F32)

    def mid_coefficient(m, _):
        for t in range(2):
            RC[m, t] = C[4 + 2 * m, t, pl.ds(8, 32), :] + C[5 + 2 * m, t, pl.ds(8, 32), :]
            two = RC[m, t, pl.ds(0, 16, stride=2), :] + RC[m, t, pl.ds(1, 16, stride=2), :]
            MC[m + 3, t, pl.ds(8, 16), :] = 0.125 * pair_sum(two, 1)

    layers(0, 4, mid_coefficient)
    mid_rows = pl.ds(8, 16)
    send(MC.at[pl.ds(4, 3), :, mid_rows, :], MC.at[pl.ds(0, 3), :, mid_rows, :], mcs, mcr, (near_x(1), j, g))
    send(MC.at[pl.ds(3, 3), :, mid_rows, :], MC.at[pl.ds(7, 3), :, mid_rows, :], mcs, mcr, (near_x(-1), j, g))

    pl.semaphore_wait(known.at[0], 2)
    tell(1)

    wait(src.at[:, pl.ds(0, 24), :], local.at[1])
    wait(cells(5), e1r.at[2])

    def fine_first(x, _):
        make_faces(x, C, fine, 8, 32, 1)
        for t in range(2):
            V1[x, t, pl.ds(8, 32), :] = E[x, t, pl.ds(8, 32), :] * (2.0 * S[x, t, pl.ds(8, 32), :])

    def fine_second(x, _):
        sweep(x, V1, V2, fine, S, 2.0, 8, 32, 1)

    layers(5, 11, fine_first)
    layers(6, 10, fine_second)

    wait(cells(6), e1r.at[1])

    @pl.when(i == 0)
    def _():
        C[pl.ds(1, 3)] = jnp.zeros((3, *C.shape[1:]), F32)

    @pl.when(i == n_gx - 1)
    def _():
        C[pl.ds(12, 3)] = jnp.zeros((3, *C.shape[1:]), F32)

    @pl.when((j == 0) & (g == 0))
    def _():
        for low in (1, 12):
            C[pl.ds(low, 3), :, pl.ds(8, 8), :] = jnp.zeros((3, 2, 8, 128), F32)

    @pl.when((j == n_gy - 1) & (g == 1))
    def _():
        for low in (1, 12):
            C[pl.ds(low, 3), :, pl.ds(32, 8), :] = jnp.zeros((3, 2, 8, 128), F32)

    wait(cells(4), e1r.at[3])
    layers(2, 5, fine_first)
    layers(11, 14, fine_first)
    last_face(14, C, fine, 8, 32)
    layers(3, 6, fine_second)
    layers(10, 13, fine_second)
    fine_rows = pl.ds(8, 32)

    def fine_residual(m, _):
        lower = left_over(4 + 2 * m, V2, fine, S, 0.5, 8, 32, 1)
        upper = left_over(5 + 2 * m, V2, fine, S, 0.5, 8, 32, 1)
        for t in range(2):
            RS[m, t] = lower[t] + upper[t]
            two = RS[m, t, pl.ds(0, 16, stride=2), :] + RS[m, t, pl.ds(1, 16, stride=2), :]
            MS[m + 3, t, mid_rows, :] = 0.125 * pair_sum(two, 1)

    layers(0, 4, fine_residual)
    send(MS.at[pl.ds(5, 2), :, mid_rows, :], MS.at[pl.ds(1, 2), :, mid_rows, :], mss, msr, (near_x(1), j, g))
    send(MS.at[pl.ds(3, 2), :, mid_rows, :], MS.at[pl.ds(7, 2), :, mid_rows, :], mss, msr, (near_x(-1), j, g))

    send(V2.at[10, :, fine_rows, :], V2.at[2, :, fine_rows, :], vs, vr.at[0], (near_x(1), j, g))
    send(V2.at[5, :, fine_rows, :], V2.at[13, :, fine_rows, :], vs, vr.at[1], (near_x(-1), j, g))

    def coarsest(field, scale):
        parts = []
        for layer in range(2):
            for t in range(2):
                R2[layer, t] = field(2 * layer, t) + field(2 * layer + 1, t)
                two = R2[layer, t, pl.ds(4, 4, stride=2), :] + R2[layer, t, pl.ds(5, 4, stride=2), :]
                parts.append(scale * pair_sum(two, 2))
        return braid(parts)

    own_target = jnp.full((4, 128), tgt[0, 0, 0].astype(F32), F32)
    ES[pl.ds(0, 4), :] = coarsest(lambda m, t: MC[3 + m, t, mid_rows, :], 0.125)
    ES[pl.ds(4, 4), :] = own_target
    EB[2 * NEAR + g] = ES[...]
    for d in (4, 3, 2, 1):
        for sign in (1, -1):
            for core in range(2):
                send(ES, EB.at[2 * (NEAR - sign * d) + g], ebs, ebr, (near_x(sign * d), j, core))
    send(ES, EB.at[2 * NEAR + g], ebs, ebr, (i, j, 1 - g))

    wait(MC.at[pl.ds(0, 6), :, mid_rows, :], mcr)

    @pl.when(i == 0)
    def _():
        MC[pl.ds(0, 3)] = jnp.zeros((3, *MC.shape[1:]), F32)

    @pl.when(i == n_gx - 1)
    def _():
        MC[pl.ds(7, 3)] = jnp.zeros((3, *MC.shape[1:]), F32)

    def mid_first(x, _):
        make_faces(x, MC, mid, 8, 16, 2)

    layers(1, 9, mid_first)
    last_face(9, MC, mid, 8, 16)
    wait(MS.at[pl.ds(0, 4), :, mid_rows, :], msr)

    def mid_start(x, _):
        for t in range(2):
            M1[x, t, mid_rows, :] = ME[x, t, mid_rows, :] * (8.0 * MS[x, t, mid_rows, :])

    layers(1, 9, mid_start)

    def mid_second(x, _):
        sweep(x, M1, M2, mid, MS, 8.0, 8, 16, 2)

    layers(2, 8, mid_second)
    mid_res = [left_over(3 + m, M2, mid, MS, 0.125, 8, 16, 2) for m in range(4)]
    low_src = coarsest(lambda m, t: mid_res[m][t], 0.125)

    pl.semaphore_wait(known.at[1], 2)
    GS[...] = low_src
    FS[pl.ds(0, 1), :] = jnp.sum(low_src, axis=0, keepdims=True)
    FS[pl.ds(1, 1), :] = own_target[:1]
    GB[2 * NEAR + g] = low_src
    for d in sorted(range(NEAR + 1, n_gx - NEAR), key=lambda d: -min(d, n_gx - d)):
        for core in range(2):
            send(FS, FB.at[2 * (n_gx - d - NEAR - 1) + g], fs, fr, (near_x(d), j, core))
    for d in (4, 3, 2, 1):
        for sign in (1, -1):
            for core in range(2):
                send(GS, GB.at[2 * (NEAR - sign * d) + g], gs, gr, (near_x(sign * d), j, core))
    send(GS, GB.at[2 * NEAR + g], gs, gr, (i, j, 1 - g))

    for m in range(4):
        for t in range(2):
            SY[m, t] = M2[3 + m, t, pl.ds(12, 8), :]
    send(SY, Y2.at[g], ys, yr, (i, j, 1 - g))
    send(SY, Y2.at[1 - g], ys, yr, (i, near_y(side), 1 - g))
    for m in range(4):
        for t in range(2):
            M2P[3 + m, t, mid_rows, :] = M2[3 + m, t, mid_rows, :]
    wait(Y2, yr)
    for m in range(4):
        for t in range(2):
            M2P[3 + m, t, pl.ds(9, 1), :] = Y2[0, m, t, pl.ds(5, 1), :]
            M2P[3 + m, t, pl.ds(22, 1), :] = Y2[1, m, t, pl.ds(2, 1), :]
    send(M2P.at[pl.ds(4, 3), :, mid_rows, :], M2P.at[pl.ds(0, 3), :, mid_rows, :], xs, xr, (near_x(1), j, g))
    send(M2P.at[pl.ds(3, 3), :, mid_rows, :], M2P.at[pl.ds(7, 3), :, mid_rows, :], xs, xr, (near_x(-1), j, g))

    wait(EB.at[pl.ds(0, 17)], ebr)
    lane = lanes_of(8)
    row = lax.broadcasted_iota(jnp.int32, (8, 128), 0)
    layer, tile, cell = (lane % 4) // 2, lane % 2, lane // 4
    boxes = 2 * NEAR + 1
    zero = jnp.zeros((8, 128), F32)
    coefs, marks = [], []
    for b in range(boxes):
        first, second = EB[2 * b], EB[2 * b + 1]
        coefs.append(jnp.concatenate([first[:4], second[:4]], axis=0))
        marks.append(jnp.where(tile == 0, jnp.broadcast_to(first[4:5], (8, 128)), jnp.broadcast_to(second[4:5], (8, 128))))
    joined = []
    for b in range(boxes - 1):
        touch = lax.rem(i + b - NEAR + n_gx, n_gx) != n_gx - 1
        joined.append(jnp.where((marks[b] == marks[b + 1]) & touch, 1.0, 0.0))

    def along_x(values):
        down = [pltpu.roll(v, 2, 1) for v in values]
        up = [pltpu.roll(v, 126, 1) for v in values]
        below, above = [], []
        for b in range(boxes):
            before = up[b - 1] * joined[b - 1] if b else zero
            after = down[b + 1] * joined[b] if b < boxes - 1 else zero
            below.append(jnp.where(layer == 0, before, down[b]))
            above.append(jnp.where(layer == 0, up[b], after))
        return below, above

    def along_yz(v):
        return (pltpu.roll(v, 1, 0), pltpu.roll(v, 7, 0), pltpu.roll(v, 4, 1), pltpu.roll(v, 124, 1))

    keeps = (row > 0, row < 7, cell > 0, cell < 31)
    c_below, c_above = along_x(coefs)
    low_faces, low_ease = [], []
    for b in range(boxes):
        c = coefs[b]
        around = [jnp.where(keep, v, 0.0) for keep, v in zip(keeps, along_yz(c))]
        faces = [c + c_below[b], c + c_above[b]] + [c + v for v in around]
        total = faces[0] + faces[1] + faces[2] + faces[3] + faces[4] + faces[5]
        low_faces.append(faces[:2] + [jnp.where(keep, f, 0.0) for keep, f in zip(keeps, faces[2:])])
        low_ease.append(RELAX / total)

    def solve(low, rhs):
        for number in range(BOTTOM):
            below, above = along_x(low)
            fresh = []
            for b in range(boxes):
                around = [below[b], above[b], *along_yz(low[b])]
                total = low_faces[b][0] * around[0]
                for face, value in zip(low_faces[b][1:], around[1:]):
                    total = total + face * value
                if rhs is not None:
                    total = total + 32.0 * rhs[b]
                fresh.append(0.2 * low[b] + low_ease[b] * total)
            low = fresh
        return low[NEAR - 1:NEAR + 2]

    from_mean = solve([jnp.full((8, 128), 4.0, F32)] * boxes, None)
    wait(GB.at[pl.ds(0, 17)], gr)
    rhs = [jnp.concatenate([GB[2 * b], GB[2 * b + 1]], axis=0) for b in range(boxes)]
    from_source = solve([zero] * boxes, rhs)
    sums = [jnp.sum(v, axis=0, keepdims=True) for v in rhs]
    names = [m[:1] for m in marks]
    top_tile = tile[:1]
    src_lane = lax.broadcasted_iota(jnp.int32, (128, 128), 0)
    dst_lane = lax.broadcasted_iota(jnp.int32, (128, 128), 1)
    same_tile = jnp.where(src_lane % 2 == dst_lane % 2, 1.0, 0.0).astype(F32)

    wait(FB, fr)
    for d in range(n_gx - boxes):
        first, second = FB[2 * d], FB[2 * d + 1]
        sums.append(first[:1] + second[:1])
        names.append(jnp.where(top_tile == 0, first[1:], second[1:]))
    sums = exact_dot(jnp.concatenate(sums, axis=0), same_tile)
    names = jnp.concatenate(names, axis=0)
    low = []
    for b in range(3):
        here = NEAR - 1 + b
        same = names == names[here:here + 1]
        total = jnp.sum(jnp.where(same, sums, 0.0), axis=0, keepdims=True)
        number = jnp.sum(jnp.where(same, 512.0, 0.0), axis=0, keepdims=True)
        low.append(from_source[b] + (total / jnp.maximum(number, 1.0)) * from_mean[b])

    for b in range(3):
        SQ[b] = low[b]
    send(SQ, Q.at[:, pl.ds(pl.multiple_of(16 - 16 * g, 8), 8), :], qs, qr, (i, near_y(side), 1 - g))
    for b in range(3):
        Q[b, pl.ds(8, 8), :] = low[b]
    wait(M2P.at[pl.ds(0, 6), :, mid_rows, :], xr)
    wait(SQ, qr)
    for b in range(3):
        fix = jnp.where(g == 0, Q[b, pl.ds(6, 8), :], Q[b, pl.ds(10, 8), :])
        for part, wide in enumerate(unbraid(fix)):
            PK[2 * b + part // 2, part % 2, pl.ds(0, 8, stride=2), :] = wide
            PK[2 * b + part // 2, part % 2, pl.ds(1, 8, stride=2), :] = wide

    def corrected(x, _):
        for t in range(2):
            better = M2P[x, t, mid_rows, :] + PK[(x + 1) // 2, t]
            M3[x, t, mid_rows, :] = jnp.where(MC[x, t, mid_rows, :] > 0.0, better, 0.0)

    layers(0, 10, corrected)

    def mid_third(x, _):
        sweep(x, M3, M4, mid, MS, 8.0, 8, 16, 2)

    layers(1, 9, mid_third)
    wait(V2.at[0, :, fine_rows, :], vr.at[0])
    wait(V2.at[0, :, fine_rows, :], vr.at[1])

    def mid_fourth(x, _):
        sweep(x, M4, M1, mid, MS, 8.0, 8, 16, 2)
        for t in range(2):
            PF[x - 2, t, pl.ds(0, 16, stride=2), :] = M1[x, t, mid_rows, :]
            PF[x - 2, t, pl.ds(1, 16, stride=2), :] = M1[x, t, mid_rows, :]
            for half in range(2):
                V3[2 * x - 2 + half, t, fine_rows, :] = V2[2 * x - 2 + half, t, fine_rows, :] + PF[x - 2, t]

    layers(2, 8, mid_fourth)

    def fine_third(x, _):
        sweep(x, V3, V1, fine, S, 2.0, 15, 18, 1)

    layers(3, 13, fine_third)

    def fine_fourth(x, _):
        at = pl.ds(16, 16)
        sums, own = pull(x, V1, fine, 16, 16, 1)
        for t in range(2):
            FO[x - 4, t] = 0.2 * own[t] + E[x, t, at, :] * (2.0 * S[x, t, at, :] + sums[t])

    layers(4, 12, fine_fourth)

    out_rows = pl.ds(pl.multiple_of(16 * g, 8), 16)
    send(FO.at[:, 1 - g], out.at[:, out_rows, :], os_, or_, (i, j, 1 - g))
    keep = pltpu.make_async_copy(FO.at[:, g], out.at[:, out_rows, :], local.at[2])
    keep.start()

    wait(cells(11), e1s.at[0])
    wait(cells(9), e1s.at[1])
    wait(V2.at[pl.ds(0, 2), :, fine_rows, :], vs)
    wait(MC.at[pl.ds(0, 6), :, mid_rows, :], mcs)
    wait(MS.at[pl.ds(0, 4), :, mid_rows, :], mss)
    wait(EB.at[pl.ds(0, 17)], ebs)
    wait(GB.at[pl.ds(0, 17)], gs)
    wait(FB, fs)
    wait(Y2, ys)
    wait(M2P.at[pl.ds(0, 6), :, mid_rows, :], xs)
    wait(SQ, qs)
    keep.wait()
    wait(FO.at[:, 0], os_)
    wait(out.at[:, pl.ds(0, 16), :], or_)


def solution(mesh):
    n_gx, n_gy = mesh.shape["gx"], mesh.shape["gy"]

    def kernel(*refs):
        cycle(n_gx, n_gy, *refs)

    def per_device(source, beta_cells, target):
        fine = pltpu.VMEM((16, 2, 48, 128), F32)
        mid = pltpu.VMEM((10, 2, 32, 128), F32)
        far = n_gx - 2 * NEAR - 1
        dma = pltpu.SemaphoreType.DMA
        return pl.pallas_call(
            kernel,
            out_shape=jax.ShapeDtypeStruct(source.shape, F32),
            in_specs=[
                pl.BlockSpec(memory_space=pltpu.HBM),
                pl.BlockSpec(memory_space=pltpu.HBM),
                pl.BlockSpec(memory_space=pltpu.SMEM),
            ],
            out_specs=pl.BlockSpec(memory_space=pl.ANY),
            scratch_shapes=[
                *[fine] * 11,
                *[mid] * 13,
                pltpu.VMEM((4, 2, 32, 128), F32),
                pltpu.VMEM((4, 2, 32, 128), F32),
                pltpu.VMEM((2, 2, 16, 128), F32),
                pltpu.VMEM((4, 2, 8, 128), F32),
                pltpu.VMEM((2, 4, 2, 8, 128), F32),
                pltpu.VMEM((8, 128), F32),
                pltpu.VMEM((4 * NEAR + 2, 8, 128), F32),
                pltpu.VMEM((8, 128), F32),
                pltpu.VMEM((4 * NEAR + 2, 4, 128), F32),
                pltpu.VMEM((4, 128), F32),
                pltpu.VMEM((2 * far, 2, 128), F32),
                pltpu.VMEM((2, 128), F32),
                pltpu.VMEM((3, 24, 128), F32),
                pltpu.VMEM((3, 8, 128), F32),
                pltpu.VMEM((6, 2, 16, 128), F32),
                pltpu.VMEM((6, 2, 32, 128), F32),
                pltpu.VMEM((8, 2, 16, 128), F32),
                dma((3,)),
                dma((2,)),
                dma((4,)),
                *[dma] * 19,
                dma((2,)),
                pltpu.SemaphoreType.REGULAR((2,)),
            ],
            compiler_params=pltpu.CompilerParams(
                collective_id=0, has_side_effects=True, vmem_limit_bytes=32 * 2**20
            ),
            name="cycle",
        )(source, beta_cells, target)

    spec = P("gx", "gy", "gz")
    return jax.shard_map(
        per_device, mesh=mesh, in_specs=(spec, spec, spec), out_specs=spec, check_vma=False
    )
```

```python
import jax
import jax.numpy as jnp
from jax import lax
from jax.experimental import pallas as pl
from jax.experimental.pallas import tpu as pltpu
from jax.sharding import PartitionSpec as P


BOTTOM = 6
RELAX = 0.8
F32 = jnp.float32
MESH = pl.DeviceIdType.MESH
NEAR = 4


def layers(low, high, work):
    for x in range(low, high):
        work(x, 0)


def lanes_of(rows):
    return lax.broadcasted_iota(jnp.int32, (rows, 128), 1)


def beside(left_tile, right_tile, step):
    lane = lanes_of(left_tile.shape[0])
    low0, low1 = pltpu.roll(left_tile, step, 1), pltpu.roll(right_tile, step, 1)
    high0, high1 = pltpu.roll(left_tile, 128 - step, 1), pltpu.roll(right_tile, 128 - step, 1)
    below = (low0, jnp.where(lane < step, low0, low1))
    above = (jnp.where(lane >= 128 - step, high1, high0), high1)
    return below, above


def make_faces(x, coef, faces, row, rows, step):
    fx, fy, fl, fr, weight, ease = faces
    at = pl.ds(row, rows)
    own = [coef[x, t, at, :] for t in range(2)]
    below, above = beside(*own, step)
    lane = lanes_of(rows)
    for t in range(2):
        c = own[t]
        low = jnp.where(lane < step, 0.0, below[0]) if t == 0 else below[1]
        high = jnp.where(lane >= 128 - step, 0.0, above[1]) if t == 1 else above[0]
        x_low = c + coef[x - 1, t, at, :]
        y_low = c + coef[x, t, pl.ds(row - 1, rows), :]
        z_low, z_high = c + low, c + high
        total = (
            x_low
            + (c + coef[x + 1, t, at, :])
            + y_low
            + (c + coef[x, t, pl.ds(row + 1, rows), :])
            + z_low
            + z_high
        )
        fx[x, t, at, :] = x_low
        fy[x, t, at, :] = y_low
        fl[x, t, at, :] = jnp.where(lane < step, 0.0, z_low) if t == 0 else z_low
        fr[x, t, at, :] = jnp.where(lane >= 128 - step, 0.0, z_high) if t == 1 else z_high
        weight[x, t, at, :] = total
        ease[x, t, at, :] = jnp.where(c > 0.0, RELAX / total, 0.0)


def last_face(x, coef, faces, row, rows):
    at = pl.ds(row, rows)
    for t in range(2):
        faces[0][x, t, at, :] = coef[x, t, at, :] + coef[x - 1, t, at, :]


def pull(x, field, faces, row, rows, step):
    fx, fy, fl, fr = faces[:4]
    at = pl.ds(row, rows)
    own = [field[x, t, at, :] for t in range(2)]
    below, above = beside(*own, step)
    sums = []
    for t in range(2):
        sums.append(
            fx[x, t, at, :] * field[x - 1, t, at, :]
            + fx[x + 1, t, at, :] * field[x + 1, t, at, :]
            + fy[x, t, at, :] * field[x, t, pl.ds(row - 1, rows), :]
            + fy[x, t, pl.ds(row + 1, rows), :] * field[x, t, pl.ds(row + 1, rows), :]
            + fl[x, t, at, :] * below[t]
            + fr[x, t, at, :] * above[t]
        )
    return sums, own


def sweep(x, field, out, faces, source, gain, row, rows, step):
    at = pl.ds(row, rows)
    sums, own = pull(x, field, faces, row, rows, step)
    for t in range(2):
        out[x, t, at, :] = 0.2 * own[t] + faces[5][x, t, at, :] * (gain * source[x, t, at, :] + sums[t])


def left_over(x, field, faces, source, half, row, rows, step):
    at = pl.ds(row, rows)
    sums, own = pull(x, field, faces, row, rows, step)
    return [source[x, t, at, :] - half * (faces[4][x, t, at, :] * own[t] - sums[t]) for t in range(2)]


def pair_sum(value, step):
    lane = lanes_of(value.shape[0])
    other = jnp.where((lane // step) % 2 == 0, pltpu.roll(value, 128 - step, 1), pltpu.roll(value, step, 1))
    return value + other


def exact_dot(a, b):
    return jnp.dot(a, b, precision=lax.Precision.HIGHEST, preferred_element_type=F32)


def braid(parts):
    kind = lanes_of(parts[0].shape[0]) % 4
    return jnp.where(kind < 2, jnp.where(kind == 0, parts[0], parts[1]), jnp.where(kind == 2, parts[2], parts[3]))


def unbraid(value):
    lane = lanes_of(value.shape[0])
    even, upper = lane % 2 == 0, lane % 4 >= 2
    pairs = (jnp.where(even, value, pltpu.roll(value, 1, 1)), jnp.where(even, pltpu.roll(value, 127, 1), value))
    return [
        jnp.where(upper, pltpu.roll(pair, 2, 1), pair) if half == 0 else jnp.where(upper, pair, pltpu.roll(pair, 126, 1))
        for half in range(2)
        for pair in pairs
    ]


def cycle(n_gx, n_gy, src, beta, tgt, out, *scratch):
    (C, S, FX, FY, FL, FR, W, E, V1, V2, V3,
     MC, MS, MFX, MFY, MFL, MFR, MW, ME, M1, M2, M2P, M3, M4,
     RS, RC, R2, SY, Y2, SX, EB, ES, GB, GS, FB, FS, Q, SQ, PK, PF, FO,
     local, e1s, e1r, mcs, mcr, mss, msr, ebs, ebr, gs, gr, fs, fr, ys, yr, xs, xr, qs, qr, os_, or_, vs, vr, known) = scratch
    i, j, g = lax.axis_index("gx"), lax.axis_index("gy"), lax.axis_index("gz")
    fine = (FX, FY, FL, FR, W, E)
    mid = (MFX, MFY, MFL, MFR, MW, ME)

    def near_x(d):
        return lax.rem(i + d + n_gx, n_gx)

    def near_y(d):
        return lax.rem(j + d + n_gy, n_gy)

    def send(source, target, send_sem, recv_sem, where):
        pltpu.make_async_remote_copy(
            src_ref=source, dst_ref=target, send_sem=send_sem, recv_sem=recv_sem,
            device_id=where, device_id_type=MESH,
        ).start()

    def tell(step):
        for sign in (1, -1):
            pl.semaphore_signal(known.at[step], inc=1, device_id=(near_x(sign * 3), j, g), device_id_type=MESH)

    def wait(ref, sem):
        pltpu.make_async_copy(ref, ref, sem).wait()

    own_rows = pl.ds(pl.multiple_of(8 * g, 8), 24)
    own_at = pl.ds(pl.multiple_of(16 - 8 * g, 8), 24)
    pltpu.make_async_copy(beta.at[:, own_rows, :], C.at[pl.ds(4, 8), g, own_at, :], local.at[0]).start()
    pltpu.make_async_copy(src.at[:, own_rows, :], S.at[pl.ds(4, 8), g, own_at, :], local.at[1]).start()

    barrier = pltpu.get_barrier_semaphore()
    side = 2 * g - 1
    up, down = j < n_gy - 1, j > 0
    has_side = jnp.where(g == 0, j, n_gy - 1 - j) > 0

    def greet(where):
        pl.semaphore_signal(barrier, inc=1, device_id=where, device_id_type=MESH)

    @pl.when(has_side)
    def _():
        for dx in (-1, 0, 1):
            for core in range(2):
                greet((near_x(dx), near_y(side), core))

    for dx in (3, 2, 1):
        for sign in (1, -1):
            for core in range(2 if dx < 3 else 1):
                greet((near_x(sign * dx), j, core if dx < 3 else g))
    greet((i, j, 1 - g))
    pl.semaphore_wait(barrier, 11 + 3 * (up.astype(jnp.int32) + down.astype(jnp.int32)))
    tell(0)

    fields = ((beta, C, 3), (src, S, 2))
    for index, (field, target, deep) in enumerate(fields):
        for dx in (1, -1):
            part = pl.ds(8 - deep, deep) if dx == 1 else pl.ds(0, deep)
            place = pl.ds(4 - deep, deep) if dx == 1 else pl.ds(12, deep)
            for core in range(2):
                send(field.at[part, pl.ds(8 * core, 24), :], target.at[place, g, pl.ds(16 - 8 * core, 24), :],
                     e1s.at[index, 0], e1r.at[index, 0], (near_x(dx), j, core))
    for index, (field, target, _) in enumerate(fields):
        send(field.at[:, pl.ds(pl.multiple_of(8 - 8 * g, 8), 24), :],
             target.at[pl.ds(4, 8), g, pl.ds(pl.multiple_of(8 + 8 * g, 8), 24), :],
             e1s.at[index, 1], e1r.at[index, 1], (i, j, 1 - g))
    for core, there, theirs, ours in ((0, up, 8, 24), (1, down, 32, 0)):

        @pl.when(there)
        def _():
            far_y = near_y(1 - 2 * core)
            for index, (field, target, _) in enumerate(fields):
                send(field.at[:, pl.ds(ours, 8), :], target.at[pl.ds(4, 8), g, pl.ds(theirs, 8), :],
                     e1s.at[index, 2 + core], e1r.at[index, 2], (i, far_y, core))
            for index, (field, target, deep) in enumerate(fields):
                for dx in (1, -1):
                    part = pl.ds(8 - deep, deep) if dx == 1 else pl.ds(0, deep)
                    place = pl.ds(4 - deep, deep) if dx == 1 else pl.ds(12, deep)
                    send(field.at[part, pl.ds(ours, 8), :], target.at[place, g, pl.ds(theirs, 8), :],
                         e1s.at[index, 4 + core], e1r.at[index, 3], (near_x(dx), far_y, core))

    def outside(edge, row):
        @pl.when(edge)
        def _():
            for field in (C, S):
                field[:, :, pl.ds(row, 8), :] = jnp.zeros((16, 2, 8, 128), F32)

    outside((j == 0) & (g == 0), 8)
    outside((j == n_gy - 1) & (g == 1), 32)

    def cells(layers, rows, tiles=2):
        return C.at[pl.ds(0, layers), pl.ds(0, tiles), pl.ds(0, rows), :]

    wait(beta.at[:, pl.ds(0, 24), :], local.at[0])
    wait(cells(8, 24, 1), e1r.at[0, 1])

    @pl.when(has_side)
    def _():
        wait(cells(8, 8), e1r.at[0, 2])

    def mid_coefficient(m, _):
        for t in range(2):
            RC[m, t] = C[4 + 2 * m, t, pl.ds(8, 32), :] + C[5 + 2 * m, t, pl.ds(8, 32), :]
            two = RC[m, t, pl.ds(0, 16, stride=2), :] + RC[m, t, pl.ds(1, 16, stride=2), :]
            MC[m + 3, t, pl.ds(8, 16), :] = 0.125 * pair_sum(two, 1)

    layers(0, 4, mid_coefficient)
    mid_rows = pl.ds(8, 16)
    send(MC.at[pl.ds(4, 3), :, mid_rows, :], MC.at[pl.ds(0, 3), :, mid_rows, :], mcs, mcr, (near_x(1), j, g))
    send(MC.at[pl.ds(3, 3), :, mid_rows, :], MC.at[pl.ds(7, 3), :, mid_rows, :], mcs, mcr, (near_x(-1), j, g))

    pl.semaphore_wait(known.at[0], 2)
    tell(1)

    wait(src.at[:, pl.ds(0, 24), :], local.at[1])
    wait(cells(8, 24, 1), e1r.at[1, 1])

    @pl.when(has_side)
    def _():
        wait(cells(8, 8), e1r.at[1, 2])


    def fine_first(x, _):
        make_faces(x, C, fine, 8, 32, 1)
        for t in range(2):
            V1[x, t, pl.ds(8, 32), :] = E[x, t, pl.ds(8, 32), :] * (2.0 * S[x, t, pl.ds(8, 32), :])

    def fine_second(x, _):
        sweep(x, V1, V2, fine, S, 2.0, 8, 32, 1)

    layers(5, 11, fine_first)
    layers(6, 10, fine_second)

    wait(cells(6, 24), e1r.at[0, 0])

    @pl.when(has_side)
    def _():
        wait(cells(6, 8), e1r.at[0, 3])


    @pl.when(i == 0)
    def _():
        C[pl.ds(1, 3)] = jnp.zeros((3, *C.shape[1:]), F32)

    @pl.when(i == n_gx - 1)
    def _():
        C[pl.ds(12, 3)] = jnp.zeros((3, *C.shape[1:]), F32)

    wait(cells(4, 24), e1r.at[1, 0])

    @pl.when(has_side)
    def _():
        wait(cells(4, 8), e1r.at[1, 3])

    layers(2, 5, fine_first)
    layers(11, 14, fine_first)
    last_face(14, C, fine, 8, 32)
    layers(3, 6, fine_second)
    layers(10, 13, fine_second)
    fine_rows = pl.ds(8, 32)

    def fine_residual(m, _):
        lower = left_over(4 + 2 * m, V2, fine, S, 0.5, 8, 32, 1)
        upper = left_over(5 + 2 * m, V2, fine, S, 0.5, 8, 32, 1)
        for t in range(2):
            RS[m, t] = lower[t] + upper[t]
            two = RS[m, t, pl.ds(0, 16, stride=2), :] + RS[m, t, pl.ds(1, 16, stride=2), :]
            MS[m + 3, t, mid_rows, :] = 0.125 * pair_sum(two, 1)

    layers(0, 4, fine_residual)
    send(MS.at[pl.ds(5, 2), :, mid_rows, :], MS.at[pl.ds(1, 2), :, mid_rows, :], mss, msr, (near_x(1), j, g))
    send(MS.at[pl.ds(3, 2), :, mid_rows, :], MS.at[pl.ds(7, 2), :, mid_rows, :], mss, msr, (near_x(-1), j, g))

    send(V2.at[10, :, fine_rows, :], V2.at[2, :, fine_rows, :], vs, vr.at[0], (near_x(1), j, g))
    send(V2.at[5, :, fine_rows, :], V2.at[13, :, fine_rows, :], vs, vr.at[1], (near_x(-1), j, g))

    def coarsest(field, scale):
        parts = []
        for layer in range(2):
            for t in range(2):
                R2[layer, t] = field(2 * layer, t) + field(2 * layer + 1, t)
                two = R2[layer, t, pl.ds(4, 4, stride=2), :] + R2[layer, t, pl.ds(5, 4, stride=2), :]
                parts.append(scale * pair_sum(two, 2))
        return braid(parts)

    own_target = jnp.full((4, 128), tgt[0, 0, 0].astype(F32), F32)
    ES[pl.ds(0, 4), :] = coarsest(lambda m, t: MC[3 + m, t, mid_rows, :], 0.125)
    ES[pl.ds(4, 4), :] = own_target
    EB[2 * NEAR + g] = ES[...]
    for d in (4, 3, 2, 1):
        for sign in (1, -1):
            for core in range(2):
                send(ES, EB.at[2 * (NEAR - sign * d) + g], ebs, ebr, (near_x(sign * d), j, core))
    send(ES, EB.at[2 * NEAR + g], ebs, ebr, (i, j, 1 - g))

    wait(MC.at[pl.ds(0, 6), :, mid_rows, :], mcr)

    @pl.when(i == 0)
    def _():
        MC[pl.ds(0, 3)] = jnp.zeros((3, *MC.shape[1:]), F32)

    @pl.when(i == n_gx - 1)
    def _():
        MC[pl.ds(7, 3)] = jnp.zeros((3, *MC.shape[1:]), F32)

    def mid_first(x, _):
        make_faces(x, MC, mid, 8, 16, 2)

    layers(1, 9, mid_first)
    last_face(9, MC, mid, 8, 16)
    wait(MS.at[pl.ds(0, 4), :, mid_rows, :], msr)

    def mid_start(x, _):
        for t in range(2):
            M1[x, t, mid_rows, :] = ME[x, t, mid_rows, :] * (8.0 * MS[x, t, mid_rows, :])

    layers(1, 9, mid_start)

    def mid_second(x, _):
        sweep(x, M1, M2, mid, MS, 8.0, 8, 16, 2)

    layers(2, 8, mid_second)
    mid_res = [left_over(3 + m, M2, mid, MS, 0.125, 8, 16, 2) for m in range(4)]
    low_src = coarsest(lambda m, t: mid_res[m][t], 0.125)

    pl.semaphore_wait(known.at[1], 2)
    GS[...] = low_src
    FS[pl.ds(0, 1), :] = jnp.sum(low_src, axis=0, keepdims=True)
    FS[pl.ds(1, 1), :] = own_target[:1]
    GB[2 * NEAR + g] = low_src
    for d in sorted(range(NEAR + 1, n_gx - NEAR), key=lambda d: -min(d, n_gx - d)):
        for core in range(2):
            send(FS, FB.at[2 * (n_gx - d - NEAR - 1) + g], fs, fr, (near_x(d), j, core))
    for d in (4, 3, 2, 1):
        for sign in (1, -1):
            for core in range(2):
                send(GS, GB.at[2 * (NEAR - sign * d) + g], gs, gr, (near_x(sign * d), j, core))
    send(GS, GB.at[2 * NEAR + g], gs, gr, (i, j, 1 - g))

    for m in range(4):
        for t in range(2):
            SY[m, t] = M2[3 + m, t, pl.ds(12, 8), :]
    send(SY, Y2.at[g], ys.at[0], yr.at[0], (i, j, 1 - g))

    @pl.when(has_side)
    def _():
        send(SY, Y2.at[1 - g], ys.at[1], yr.at[1], (i, near_y(side), 1 - g))

    for m in range(4):
        for t in range(2):
            M2P[3 + m, t, mid_rows, :] = M2[3 + m, t, mid_rows, :]
    wait(Y2.at[0], yr.at[0])

    @pl.when(has_side)
    def _():
        wait(Y2.at[0], yr.at[1])

    for m in range(4):
        for t in range(2):
            M2P[3 + m, t, pl.ds(9, 1), :] = Y2[0, m, t, pl.ds(5, 1), :]
            M2P[3 + m, t, pl.ds(22, 1), :] = Y2[1, m, t, pl.ds(2, 1), :]
    send(M2P.at[pl.ds(4, 3), :, mid_rows, :], M2P.at[pl.ds(0, 3), :, mid_rows, :], xs, xr, (near_x(1), j, g))
    send(M2P.at[pl.ds(3, 3), :, mid_rows, :], M2P.at[pl.ds(7, 3), :, mid_rows, :], xs, xr, (near_x(-1), j, g))

    wait(EB.at[pl.ds(0, 17)], ebr)
    lane = lanes_of(8)
    row = lax.broadcasted_iota(jnp.int32, (8, 128), 0)
    layer, tile, cell = (lane % 4) // 2, lane % 2, lane // 4
    boxes = 2 * NEAR + 1
    zero = jnp.zeros((8, 128), F32)
    coefs, marks = [], []
    for b in range(boxes):
        first, second = EB[2 * b], EB[2 * b + 1]
        coefs.append(jnp.concatenate([first[:4], second[:4]], axis=0))
        marks.append(jnp.where(tile == 0, jnp.broadcast_to(first[4:5], (8, 128)), jnp.broadcast_to(second[4:5], (8, 128))))
    joined = []
    for b in range(boxes - 1):
        touch = lax.rem(i + b - NEAR + n_gx, n_gx) != n_gx - 1
        joined.append(jnp.where((marks[b] == marks[b + 1]) & touch, 1.0, 0.0))

    def along_x(values):
        down = [pltpu.roll(v, 2, 1) for v in values]
        up = [pltpu.roll(v, 126, 1) for v in values]
        below, above = [], []
        for b in range(boxes):
            before = up[b - 1] * joined[b - 1] if b else zero
            after = down[b + 1] * joined[b] if b < boxes - 1 else zero
            below.append(jnp.where(layer == 0, before, down[b]))
            above.append(jnp.where(layer == 0, up[b], after))
        return below, above

    def along_yz(v):
        return (pltpu.roll(v, 1, 0), pltpu.roll(v, 7, 0), pltpu.roll(v, 4, 1), pltpu.roll(v, 124, 1))

    keeps = (row > 0, row < 7, cell > 0, cell < 31)
    c_below, c_above = along_x(coefs)
    low_faces, low_ease = [], []
    for b in range(boxes):
        c = coefs[b]
        around = [jnp.where(keep, v, 0.0) for keep, v in zip(keeps, along_yz(c))]
        faces = [c + c_below[b], c + c_above[b]] + [c + v for v in around]
        total = faces[0] + faces[1] + faces[2] + faces[3] + faces[4] + faces[5]
        low_faces.append(faces[:2] + [jnp.where(keep, f, 0.0) for keep, f in zip(keeps, faces[2:])])
        low_ease.append(RELAX / total)

    def solve(low, rhs):
        for number in range(BOTTOM):
            below, above = along_x(low)
            fresh = []
            for b in range(boxes):
                around = [below[b], above[b], *along_yz(low[b])]
                total = low_faces[b][0] * around[0]
                for face, value in zip(low_faces[b][1:], around[1:]):
                    total = total + face * value
                if rhs is not None:
                    total = total + 32.0 * rhs[b]
                fresh.append(0.2 * low[b] + low_ease[b] * total)
            low = fresh
        return low[NEAR - 1:NEAR + 2]

    from_mean = solve([jnp.full((8, 128), 4.0, F32)] * boxes, None)
    wait(GB.at[pl.ds(0, 17)], gr)
    rhs = [jnp.concatenate([GB[2 * b], GB[2 * b + 1]], axis=0) for b in range(boxes)]
    from_source = solve([zero] * boxes, rhs)
    sums = [jnp.sum(v, axis=0, keepdims=True) for v in rhs]
    names = [m[:1] for m in marks]
    top_tile = tile[:1]
    src_lane = lax.broadcasted_iota(jnp.int32, (128, 128), 0)
    dst_lane = lax.broadcasted_iota(jnp.int32, (128, 128), 1)
    same_tile = jnp.where(src_lane % 2 == dst_lane % 2, 1.0, 0.0).astype(F32)

    wait(FB, fr)
    for d in range(n_gx - boxes):
        first, second = FB[2 * d], FB[2 * d + 1]
        sums.append(first[:1] + second[:1])
        names.append(jnp.where(top_tile == 0, first[1:], second[1:]))
    sums = exact_dot(jnp.concatenate(sums, axis=0), same_tile)
    names = jnp.concatenate(names, axis=0)
    low = []
    for b in range(3):
        here = NEAR - 1 + b
        same = names == names[here:here + 1]
        total = jnp.sum(jnp.where(same, sums, 0.0), axis=0, keepdims=True)
        number = jnp.sum(jnp.where(same, 512.0, 0.0), axis=0, keepdims=True)
        low.append(from_source[b] + (total / jnp.maximum(number, 1.0)) * from_mean[b])

    for b in range(3):
        SQ[b] = low[b]

    @pl.when(has_side)
    def _():
        send(SQ, Q.at[:, pl.ds(pl.multiple_of(16 - 16 * g, 8), 8), :], qs, qr, (i, near_y(side), 1 - g))

    for b in range(3):
        Q[b, pl.ds(8, 8), :] = low[b]
    wait(M2P.at[pl.ds(0, 6), :, mid_rows, :], xr)

    @pl.when(has_side)
    def _():
        wait(SQ, qr)

    for b in range(3):
        fix = jnp.where(g == 0, Q[b, pl.ds(6, 8), :], Q[b, pl.ds(10, 8), :])
        for part, wide in enumerate(unbraid(fix)):
            PK[2 * b + part // 2, part % 2, pl.ds(0, 8, stride=2), :] = wide
            PK[2 * b + part // 2, part % 2, pl.ds(1, 8, stride=2), :] = wide

    def corrected(x, _):
        for t in range(2):
            better = M2P[x, t, mid_rows, :] + PK[(x + 1) // 2, t]
            M3[x, t, mid_rows, :] = jnp.where(MC[x, t, mid_rows, :] > 0.0, better, 0.0)

    layers(0, 10, corrected)

    def mid_third(x, _):
        sweep(x, M3, M4, mid, MS, 8.0, 8, 16, 2)

    layers(1, 9, mid_third)
    wait(V2.at[0, :, fine_rows, :], vr.at[0])
    wait(V2.at[0, :, fine_rows, :], vr.at[1])

    def mid_fourth(x, _):
        sweep(x, M4, M1, mid, MS, 8.0, 8, 16, 2)
        for t in range(2):
            PF[x - 2, t, pl.ds(0, 16, stride=2), :] = M1[x, t, mid_rows, :]
            PF[x - 2, t, pl.ds(1, 16, stride=2), :] = M1[x, t, mid_rows, :]
            for half in range(2):
                V3[2 * x - 2 + half, t, fine_rows, :] = V2[2 * x - 2 + half, t, fine_rows, :] + PF[x - 2, t]

    layers(2, 8, mid_fourth)

    def fine_third(x, _):
        sweep(x, V3, V1, fine, S, 2.0, 15, 18, 1)

    layers(3, 13, fine_third)

    def fine_fourth(x, _):
        at = pl.ds(16, 16)
        sums, own = pull(x, V1, fine, 16, 16, 1)
        for t in range(2):
            FO[x - 4, t] = 0.2 * own[t] + E[x, t, at, :] * (2.0 * S[x, t, at, :] + sums[t])

    layers(4, 12, fine_fourth)

    out_rows = pl.ds(pl.multiple_of(16 * g, 8), 16)
    send(FO.at[:, 1 - g], out.at[:, out_rows, :], os_, or_, (i, j, 1 - g))
    keep = pltpu.make_async_copy(FO.at[:, g], out.at[:, out_rows, :], local.at[2])
    keep.start()

    for index, deep in ((0, 3), (1, 2)):
        wait(cells(2 * deep, 24), e1s.at[index, 0])
        wait(cells(8, 24, 1), e1s.at[index, 1])
    for core, there in ((0, up), (1, down)):

        @pl.when(there)
        def _():
            for index, deep in ((0, 3), (1, 2)):
                wait(cells(8, 8, 1), e1s.at[index, 2 + core])
                wait(cells(2 * deep, 8, 1), e1s.at[index, 4 + core])

    wait(V2.at[pl.ds(0, 2), :, fine_rows, :], vs)
    wait(MC.at[pl.ds(0, 6), :, mid_rows, :], mcs)
    wait(MS.at[pl.ds(0, 4), :, mid_rows, :], mss)
    wait(EB.at[pl.ds(0, 17)], ebs)
    wait(GB.at[pl.ds(0, 17)], gs)
    wait(FB, fs)
    wait(Y2.at[0], ys.at[0])
    wait(M2P.at[pl.ds(0, 6), :, mid_rows, :], xs)

    @pl.when(has_side)
    def _():
        wait(Y2.at[0], ys.at[1])
        wait(SQ, qs)

    keep.wait()
    wait(FO.at[:, 0], os_)
    wait(out.at[:, pl.ds(0, 16), :], or_)


def solution(mesh):
    n_gx, n_gy = mesh.shape["gx"], mesh.shape["gy"]

    def kernel(*refs):
        cycle(n_gx, n_gy, *refs)

    def per_device(source, beta_cells, target):
        fine = pltpu.VMEM((16, 2, 48, 128), F32)
        mid = pltpu.VMEM((10, 2, 32, 128), F32)
        far = n_gx - 2 * NEAR - 1
        dma = pltpu.SemaphoreType.DMA
        return pl.pallas_call(
            kernel,
            out_shape=jax.ShapeDtypeStruct(source.shape, F32),
            in_specs=[
                pl.BlockSpec(memory_space=pltpu.HBM),
                pl.BlockSpec(memory_space=pltpu.HBM),
                pl.BlockSpec(memory_space=pltpu.SMEM),
            ],
            out_specs=pl.BlockSpec(memory_space=pl.ANY),
            scratch_shapes=[
                *[fine] * 11,
                *[mid] * 13,
                pltpu.VMEM((4, 2, 32, 128), F32),
                pltpu.VMEM((4, 2, 32, 128), F32),
                pltpu.VMEM((2, 2, 16, 128), F32),
                pltpu.VMEM((4, 2, 8, 128), F32),
                pltpu.VMEM((2, 4, 2, 8, 128), F32),
                pltpu.VMEM((8, 128), F32),
                pltpu.VMEM((4 * NEAR + 2, 8, 128), F32),
                pltpu.VMEM((8, 128), F32),
                pltpu.VMEM((4 * NEAR + 2, 4, 128), F32),
                pltpu.VMEM((4, 128), F32),
                pltpu.VMEM((2 * far, 2, 128), F32),
                pltpu.VMEM((2, 128), F32),
                pltpu.VMEM((3, 24, 128), F32),
                pltpu.VMEM((3, 8, 128), F32),
                pltpu.VMEM((6, 2, 16, 128), F32),
                pltpu.VMEM((6, 2, 32, 128), F32),
                pltpu.VMEM((8, 2, 16, 128), F32),
                dma((3,)),
                dma((2, 6)),
                dma((2, 4)),
                *[dma] * 10,
                dma((2,)),
                dma((2,)),
                *[dma] * 7,
                dma((2,)),
                pltpu.SemaphoreType.REGULAR((2,)),
            ],
            compiler_params=pltpu.CompilerParams(
                collective_id=0, has_side_effects=True, vmem_limit_bytes=32 * 2**20
            ),
            name="cycle",
        )(source, beta_cells, target)

    spec = P("gx", "gy", "gz")
    return jax.shard_map(
        per_device, mesh=mesh, in_specs=(spec, spec, spec), out_specs=spec, check_vma=False
    )
```

```python
import jax
import jax.numpy as jnp
from jax import lax
from jax.experimental import pallas as pl
from jax.experimental.pallas import tpu as pltpu
from jax.sharding import PartitionSpec as P


BOTTOM = 6
RELAX = 0.8
F32 = jnp.float32
MESH = pl.DeviceIdType.MESH
NEAR = 4


def layers(low, high, work):
    for x in range(low, high):
        work(x, 0)


def lanes_of(rows):
    return lax.broadcasted_iota(jnp.int32, (rows, 128), 1)


def beside(left_tile, right_tile, step):
    lane = lanes_of(left_tile.shape[0])
    low0, low1 = pltpu.roll(left_tile, step, 1), pltpu.roll(right_tile, step, 1)
    high0, high1 = pltpu.roll(left_tile, 128 - step, 1), pltpu.roll(right_tile, 128 - step, 1)
    below = (low0, jnp.where(lane < step, low0, low1))
    above = (jnp.where(lane >= 128 - step, high1, high0), high1)
    return below, above


def make_faces(x, coef, faces, row, rows, step):
    fx, fy, fl, fr, weight, ease = faces
    at = pl.ds(row, rows)
    own = [coef[x, t, at, :] for t in range(2)]
    below, above = beside(*own, step)
    lane = lanes_of(rows)
    for t in range(2):
        c = own[t]
        low = jnp.where(lane < step, 0.0, below[0]) if t == 0 else below[1]
        high = jnp.where(lane >= 128 - step, 0.0, above[1]) if t == 1 else above[0]
        x_low = c + coef[x - 1, t, at, :]
        y_low = c + coef[x, t, pl.ds(row - 1, rows), :]
        z_low, z_high = c + low, c + high
        total = (
            x_low
            + (c + coef[x + 1, t, at, :])
            + y_low
            + (c + coef[x, t, pl.ds(row + 1, rows), :])
            + z_low
            + z_high
        )
        fx[x, t, at, :] = x_low
        fy[x, t, at, :] = y_low
        fl[x, t, at, :] = jnp.where(lane < step, 0.0, z_low) if t == 0 else z_low
        fr[x, t, at, :] = jnp.where(lane >= 128 - step, 0.0, z_high) if t == 1 else z_high
        weight[x, t, at, :] = total
        ease[x, t, at, :] = jnp.where(c > 0.0, RELAX / total, 0.0)


def last_face(x, coef, faces, row, rows):
    at = pl.ds(row, rows)
    for t in range(2):
        faces[0][x, t, at, :] = coef[x, t, at, :] + coef[x - 1, t, at, :]


def pull(x, field, faces, row, rows, step):
    fx, fy, fl, fr = faces[:4]
    at = pl.ds(row, rows)
    own = [field[x, t, at, :] for t in range(2)]
    below, above = beside(*own, step)
    sums = []
    for t in range(2):
        sums.append(
            fx[x, t, at, :] * field[x - 1, t, at, :]
            + fx[x + 1, t, at, :] * field[x + 1, t, at, :]
            + fy[x, t, at, :] * field[x, t, pl.ds(row - 1, rows), :]
            + fy[x, t, pl.ds(row + 1, rows), :] * field[x, t, pl.ds(row + 1, rows), :]
            + fl[x, t, at, :] * below[t]
            + fr[x, t, at, :] * above[t]
        )
    return sums, own


def sweep(x, field, out, faces, source, gain, row, rows, step):
    at = pl.ds(row, rows)
    sums, own = pull(x, field, faces, row, rows, step)
    for t in range(2):
        out[x, t, at, :] = 0.2 * own[t] + faces[5][x, t, at, :] * (gain * source[x, t, at, :] + sums[t])


def left_over(x, field, faces, source, half, row, rows, step):
    at = pl.ds(row, rows)
    sums, own = pull(x, field, faces, row, rows, step)
    return [source[x, t, at, :] - half * (faces[4][x, t, at, :] * own[t] - sums[t]) for t in range(2)]


def pair_sum(value, step):
    lane = lanes_of(value.shape[0])
    other = jnp.where((lane // step) % 2 == 0, pltpu.roll(value, 128 - step, 1), pltpu.roll(value, step, 1))
    return value + other


def exact_dot(a, b):
    return jnp.dot(a, b, precision=lax.Precision.HIGHEST, preferred_element_type=F32)


def braid(parts):
    kind = lanes_of(parts[0].shape[0]) % 4
    return jnp.where(kind < 2, jnp.where(kind == 0, parts[0], parts[1]), jnp.where(kind == 2, parts[2], parts[3]))


def unbraid(value):
    lane = lanes_of(value.shape[0])
    even, upper = lane % 2 == 0, lane % 4 >= 2
    pairs = (jnp.where(even, value, pltpu.roll(value, 1, 1)), jnp.where(even, pltpu.roll(value, 127, 1), value))
    return [
        jnp.where(upper, pltpu.roll(pair, 2, 1), pair) if half == 0 else jnp.where(upper, pair, pltpu.roll(pair, 126, 1))
        for half in range(2)
        for pair in pairs
    ]


def cycle(n_gx, n_gy, src, beta, tgt, out, *scratch):
    (C, S, FX, FY, FL, FR, W, E, V1, V2, V3,
     MC, MS, MFX, MFY, MFL, MFR, MW, ME, M1, M2, M2P, M3, M4,
     RS, RC, R2, SY, Y2, SX, EB, ES, GB, GS, FB, Q, SQ, PK, PF, FO,
     local, e1s, e1r, mcs, mcr, mss, msr, ebs, ebr, gs, gr, fs, fr, ys, yr, xs, xr, qs, qr, os_, or_, vs, vr, ebss, ebsr, gss, gsr, ts, tr, TS, TB, QP, known) = scratch
    i, j, g = lax.axis_index("gx"), lax.axis_index("gy"), lax.axis_index("gz")
    fine = (FX, FY, FL, FR, W, E)
    mid = (MFX, MFY, MFL, MFR, MW, ME)

    def near_x(d):
        return lax.rem(i + d + n_gx, n_gx)

    def near_y(d):
        return lax.rem(j + d + n_gy, n_gy)

    def send(source, target, send_sem, recv_sem, where):
        pltpu.make_async_remote_copy(
            src_ref=source, dst_ref=target, send_sem=send_sem, recv_sem=recv_sem,
            device_id=where, device_id_type=MESH,
        ).start()

    def tell():
        for sign in (1, -1):
            pl.semaphore_signal(known.at[0], inc=1, device_id=(near_x(sign * 4), j, g), device_id_type=MESH)

    def wait(ref, sem):
        pltpu.make_async_copy(ref, ref, sem).wait()

    own_rows = pl.ds(pl.multiple_of(8 * g, 8), 24)
    own_at = pl.ds(pl.multiple_of(16 - 8 * g, 8), 24)
    pltpu.make_async_copy(beta.at[:, own_rows, :], C.at[pl.ds(4, 8), g, own_at, :], local.at[0]).start()
    pltpu.make_async_copy(src.at[:, own_rows, :], S.at[pl.ds(4, 8), g, own_at, :], local.at[1]).start()

    barrier = pltpu.get_barrier_semaphore()
    side = 2 * g - 1
    up, down = j < n_gy - 1, j > 0
    has_side = jnp.where(g == 0, j, n_gy - 1 - j) > 0

    def greet(where):
        pl.semaphore_signal(barrier, inc=1, device_id=where, device_id_type=MESH)

    @pl.when(has_side)
    def _():
        for dx in (-1, 0, 1):
            for core in range(2):
                greet((near_x(dx), near_y(side), core))

    for dx in (4, 3, 2, 1):
        for sign in (1, -1):
            for core in range(2 if dx == 1 else 1):
                greet((near_x(sign * dx), j, core if dx == 1 else g))
    greet((i, j, 1 - g))
    pl.semaphore_wait(barrier, 11 + 3 * (up.astype(jnp.int32) + down.astype(jnp.int32)))
    tell()

    fields = ((beta, C, 3), (src, S, 2))
    for core, there, theirs, ours in ((0, up, 8, 24), (1, down, 32, 0)):

        @pl.when(there)
        def _():
            far_y = near_y(1 - 2 * core)
            for index, (field, target, deep) in enumerate(fields):
                for dx in (1, -1):
                    part = pl.ds(8 - deep, deep) if dx == 1 else pl.ds(0, deep)
                    place = pl.ds(4 - deep, deep) if dx == 1 else pl.ds(12, deep)
                    send(field.at[part, pl.ds(ours, 8), :], target.at[place, g, pl.ds(theirs, 8), :],
                         e1s.at[index, 4 + core], e1r.at[index, 3], (near_x(dx), far_y, core))
            for index, (field, target, _) in enumerate(fields):
                send(field.at[:, pl.ds(ours, 8), :], target.at[pl.ds(4, 8), g, pl.ds(theirs, 8), :],
                     e1s.at[index, 2 + core], e1r.at[index, 2], (i, far_y, core))

    for index, (field, target, deep) in enumerate(fields):
        for dx in (1, -1):
            part = pl.ds(8 - deep, deep) if dx == 1 else pl.ds(0, deep)
            place = pl.ds(4 - deep, deep) if dx == 1 else pl.ds(12, deep)
            for core in range(2):
                send(field.at[part, pl.ds(8 * core, 24), :], target.at[place, g, pl.ds(16 - 8 * core, 24), :],
                     e1s.at[index, 0], e1r.at[index, 0], (near_x(dx), j, core))
    for index, (field, target, _) in enumerate(fields):
        send(field.at[:, pl.ds(pl.multiple_of(8 - 8 * g, 8), 24), :],
             target.at[pl.ds(4, 8), g, pl.ds(pl.multiple_of(8 + 8 * g, 8), 24), :],
             e1s.at[index, 1], e1r.at[index, 1], (i, j, 1 - g))
    def outside(edge, row):
        @pl.when(edge)
        def _():
            for field in (C, S):
                field[:, :, pl.ds(row, 8), :] = jnp.zeros((16, 2, 8, 128), F32)

    outside((j == 0) & (g == 0), 8)
    outside((j == n_gy - 1) & (g == 1), 32)

    def cells(layers, rows, tiles=2):
        return C.at[pl.ds(0, layers), pl.ds(0, tiles), pl.ds(0, rows), :]

    wait(beta.at[:, pl.ds(0, 24), :], local.at[0])
    wait(cells(8, 24, 1), e1r.at[0, 1])

    @pl.when(has_side)
    def _():
        wait(cells(8, 8), e1r.at[0, 2])

    def mid_coefficient(m, _):
        for t in range(2):
            RC[m, t] = C[4 + 2 * m, t, pl.ds(8, 32), :] + C[5 + 2 * m, t, pl.ds(8, 32), :]
            two = RC[m, t, pl.ds(0, 16, stride=2), :] + RC[m, t, pl.ds(1, 16, stride=2), :]
            MC[m + 3, t, pl.ds(8, 16), :] = 0.125 * pair_sum(two, 1)

    layers(0, 4, mid_coefficient)
    mid_rows = pl.ds(8, 16)
    send(MC.at[pl.ds(4, 3), :, mid_rows, :], MC.at[pl.ds(0, 3), :, mid_rows, :], mcs, mcr, (near_x(1), j, g))
    send(MC.at[pl.ds(3, 3), :, mid_rows, :], MC.at[pl.ds(7, 3), :, mid_rows, :], mcs, mcr, (near_x(-1), j, g))

    pl.semaphore_wait(known.at[0], 2)

    @pl.when(has_side)
    def _():
        pl.semaphore_signal(known.at[1], inc=1, device_id=(i, near_y(side), 1 - g), device_id_type=MESH)

    wait(src.at[:, pl.ds(0, 24), :], local.at[1])
    wait(cells(8, 24, 1), e1r.at[1, 1])

    @pl.when(has_side)
    def _():
        wait(cells(8, 8), e1r.at[1, 2])


    def fine_first(x, _):
        make_faces(x, C, fine, 8, 32, 1)
        for t in range(2):
            V1[x, t, pl.ds(8, 32), :] = E[x, t, pl.ds(8, 32), :] * (2.0 * S[x, t, pl.ds(8, 32), :])

    def fine_second(x, _):
        sweep(x, V1, V2, fine, S, 2.0, 8, 32, 1)

    layers(5, 11, fine_first)
    layers(6, 10, fine_second)

    wait(cells(6, 24), e1r.at[0, 0])

    @pl.when(has_side)
    def _():
        wait(cells(6, 8), e1r.at[0, 3])


    @pl.when(i == 0)
    def _():
        C[pl.ds(1, 3)] = jnp.zeros((3, *C.shape[1:]), F32)

    @pl.when(i == n_gx - 1)
    def _():
        C[pl.ds(12, 3)] = jnp.zeros((3, *C.shape[1:]), F32)

    wait(cells(4, 24), e1r.at[1, 0])

    @pl.when(has_side)
    def _():
        wait(cells(4, 8), e1r.at[1, 3])

    layers(2, 5, fine_first)
    layers(11, 14, fine_first)
    last_face(14, C, fine, 8, 32)
    layers(3, 6, fine_second)
    layers(10, 13, fine_second)
    fine_rows = pl.ds(8, 32)

    def fine_residual(m, _):
        lower = left_over(4 + 2 * m, V2, fine, S, 0.5, 8, 32, 1)
        upper = left_over(5 + 2 * m, V2, fine, S, 0.5, 8, 32, 1)
        for t in range(2):
            RS[m, t] = lower[t] + upper[t]
            two = RS[m, t, pl.ds(0, 16, stride=2), :] + RS[m, t, pl.ds(1, 16, stride=2), :]
            MS[m + 3, t, mid_rows, :] = 0.125 * pair_sum(two, 1)

    layers(0, 4, fine_residual)
    send(MS.at[pl.ds(5, 2), :, mid_rows, :], MS.at[pl.ds(1, 2), :, mid_rows, :], mss, msr, (near_x(1), j, g))
    send(MS.at[pl.ds(3, 2), :, mid_rows, :], MS.at[pl.ds(7, 2), :, mid_rows, :], mss, msr, (near_x(-1), j, g))

    send(V2.at[10, :, fine_rows, :], V2.at[2, :, fine_rows, :], vs, vr.at[0], (near_x(1), j, g))
    send(V2.at[5, :, fine_rows, :], V2.at[13, :, fine_rows, :], vs, vr.at[1], (near_x(-1), j, g))

    def coarsest(field, scale):
        parts = []
        for layer in range(2):
            for t in range(2):
                R2[layer, t] = field(2 * layer, t) + field(2 * layer + 1, t)
                two = R2[layer, t, pl.ds(4, 4, stride=2), :] + R2[layer, t, pl.ds(5, 4, stride=2), :]
                parts.append(scale * pair_sum(two, 2))
        return braid(parts)

    own_target = jnp.full((4, 128), tgt[0, 0, 0].astype(F32), F32)
    ES[pl.ds(0, 4), :] = coarsest(lambda m, t: MC[3 + m, t, mid_rows, :], 0.125)
    ES[pl.ds(4, 4), :] = own_target
    EB[2 * NEAR + g] = ES[...]
    for d in (4, 3, 2, 1):
        for sign in (1, -1):
            for core in range(2):
                send(ES, EB.at[2 * (NEAR - sign * d) + g], ebs, ebr, (near_x(sign * d), j, core))
    send(ES, EB.at[2 * NEAR + g], ebss, ebsr, (i, j, 1 - g))

    wait(MC.at[pl.ds(0, 6), :, mid_rows, :], mcr)

    @pl.when(i == 0)
    def _():
        MC[pl.ds(0, 3)] = jnp.zeros((3, *MC.shape[1:]), F32)

    @pl.when(i == n_gx - 1)
    def _():
        MC[pl.ds(7, 3)] = jnp.zeros((3, *MC.shape[1:]), F32)

    def mid_first(x, _):
        make_faces(x, MC, mid, 8, 16, 2)

    layers(1, 9, mid_first)
    last_face(9, MC, mid, 8, 16)
    wait(MS.at[pl.ds(0, 4), :, mid_rows, :], msr)

    def mid_start(x, _):
        for t in range(2):
            M1[x, t, mid_rows, :] = ME[x, t, mid_rows, :] * (8.0 * MS[x, t, mid_rows, :])

    layers(1, 9, mid_start)

    def mid_second(x, _):
        sweep(x, M1, M2, mid, MS, 8.0, 8, 16, 2)

    layers(2, 8, mid_second)
    mid_res = [left_over(3 + m, M2, mid, MS, 0.125, 8, 16, 2) for m in range(4)]
    low_src = coarsest(lambda m, t: mid_res[m][t], 0.125)

    GS[...] = low_src
    GB[2 * NEAR + g] = low_src
    send(GS, GB.at[2 * NEAR + g], gss, gsr, (i, j, 1 - g))
    for d in (4, 3, 2, 1):
        for sign in (1, -1):
            for core in range(2):
                send(GS, GB.at[2 * (NEAR - sign * d) + g], gs, gr, (near_x(sign * d), j, core))
    wait(GB.at[0], gsr)

    wait(EB.at[0], ebsr)
    halves = [EB[2 * NEAR + core][4:5] for core in range(2)]
    TS[pl.ds(0, 1), :] = jnp.sum(low_src + GB[2 * NEAR + 1 - g], axis=0, keepdims=True)
    TS[pl.ds(1, 1), :] = jnp.where(lanes_of(1) % 2 == 0, halves[0], halves[1])

    @pl.when(has_side)
    def _():
        pl.semaphore_wait(known.at[1], 1)

    far_y = near_y(side)
    for d in sorted(range(NEAR + 1, n_gx - NEAR), key=lambda d: -min(d, n_gx - d)):
        slot = n_gx - d - NEAR - 1

        @pl.when(has_side)
        def _():
            send(TS, TB.at[slot], ts, tr, (near_x(d), far_y, 1 - g))

        send(TS, FB.at[slot], fs, fr, (near_x(d), j, g))

    for m in range(4):
        for t in range(2):
            SY[m, t] = M2[3 + m, t, pl.ds(12, 8), :]
    @pl.when(has_side)
    def _():
        send(SY, Y2.at[1 - g], ys.at[1], yr.at[1], (i, near_y(side), 1 - g))

    send(SY, Y2.at[g], ys.at[0], yr.at[0], (i, j, 1 - g))
    for m in range(4):
        for t in range(2):
            M2P[3 + m, t, mid_rows, :] = M2[3 + m, t, mid_rows, :]
    wait(Y2.at[0], yr.at[0])

    @pl.when(has_side)
    def _():
        wait(Y2.at[0], yr.at[1])

    for m in range(4):
        for t in range(2):
            M2P[3 + m, t, pl.ds(9, 1), :] = Y2[0, m, t, pl.ds(5, 1), :]
            M2P[3 + m, t, pl.ds(22, 1), :] = Y2[1, m, t, pl.ds(2, 1), :]
    send(M2P.at[pl.ds(4, 3), :, mid_rows, :], M2P.at[pl.ds(0, 3), :, mid_rows, :], xs, xr, (near_x(1), j, g))
    send(M2P.at[pl.ds(3, 3), :, mid_rows, :], M2P.at[pl.ds(7, 3), :, mid_rows, :], xs, xr, (near_x(-1), j, g))

    wait(EB.at[pl.ds(0, 16)], ebr)
    lane = lanes_of(8)
    row = lax.broadcasted_iota(jnp.int32, (8, 128), 0)
    layer, tile, cell = (lane % 4) // 2, lane % 2, lane // 4
    boxes = 2 * NEAR + 1
    zero = jnp.zeros((8, 128), F32)
    coefs, marks = [], []
    for b in range(boxes):
        first, second = EB[2 * b], EB[2 * b + 1]
        coefs.append(jnp.concatenate([first[:4], second[:4]], axis=0))
        marks.append(jnp.where(tile == 0, jnp.broadcast_to(first[4:5], (8, 128)), jnp.broadcast_to(second[4:5], (8, 128))))
    joined = []
    for b in range(boxes - 1):
        touch = lax.rem(i + b - NEAR + n_gx, n_gx) != n_gx - 1
        joined.append(jnp.where((marks[b] == marks[b + 1]) & touch, 1.0, 0.0))

    def along_x(values):
        down = [pltpu.roll(v, 2, 1) for v in values]
        up = [pltpu.roll(v, 126, 1) for v in values]
        below, above = [], []
        for b in range(boxes):
            before = up[b - 1] * joined[b - 1] if b else zero
            after = down[b + 1] * joined[b] if b < boxes - 1 else zero
            below.append(jnp.where(layer == 0, before, down[b]))
            above.append(jnp.where(layer == 0, up[b], after))
        return below, above

    def along_yz(v):
        return (pltpu.roll(v, 1, 0), pltpu.roll(v, 7, 0), pltpu.roll(v, 4, 1), pltpu.roll(v, 124, 1))

    keeps = (row > 0, row < 7, cell > 0, cell < 31)
    c_below, c_above = along_x(coefs)
    low_faces, low_ease = [], []
    for b in range(boxes):
        c = coefs[b]
        around = [jnp.where(keep, v, 0.0) for keep, v in zip(keeps, along_yz(c))]
        faces = [c + c_below[b], c + c_above[b]] + [c + v for v in around]
        total = faces[0] + faces[1] + faces[2] + faces[3] + faces[4] + faces[5]
        low_faces.append(faces[:2] + [jnp.where(keep, f, 0.0) for keep, f in zip(keeps, faces[2:])])
        low_ease.append(RELAX / total)

    def solve(low, rhs):
        for number in range(BOTTOM):
            below, above = along_x(low)
            fresh = []
            for b in range(boxes):
                around = [below[b], above[b], *along_yz(low[b])]
                total = low_faces[b][0] * around[0]
                for face, value in zip(low_faces[b][1:], around[1:]):
                    total = total + face * value
                if rhs is not None:
                    total = total + 32.0 * rhs[b]
                fresh.append(0.2 * low[b] + low_ease[b] * total)
            low = fresh
        return low[NEAR - 1:NEAR + 2]

    from_mean = solve([jnp.full((8, 128), 4.0, F32)] * boxes, None)
    wait(GB.at[pl.ds(0, 16)], gr)
    rhs = [jnp.concatenate([GB[2 * b], GB[2 * b + 1]], axis=0) for b in range(boxes)]
    from_source = solve([zero] * boxes, rhs)
    sums = [jnp.sum(v, axis=0, keepdims=True) for v in rhs]
    for b in range(3):
        SQ[b] = from_source[b]
        SQ[3 + b] = from_mean[b]
    for b in range(boxes):
        SQ[6 + b // 8, pl.ds(b % 8, 1), :] = sums[b]
        SQ[8 + b // 8, pl.ds(b % 8, 1), :] = marks[b][:1]

    @pl.when(has_side)
    def _():
        send(SQ, QP, qs, qr, (i, near_y(side), 1 - g))

    names = [m[:1] for m in marks]
    src_lane = lax.broadcasted_iota(jnp.int32, (128, 128), 0)
    dst_lane = lax.broadcasted_iota(jnp.int32, (128, 128), 1)
    same_tile = jnp.where(src_lane % 2 == dst_lane % 2, 1.0, 0.0).astype(F32)

    wait(FB, fr)
    for d in range(n_gx - boxes):
        sums.append(FB[d][:1])
        names.append(FB[d][1:])
    @pl.when(has_side)
    def _():
        wait(TB, tr)
        wait(SQ, qr)

    for b in range(boxes):
        sums.append(QP[6 + b // 8, pl.ds(b % 8, 1), :])
        names.append(QP[8 + b // 8, pl.ds(b % 8, 1), :])
    for d in range(n_gx - boxes):
        sums.append(TB[d][:1])
        names.append(TB[d][1:])
    sums = exact_dot(jnp.concatenate(sums, axis=0), same_tile)
    names = jnp.concatenate(names, axis=0)

    def means(first):
        row_sums, row_names = sums[first:first + n_gx], names[first:first + n_gx]
        for place in (NEAR - 1, NEAR, NEAR + 1):
            same = row_names == row_names[place:place + 1]
            total = jnp.sum(jnp.where(same, row_sums, 0.0), axis=0, keepdims=True)
            number = jnp.sum(jnp.where(same, 512.0, 0.0), axis=0, keepdims=True)
            yield total / jnp.maximum(number, 1.0)

    side_at = pl.ds(pl.multiple_of(16 * g, 8), 8)
    for b, mean in enumerate(means(0)):
        Q[b, pl.ds(8, 8), :] = from_source[b] + mean * from_mean[b]
    for b, mean in enumerate(means(n_gx)):
        Q[b, side_at, :] = QP[b] + mean * QP[3 + b]

    wait(M2P.at[pl.ds(0, 6), :, mid_rows, :], xr)

    for b in range(3):
        fix = jnp.where(g == 0, Q[b, pl.ds(6, 8), :], Q[b, pl.ds(10, 8), :])
        for part, wide in enumerate(unbraid(fix)):
            PK[2 * b + part // 2, part % 2, pl.ds(0, 8, stride=2), :] = wide
            PK[2 * b + part // 2, part % 2, pl.ds(1, 8, stride=2), :] = wide

    def corrected(x, _):
        for t in range(2):
            better = M2P[x, t, mid_rows, :] + PK[(x + 1) // 2, t]
            M3[x, t, mid_rows, :] = jnp.where(MC[x, t, mid_rows, :] > 0.0, better, 0.0)

    layers(0, 10, corrected)

    def mid_third(x, _):
        sweep(x, M3, M4, mid, MS, 8.0, 8, 16, 2)

    layers(1, 9, mid_third)
    wait(V2.at[0, :, fine_rows, :], vr.at[0])
    wait(V2.at[0, :, fine_rows, :], vr.at[1])

    def mid_fourth(x, _):
        sweep(x, M4, M1, mid, MS, 8.0, 8, 16, 2)
        for t in range(2):
            PF[x - 2, t, pl.ds(0, 16, stride=2), :] = M1[x, t, mid_rows, :]
            PF[x - 2, t, pl.ds(1, 16, stride=2), :] = M1[x, t, mid_rows, :]
            for half in range(2):
                V3[2 * x - 2 + half, t, fine_rows, :] = V2[2 * x - 2 + half, t, fine_rows, :] + PF[x - 2, t]

    layers(2, 8, mid_fourth)

    def fine_third(x, _):
        sweep(x, V3, V1, fine, S, 2.0, 15, 18, 1)

    layers(3, 13, fine_third)

    def fine_fourth(x, _):
        at = pl.ds(16, 16)
        sums, own = pull(x, V1, fine, 16, 16, 1)
        for t in range(2):
            FO[x - 4, t] = 0.2 * own[t] + E[x, t, at, :] * (2.0 * S[x, t, at, :] + sums[t])

    layers(4, 12, fine_fourth)

    out_rows = pl.ds(pl.multiple_of(16 * g, 8), 16)
    send(FO.at[:, 1 - g], out.at[:, out_rows, :], os_, or_, (i, j, 1 - g))
    keep = pltpu.make_async_copy(FO.at[:, g], out.at[:, out_rows, :], local.at[2])
    keep.start()

    for index, deep in ((0, 3), (1, 2)):
        wait(cells(2 * deep, 24), e1s.at[index, 0])
        wait(cells(8, 24, 1), e1s.at[index, 1])
    for core, there in ((0, up), (1, down)):

        @pl.when(there)
        def _():
            for index, deep in ((0, 3), (1, 2)):
                wait(cells(8, 8, 1), e1s.at[index, 2 + core])
                wait(cells(2 * deep, 8, 1), e1s.at[index, 4 + core])

    wait(V2.at[pl.ds(0, 2), :, fine_rows, :], vs)
    wait(MC.at[pl.ds(0, 6), :, mid_rows, :], mcs)
    wait(MS.at[pl.ds(0, 4), :, mid_rows, :], mss)
    wait(EB.at[pl.ds(0, 16)], ebs)
    wait(EB.at[0], ebss)
    wait(GB.at[pl.ds(0, 16)], gs)
    wait(GB.at[0], gss)
    wait(FB, fs)
    wait(Y2.at[0], ys.at[0])
    wait(M2P.at[pl.ds(0, 6), :, mid_rows, :], xs)

    @pl.when(has_side)
    def _():
        wait(Y2.at[0], ys.at[1])
        wait(SQ, qs)
        wait(TB, ts)

    keep.wait()
    wait(FO.at[:, 0], os_)
    wait(out.at[:, pl.ds(0, 16), :], or_)


def solution(mesh):
    n_gx, n_gy = mesh.shape["gx"], mesh.shape["gy"]

    def kernel(*refs):
        cycle(n_gx, n_gy, *refs)

    def per_device(source, beta_cells, target):
        fine = pltpu.VMEM((16, 2, 48, 128), F32)
        mid = pltpu.VMEM((10, 2, 32, 128), F32)
        far = n_gx - 2 * NEAR - 1
        dma = pltpu.SemaphoreType.DMA
        return pl.pallas_call(
            kernel,
            out_shape=jax.ShapeDtypeStruct(source.shape, F32),
            in_specs=[
                pl.BlockSpec(memory_space=pltpu.HBM),
                pl.BlockSpec(memory_space=pltpu.HBM),
                pl.BlockSpec(memory_space=pltpu.SMEM),
            ],
            out_specs=pl.BlockSpec(memory_space=pl.ANY),
            scratch_shapes=[
                *[fine] * 11,
                *[mid] * 13,
                pltpu.VMEM((4, 2, 32, 128), F32),
                pltpu.VMEM((4, 2, 32, 128), F32),
                pltpu.VMEM((2, 2, 16, 128), F32),
                pltpu.VMEM((4, 2, 8, 128), F32),
                pltpu.VMEM((2, 4, 2, 8, 128), F32),
                pltpu.VMEM((8, 128), F32),
                pltpu.VMEM((4 * NEAR + 2, 8, 128), F32),
                pltpu.VMEM((8, 128), F32),
                pltpu.VMEM((4 * NEAR + 2, 4, 128), F32),
                pltpu.VMEM((4, 128), F32),
                pltpu.VMEM((far, 2, 128), F32),
                pltpu.VMEM((3, 24, 128), F32),
                pltpu.VMEM((10, 8, 128), F32),
                pltpu.VMEM((6, 2, 16, 128), F32),
                pltpu.VMEM((6, 2, 32, 128), F32),
                pltpu.VMEM((8, 2, 16, 128), F32),
                dma((3,)),
                dma((2, 6)),
                dma((2, 4)),
                *[dma] * 10,
                dma((2,)),
                dma((2,)),
                *[dma] * 7,
                dma((2,)),
                *[dma] * 6,
                pltpu.VMEM((2, 128), F32),
                pltpu.VMEM((far, 2, 128), F32),
                pltpu.VMEM((10, 8, 128), F32),
                pltpu.SemaphoreType.REGULAR((2,)),
            ],
            compiler_params=pltpu.CompilerParams(
                collective_id=0, has_side_effects=True, vmem_limit_bytes=32 * 2**20
            ),
            name="cycle",
        )(source, beta_cells, target)

    spec = P("gx", "gy", "gz")
    return jax.shard_map(
        per_device, mesh=mesh, in_specs=(spec, spec, spec), out_specs=spec, check_vma=False
    )
```

```python
import jax
import jax.numpy as jnp
from jax import lax
from jax.experimental import pallas as pl
from jax.experimental.pallas import tpu as pltpu
from jax.sharding import PartitionSpec as P


BOTTOM = 6
RELAX = 0.8
F32 = jnp.float32
MESH = pl.DeviceIdType.MESH
NEAR = 4


def layers(low, high, work):
    for x in range(low, high):
        work(x, 0)


def lanes_of(rows):
    return lax.broadcasted_iota(jnp.int32, (rows, 128), 1)


def beside(left_tile, right_tile, step):
    lane = lanes_of(left_tile.shape[0])
    low0, low1 = pltpu.roll(left_tile, step, 1), pltpu.roll(right_tile, step, 1)
    high0, high1 = pltpu.roll(left_tile, 128 - step, 1), pltpu.roll(right_tile, 128 - step, 1)
    below = (low0, jnp.where(lane < step, low0, low1))
    above = (jnp.where(lane >= 128 - step, high1, high0), high1)
    return below, above


def make_faces(x, coef, faces, row, rows, step):
    fx, fy, fl, fr, weight, ease = faces
    at = pl.ds(row, rows)
    own = [coef[x, t, at, :] for t in range(2)]
    below, above = beside(*own, step)
    lane = lanes_of(rows)
    for t in range(2):
        c = own[t]
        low = jnp.where(lane < step, 0.0, below[0]) if t == 0 else below[1]
        high = jnp.where(lane >= 128 - step, 0.0, above[1]) if t == 1 else above[0]
        x_low = c + coef[x - 1, t, at, :]
        y_low = c + coef[x, t, pl.ds(row - 1, rows), :]
        z_low, z_high = c + low, c + high
        total = (
            x_low
            + (c + coef[x + 1, t, at, :])
            + y_low
            + (c + coef[x, t, pl.ds(row + 1, rows), :])
            + z_low
            + z_high
        )
        fx[x, t, at, :] = x_low
        fy[x, t, at, :] = y_low
        fl[x, t, at, :] = jnp.where(lane < step, 0.0, z_low) if t == 0 else z_low
        fr[x, t, at, :] = jnp.where(lane >= 128 - step, 0.0, z_high) if t == 1 else z_high
        weight[x, t, at, :] = total
        ease[x, t, at, :] = jnp.where(c > 0.0, RELAX / total, 0.0)


def last_face(x, coef, faces, row, rows):
    at = pl.ds(row, rows)
    for t in range(2):
        faces[0][x, t, at, :] = coef[x, t, at, :] + coef[x - 1, t, at, :]


def pull(x, field, faces, row, rows, step):
    fx, fy, fl, fr = faces[:4]
    at = pl.ds(row, rows)
    own = [field[x, t, at, :] for t in range(2)]
    below, above = beside(*own, step)
    sums = []
    for t in range(2):
        sums.append(
            fx[x, t, at, :] * field[x - 1, t, at, :]
            + fx[x + 1, t, at, :] * field[x + 1, t, at, :]
            + fy[x, t, at, :] * field[x, t, pl.ds(row - 1, rows), :]
            + fy[x, t, pl.ds(row + 1, rows), :] * field[x, t, pl.ds(row + 1, rows), :]
            + fl[x, t, at, :] * below[t]
            + fr[x, t, at, :] * above[t]
        )
    return sums, own


def sweep(x, field, out, faces, source, gain, row, rows, step):
    at = pl.ds(row, rows)
    sums, own = pull(x, field, faces, row, rows, step)
    for t in range(2):
        out[x, t, at, :] = 0.2 * own[t] + faces[5][x, t, at, :] * (gain * source[x, t, at, :] + sums[t])


def left_over(x, field, faces, source, half, row, rows, step):
    at = pl.ds(row, rows)
    sums, own = pull(x, field, faces, row, rows, step)
    return [source[x, t, at, :] - half * (faces[4][x, t, at, :] * own[t] - sums[t]) for t in range(2)]


def pair_sum(value, step):
    lane = lanes_of(value.shape[0])
    other = jnp.where((lane // step) % 2 == 0, pltpu.roll(value, 128 - step, 1), pltpu.roll(value, step, 1))
    return value + other


def exact_dot(a, b):
    return jnp.dot(a, b, precision=lax.Precision.HIGHEST, preferred_element_type=F32)


def braid(parts):
    kind = lanes_of(parts[0].shape[0]) % 4
    return jnp.where(kind < 2, jnp.where(kind == 0, parts[0], parts[1]), jnp.where(kind == 2, parts[2], parts[3]))


def unbraid(value):
    lane = lanes_of(value.shape[0])
    even, upper = lane % 2 == 0, lane % 4 >= 2
    pairs = (jnp.where(even, value, pltpu.roll(value, 1, 1)), jnp.where(even, pltpu.roll(value, 127, 1), value))
    return [
        jnp.where(upper, pltpu.roll(pair, 2, 1), pair) if half == 0 else jnp.where(upper, pair, pltpu.roll(pair, 126, 1))
        for half in range(2)
        for pair in pairs
    ]


def cycle(n_gx, n_gy, src, beta, tgt, out, *scratch):
    (C, S, FX, FY, FL, FR, W, E, V1, V2, V3,
     MC, MS, MFX, MFY, MFL, MFR, MW, ME, M1, M2, M2P, M3, M4,
     RS, RC, R2, SY, Y2, SX, EB, ES, GB, GS, FB, Q, SQ, PK, PF, FO,
     local, e1s, e1r, mcs, mcr, mss, msr, ebs, ebr, gs, gr, fs, fr, ys, yr, xs, xr, qs, qr, os_, or_, vs, vr, ebss, ebsr, gss, gsr, ts, tr, TS, TB, QP, known) = scratch
    i, j, g = lax.axis_index("gx"), lax.axis_index("gy"), lax.axis_index("gz")
    fine = (FX, FY, FL, FR, W, E)
    mid = (MFX, MFY, MFL, MFR, MW, ME)

    def near_x(d):
        return lax.rem(i + d + n_gx, n_gx)

    def near_y(d):
        return lax.rem(j + d + n_gy, n_gy)

    def send(source, target, send_sem, recv_sem, where):
        pltpu.make_async_remote_copy(
            src_ref=source, dst_ref=target, send_sem=send_sem, recv_sem=recv_sem,
            device_id=where, device_id_type=MESH,
        ).start()

    def tell():
        for sign in (1, -1):
            pl.semaphore_signal(known.at[0], inc=1, device_id=(near_x(sign * 4), j, g), device_id_type=MESH)

    def wait(ref, sem):
        pltpu.make_async_copy(ref, ref, sem).wait()

    own_rows = pl.ds(pl.multiple_of(8 * g, 8), 24)
    own_at = pl.ds(pl.multiple_of(16 - 8 * g, 8), 24)
    pltpu.make_async_copy(beta.at[:, own_rows, :], C.at[pl.ds(4, 8), g, own_at, :], local.at[0]).start()
    pltpu.make_async_copy(src.at[:, own_rows, :], S.at[pl.ds(4, 8), g, own_at, :], local.at[1]).start()

    barrier = pltpu.get_barrier_semaphore()
    side = 2 * g - 1
    up, down = j < n_gy - 1, j > 0
    has_side = jnp.where(g == 0, j, n_gy - 1 - j) > 0

    def greet(where):
        pl.semaphore_signal(barrier, inc=1, device_id=where, device_id_type=MESH)

    @pl.when(has_side)
    def _():
        for dx in (-1, 0, 1):
            for core in range(2):
                greet((near_x(dx), near_y(side), core))

    for dx in (4, 3, 2, 1):
        for sign in (1, -1):
            for core in range(2 if dx == 1 else 1):
                greet((near_x(sign * dx), j, core if dx == 1 else g))
    greet((i, j, 1 - g))
    pl.semaphore_wait(barrier, 11 + 3 * (up.astype(jnp.int32) + down.astype(jnp.int32)))
    tell()

    fields = ((beta, C, 3), (src, S, 2))
    for core, there, theirs, ours in ((0, up, 8, 24), (1, down, 32, 0)):

        @pl.when(there)
        def _():
            far_y = near_y(1 - 2 * core)
            for index, (field, target, deep) in enumerate(fields):
                for dx in (1, -1):
                    part = pl.ds(8 - deep, deep) if dx == 1 else pl.ds(0, deep)
                    place = pl.ds(4 - deep, deep) if dx == 1 else pl.ds(12, deep)
                    send(field.at[part, pl.ds(ours, 8), :], target.at[place, g, pl.ds(theirs, 8), :],
                         e1s.at[index, 4 + core], e1r.at[index, 3], (near_x(dx), far_y, core))
            for index, (field, target, _) in enumerate(fields):
                send(field.at[:, pl.ds(ours, 8), :], target.at[pl.ds(4, 8), g, pl.ds(theirs, 8), :],
                     e1s.at[index, 2 + core], e1r.at[index, 2], (i, far_y, core))

    for index, (field, target, deep) in enumerate(fields):
        for dx in (1, -1):
            part = pl.ds(8 - deep, deep) if dx == 1 else pl.ds(0, deep)
            place = pl.ds(4 - deep, deep) if dx == 1 else pl.ds(12, deep)
            for core in range(2):
                send(field.at[part, pl.ds(8 * core, 24), :], target.at[place, g, pl.ds(16 - 8 * core, 24), :],
                     e1s.at[index, 0], e1r.at[index, 0], (near_x(dx), j, core))
    for index, (field, target, _) in enumerate(fields):
        send(field.at[:, pl.ds(pl.multiple_of(8 - 8 * g, 8), 24), :],
             target.at[pl.ds(4, 8), g, pl.ds(pl.multiple_of(8 + 8 * g, 8), 24), :],
             e1s.at[index, 1], e1r.at[index, 1], (i, j, 1 - g))
    def outside(edge, row):
        @pl.when(edge)
        def _():
            for field in (C, S):
                field[:, :, pl.ds(row, 8), :] = jnp.zeros((16, 2, 8, 128), F32)

    outside((j == 0) & (g == 0), 8)
    outside((j == n_gy - 1) & (g == 1), 32)

    def cells(layers, rows, tiles=2):
        return C.at[pl.ds(0, layers), pl.ds(0, tiles), pl.ds(0, rows), :]

    wait(beta.at[:, pl.ds(0, 24), :], local.at[0])
    wait(cells(8, 24, 1), e1r.at[0, 1])

    @pl.when(has_side)
    def _():
        wait(cells(8, 8), e1r.at[0, 2])

    def mid_coefficient(m, _):
        for t in range(2):
            RC[m, t] = C[4 + 2 * m, t, pl.ds(8, 32), :] + C[5 + 2 * m, t, pl.ds(8, 32), :]
            two = RC[m, t, pl.ds(0, 16, stride=2), :] + RC[m, t, pl.ds(1, 16, stride=2), :]
            MC[m + 3, t, pl.ds(8, 16), :] = 0.125 * pair_sum(two, 1)

    layers(0, 4, mid_coefficient)
    mid_rows = pl.ds(8, 16)
    send(MC.at[pl.ds(4, 3), :, mid_rows, :], MC.at[pl.ds(0, 3), :, mid_rows, :], mcs, mcr, (near_x(1), j, g))
    send(MC.at[pl.ds(3, 3), :, mid_rows, :], MC.at[pl.ds(7, 3), :, mid_rows, :], mcs, mcr, (near_x(-1), j, g))

    wait(src.at[:, pl.ds(0, 24), :], local.at[1])
    wait(cells(8, 24, 1), e1r.at[1, 1])

    @pl.when(has_side)
    def _():
        wait(cells(8, 8), e1r.at[1, 2])


    def fine_first(x, _):
        make_faces(x, C, fine, 8, 32, 1)
        for t in range(2):
            V1[x, t, pl.ds(8, 32), :] = E[x, t, pl.ds(8, 32), :] * (2.0 * S[x, t, pl.ds(8, 32), :])

    def fine_second(x, _):
        sweep(x, V1, V2, fine, S, 2.0, 8, 32, 1)

    layers(5, 11, fine_first)
    layers(6, 10, fine_second)

    pl.semaphore_wait(known.at[0], 2)

    @pl.when(has_side)
    def _():
        pl.semaphore_signal(known.at[1], inc=1, device_id=(i, near_y(side), 1 - g), device_id_type=MESH)

    wait(cells(6, 24), e1r.at[0, 0])

    @pl.when(has_side)
    def _():
        wait(cells(6, 8), e1r.at[0, 3])


    @pl.when(i == 0)
    def _():
        C[pl.ds(1, 3)] = jnp.zeros((3, *C.shape[1:]), F32)

    @pl.when(i == n_gx - 1)
    def _():
        C[pl.ds(12, 3)] = jnp.zeros((3, *C.shape[1:]), F32)

    wait(cells(4, 24), e1r.at[1, 0])

    @pl.when(has_side)
    def _():
        wait(cells(4, 8), e1r.at[1, 3])

    layers(2, 5, fine_first)
    layers(11, 14, fine_first)
    last_face(14, C, fine, 8, 32)
    layers(3, 6, fine_second)
    layers(10, 13, fine_second)
    fine_rows = pl.ds(8, 32)

    def fine_residual(m, _):
        lower = left_over(4 + 2 * m, V2, fine, S, 0.5, 8, 32, 1)
        upper = left_over(5 + 2 * m, V2, fine, S, 0.5, 8, 32, 1)
        for t in range(2):
            RS[m, t] = lower[t] + upper[t]
            two = RS[m, t, pl.ds(0, 16, stride=2), :] + RS[m, t, pl.ds(1, 16, stride=2), :]
            MS[m + 3, t, mid_rows, :] = 0.125 * pair_sum(two, 1)

    layers(0, 4, fine_residual)
    send(MS.at[pl.ds(5, 2), :, mid_rows, :], MS.at[pl.ds(1, 2), :, mid_rows, :], mss, msr, (near_x(1), j, g))
    send(MS.at[pl.ds(3, 2), :, mid_rows, :], MS.at[pl.ds(7, 2), :, mid_rows, :], mss, msr, (near_x(-1), j, g))

    send(V2.at[10, :, fine_rows, :], V2.at[2, :, fine_rows, :], vs, vr.at[0], (near_x(1), j, g))
    send(V2.at[5, :, fine_rows, :], V2.at[13, :, fine_rows, :], vs, vr.at[1], (near_x(-1), j, g))

    def coarsest(field, scale):
        parts = []
        for layer in range(2):
            for t in range(2):
                R2[layer, t] = field(2 * layer, t) + field(2 * layer + 1, t)
                two = R2[layer, t, pl.ds(4, 4, stride=2), :] + R2[layer, t, pl.ds(5, 4, stride=2), :]
                parts.append(scale * pair_sum(two, 2))
        return braid(parts)

    own_target = jnp.full((4, 128), tgt[0, 0, 0].astype(F32), F32)
    ES[pl.ds(0, 4), :] = coarsest(lambda m, t: MC[3 + m, t, mid_rows, :], 0.125)
    ES[pl.ds(4, 4), :] = own_target
    EB[2 * NEAR + g] = ES[...]
    for d in (4, 3, 2, 1):
        for sign in (1, -1):
            for core in range(2):
                send(ES, EB.at[2 * (NEAR - sign * d) + g], ebs, ebr, (near_x(sign * d), j, core))
    send(ES, EB.at[2 * NEAR + g], ebss, ebsr, (i, j, 1 - g))

    wait(MC.at[pl.ds(0, 6), :, mid_rows, :], mcr)

    @pl.when(i == 0)
    def _():
        MC[pl.ds(0, 3)] = jnp.zeros((3, *MC.shape[1:]), F32)

    @pl.when(i == n_gx - 1)
    def _():
        MC[pl.ds(7, 3)] = jnp.zeros((3, *MC.shape[1:]), F32)

    def mid_first(x, _):
        make_faces(x, MC, mid, 8, 16, 2)

    layers(1, 9, mid_first)
    last_face(9, MC, mid, 8, 16)
    wait(MS.at[pl.ds(0, 4), :, mid_rows, :], msr)

    def mid_start(x, _):
        for t in range(2):
            M1[x, t, mid_rows, :] = ME[x, t, mid_rows, :] * (8.0 * MS[x, t, mid_rows, :])

    layers(1, 9, mid_start)

    def mid_second(x, _):
        sweep(x, M1, M2, mid, MS, 8.0, 8, 16, 2)

    layers(2, 8, mid_second)
    mid_res = [left_over(3 + m, M2, mid, MS, 0.125, 8, 16, 2) for m in range(4)]
    low_src = coarsest(lambda m, t: mid_res[m][t], 0.125)

    GS[...] = low_src
    GB[2 * NEAR + g] = low_src
    send(GS, GB.at[2 * NEAR + g], gss, gsr, (i, j, 1 - g))
    for d in (4, 3, 2, 1):
        for sign in (1, -1):
            for core in range(2):
                send(GS, GB.at[2 * (NEAR - sign * d) + g], gs, gr, (near_x(sign * d), j, core))
    for m in range(6):
        for t in range(2):
            SY[m, t] = M2[2 + m, t, pl.ds(12, 8), :]

    @pl.when(has_side)
    def _():
        send(SY, Y2.at[1 - g], ys.at[1], yr.at[1], (i, near_y(side), 1 - g))

    send(SY, Y2.at[g], ys.at[0], yr.at[0], (i, j, 1 - g))
    send(M2.at[pl.ds(4, 2), :, mid_rows, :], M2P.at[pl.ds(0, 2), :, mid_rows, :], xs, xr, (near_x(1), j, g))
    send(M2.at[pl.ds(4, 2), :, mid_rows, :], M2P.at[pl.ds(8, 2), :, mid_rows, :], xs, xr, (near_x(-1), j, g))

    wait(GB.at[0], gsr)

    wait(EB.at[0], ebsr)
    halves = [EB[2 * NEAR + core][4:5] for core in range(2)]
    TS[pl.ds(0, 1), :] = jnp.sum(low_src + GB[2 * NEAR + 1 - g], axis=0, keepdims=True)
    TS[pl.ds(1, 1), :] = jnp.where(lanes_of(1) % 2 == 0, halves[0], halves[1])

    @pl.when(has_side)
    def _():
        pl.semaphore_wait(known.at[1], 1)

    far_y = near_y(side)
    for d in sorted(range(NEAR + 1, n_gx - NEAR), key=lambda d: -min(d, n_gx - d)):
        slot = n_gx - d - NEAR - 1

        @pl.when(has_side)
        def _():
            send(TS, TB.at[slot], ts, tr, (near_x(d), far_y, 1 - g))

        send(TS, FB.at[slot], fs, fr, (near_x(d), j, g))

    wait(EB.at[pl.ds(0, 16)], ebr)
    lane = lanes_of(8)
    row = lax.broadcasted_iota(jnp.int32, (8, 128), 0)
    layer, tile, cell = (lane % 4) // 2, lane % 2, lane // 4
    boxes = 2 * NEAR + 1
    zero = jnp.zeros((8, 128), F32)
    coefs, marks = [], []
    for b in range(boxes):
        first, second = EB[2 * b], EB[2 * b + 1]
        coefs.append(jnp.concatenate([first[:4], second[:4]], axis=0))
        marks.append(jnp.where(tile == 0, jnp.broadcast_to(first[4:5], (8, 128)), jnp.broadcast_to(second[4:5], (8, 128))))
    joined = []
    for b in range(boxes - 1):
        touch = lax.rem(i + b - NEAR + n_gx, n_gx) != n_gx - 1
        joined.append(jnp.where((marks[b] == marks[b + 1]) & touch, 1.0, 0.0))

    def along_x(values):
        down = [pltpu.roll(v, 2, 1) for v in values]
        up = [pltpu.roll(v, 126, 1) for v in values]
        below, above = [], []
        for b in range(boxes):
            before = up[b - 1] * joined[b - 1] if b else zero
            after = down[b + 1] * joined[b] if b < boxes - 1 else zero
            below.append(jnp.where(layer == 0, before, down[b]))
            above.append(jnp.where(layer == 0, up[b], after))
        return below, above

    def along_yz(v):
        return (pltpu.roll(v, 1, 0), pltpu.roll(v, 7, 0), pltpu.roll(v, 4, 1), pltpu.roll(v, 124, 1))

    keeps = (row > 0, row < 7, cell > 0, cell < 31)
    c_below, c_above = along_x(coefs)
    low_faces, low_ease = [], []
    for b in range(boxes):
        c = coefs[b]
        around = [jnp.where(keep, v, 0.0) for keep, v in zip(keeps, along_yz(c))]
        faces = [c + c_below[b], c + c_above[b]] + [c + v for v in around]
        total = faces[0] + faces[1] + faces[2] + faces[3] + faces[4] + faces[5]
        low_faces.append(faces[:2] + [jnp.where(keep, f, 0.0) for keep, f in zip(keeps, faces[2:])])
        low_ease.append(RELAX / total)

    def solve(low, rhs, sweeps):
        for number in range(sweeps):
            below, above = along_x(low)
            fresh = []
            for b in range(boxes):
                around = [below[b], above[b], *along_yz(low[b])]
                total = low_faces[b][0] * around[0]
                for face, value in zip(low_faces[b][1:], around[1:]):
                    total = total + face * value
                if rhs is not None:
                    total = total + 32.0 * rhs[b]
                fresh.append(0.2 * low[b] + low_ease[b] * total)
            low = fresh
        return low[NEAR - 1:NEAR + 2]

    from_mean = solve([jnp.full((8, 128), 4.0, F32)] * boxes, None, BOTTOM)
    wait(GB.at[pl.ds(0, 16)], gr)
    rhs = [jnp.concatenate([GB[2 * b], GB[2 * b + 1]], axis=0) for b in range(boxes)]
    from_source = solve([low_ease[b] * (32.0 * rhs[b]) for b in range(boxes)], rhs, BOTTOM - 1)
    sums = [jnp.sum(v, axis=0, keepdims=True) for v in rhs]
    for b in range(3):
        SQ[b] = from_source[b]
        SQ[3 + b] = from_mean[b]
    for b in range(boxes):
        SQ[6 + b // 8, pl.ds(b % 8, 1), :] = sums[b]
        SQ[8 + b // 8, pl.ds(b % 8, 1), :] = marks[b][:1]

    @pl.when(has_side)
    def _():
        send(SQ, QP, qs, qr, (i, near_y(side), 1 - g))

    for m in range(6):
        for t in range(2):
            M2P[2 + m, t, mid_rows, :] = M2[2 + m, t, mid_rows, :]
    wait(Y2.at[0], yr.at[0])

    @pl.when(has_side)
    def _():
        wait(Y2.at[0], yr.at[1])

    for m in range(6):
        for t in range(2):
            M2P[2 + m, t, pl.ds(9, 1), :] = Y2[0, m, t, pl.ds(5, 1), :]
            M2P[2 + m, t, pl.ds(22, 1), :] = Y2[1, m, t, pl.ds(2, 1), :]
    names = [m[:1] for m in marks]
    src_lane = lax.broadcasted_iota(jnp.int32, (128, 128), 0)
    dst_lane = lax.broadcasted_iota(jnp.int32, (128, 128), 1)
    same_tile = jnp.where(src_lane % 2 == dst_lane % 2, 1.0, 0.0).astype(F32)

    wait(FB, fr)
    for d in range(n_gx - boxes):
        sums.append(FB[d][:1])
        names.append(FB[d][1:])
    @pl.when(has_side)
    def _():
        wait(TB, tr)
        wait(SQ, qr)

    for b in range(boxes):
        sums.append(QP[6 + b // 8, pl.ds(b % 8, 1), :])
        names.append(QP[8 + b // 8, pl.ds(b % 8, 1), :])
    for d in range(n_gx - boxes):
        sums.append(TB[d][:1])
        names.append(TB[d][1:])
    sums = exact_dot(jnp.concatenate(sums, axis=0), same_tile)
    names = jnp.concatenate(names, axis=0)

    def means(first):
        row_sums, row_names = sums[first:first + n_gx], names[first:first + n_gx]
        for place in (NEAR - 1, NEAR, NEAR + 1):
            same = row_names == row_names[place:place + 1]
            total = jnp.sum(jnp.where(same, row_sums, 0.0), axis=0, keepdims=True)
            number = jnp.sum(jnp.where(same, 512.0, 0.0), axis=0, keepdims=True)
            yield total / jnp.maximum(number, 1.0)

    side_at = pl.ds(pl.multiple_of(16 * g, 8), 8)
    for b, mean in enumerate(means(0)):
        Q[b, pl.ds(8, 8), :] = from_source[b] + mean * from_mean[b]
    for b, mean in enumerate(means(n_gx)):
        Q[b, side_at, :] = QP[b] + mean * QP[3 + b]

    wait(M2P.at[pl.ds(0, 4), :, mid_rows, :], xr)

    for b in range(3):
        fix = jnp.where(g == 0, Q[b, pl.ds(6, 8), :], Q[b, pl.ds(10, 8), :])
        for part, wide in enumerate(unbraid(fix)):
            PK[2 * b + part // 2, part % 2, pl.ds(0, 8, stride=2), :] = wide
            PK[2 * b + part // 2, part % 2, pl.ds(1, 8, stride=2), :] = wide

    def corrected(x, _):
        for t in range(2):
            better = M2P[x, t, mid_rows, :] + PK[(x + 1) // 2, t]
            M3[x, t, mid_rows, :] = jnp.where(MC[x, t, mid_rows, :] > 0.0, better, 0.0)

    layers(0, 10, corrected)

    def mid_third(x, _):
        sweep(x, M3, M4, mid, MS, 8.0, 8, 16, 2)

    layers(1, 9, mid_third)
    wait(V2.at[0, :, fine_rows, :], vr.at[0])
    wait(V2.at[0, :, fine_rows, :], vr.at[1])

    def mid_fourth(x, _):
        sweep(x, M4, M1, mid, MS, 8.0, 8, 16, 2)
        for t in range(2):
            PF[x - 2, t, pl.ds(0, 16, stride=2), :] = M1[x, t, mid_rows, :]
            PF[x - 2, t, pl.ds(1, 16, stride=2), :] = M1[x, t, mid_rows, :]
            for half in range(2):
                V3[2 * x - 2 + half, t, fine_rows, :] = V2[2 * x - 2 + half, t, fine_rows, :] + PF[x - 2, t]

    layers(2, 8, mid_fourth)

    def fine_third(x, _):
        sweep(x, V3, V1, fine, S, 2.0, 15, 18, 1)

    layers(3, 13, fine_third)

    def fine_fourth(x, _):
        at = pl.ds(16, 16)
        sums, own = pull(x, V1, fine, 16, 16, 1)
        for t in range(2):
            FO[x - 4, t] = 0.2 * own[t] + E[x, t, at, :] * (2.0 * S[x, t, at, :] + sums[t])

    layers(4, 12, fine_fourth)

    out_rows = pl.ds(pl.multiple_of(16 * g, 8), 16)
    send(FO.at[:, 1 - g], out.at[:, out_rows, :], os_, or_, (i, j, 1 - g))
    keep = pltpu.make_async_copy(FO.at[:, g], out.at[:, out_rows, :], local.at[2])
    keep.start()

    for index, deep in ((0, 3), (1, 2)):
        wait(cells(2 * deep, 24), e1s.at[index, 0])
        wait(cells(8, 24, 1), e1s.at[index, 1])
    for core, there in ((0, up), (1, down)):

        @pl.when(there)
        def _():
            for index, deep in ((0, 3), (1, 2)):
                wait(cells(8, 8, 1), e1s.at[index, 2 + core])
                wait(cells(2 * deep, 8, 1), e1s.at[index, 4 + core])

    wait(V2.at[pl.ds(0, 2), :, fine_rows, :], vs)
    wait(MC.at[pl.ds(0, 6), :, mid_rows, :], mcs)
    wait(MS.at[pl.ds(0, 4), :, mid_rows, :], mss)
    wait(EB.at[pl.ds(0, 16)], ebs)
    wait(EB.at[0], ebss)
    wait(GB.at[pl.ds(0, 16)], gs)
    wait(GB.at[0], gss)
    wait(FB, fs)
    wait(Y2.at[0], ys.at[0])
    wait(M2P.at[pl.ds(0, 4), :, mid_rows, :], xs)

    @pl.when(has_side)
    def _():
        wait(Y2.at[0], ys.at[1])
        wait(SQ, qs)
        wait(TB, ts)

    keep.wait()
    wait(FO.at[:, 0], os_)
    wait(out.at[:, pl.ds(0, 16), :], or_)


def solution(mesh):
    n_gx, n_gy = mesh.shape["gx"], mesh.shape["gy"]

    def kernel(*refs):
        cycle(n_gx, n_gy, *refs)

    def per_device(source, beta_cells, target):
        fine = pltpu.VMEM((16, 2, 48, 128), F32)
        mid = pltpu.VMEM((10, 2, 32, 128), F32)
        far = n_gx - 2 * NEAR - 1
        dma = pltpu.SemaphoreType.DMA
        return pl.pallas_call(
            kernel,
            out_shape=jax.ShapeDtypeStruct(source.shape, F32),
            in_specs=[
                pl.BlockSpec(memory_space=pltpu.HBM),
                pl.BlockSpec(memory_space=pltpu.HBM),
                pl.BlockSpec(memory_space=pltpu.SMEM),
            ],
            out_specs=pl.BlockSpec(memory_space=pl.ANY),
            scratch_shapes=[
                *[fine] * 11,
                *[mid] * 13,
                pltpu.VMEM((4, 2, 32, 128), F32),
                pltpu.VMEM((4, 2, 32, 128), F32),
                pltpu.VMEM((2, 2, 16, 128), F32),
                pltpu.VMEM((6, 2, 8, 128), F32),
                pltpu.VMEM((2, 6, 2, 8, 128), F32),
                pltpu.VMEM((8, 128), F32),
                pltpu.VMEM((4 * NEAR + 2, 8, 128), F32),
                pltpu.VMEM((8, 128), F32),
                pltpu.VMEM((4 * NEAR + 2, 4, 128), F32),
                pltpu.VMEM((4, 128), F32),
                pltpu.VMEM((far, 2, 128), F32),
                pltpu.VMEM((3, 24, 128), F32),
                pltpu.VMEM((10, 8, 128), F32),
                pltpu.VMEM((6, 2, 16, 128), F32),
                pltpu.VMEM((6, 2, 32, 128), F32),
                pltpu.VMEM((8, 2, 16, 128), F32),
                dma((3,)),
                dma((2, 6)),
                dma((2, 4)),
                *[dma] * 10,
                dma((2,)),
                dma((2,)),
                *[dma] * 7,
                dma((2,)),
                *[dma] * 6,
                pltpu.VMEM((2, 128), F32),
                pltpu.VMEM((far, 2, 128), F32),
                pltpu.VMEM((10, 8, 128), F32),
                pltpu.SemaphoreType.REGULAR((2,)),
            ],
            compiler_params=pltpu.CompilerParams(
                collective_id=0, has_side_effects=True, vmem_limit_bytes=32 * 2**20
            ),
            name="cycle",
        )(source, beta_cells, target)

    spec = P("gx", "gy", "gz")
    return jax.shard_map(
        per_device, mesh=mesh, in_specs=(spec, spec, spec), out_specs=spec, check_vma=False
    )
```

```python
import jax
import jax.numpy as jnp
from jax import lax
from jax.experimental import pallas as pl
from jax.experimental.pallas import tpu as pltpu
from jax.sharding import PartitionSpec as P


BOTTOM = 6
RELAX = 0.8
F32 = jnp.float32
MESH = pl.DeviceIdType.MESH
NEAR = 4


def layers(low, high, work):
    for x in range(low, high):
        work(x, 0)


def lanes_of(rows):
    return lax.broadcasted_iota(jnp.int32, (rows, 128), 1)


def beside(left_tile, right_tile, step):
    lane = lanes_of(left_tile.shape[0])
    low0, low1 = pltpu.roll(left_tile, step, 1), pltpu.roll(right_tile, step, 1)
    high0, high1 = pltpu.roll(left_tile, 128 - step, 1), pltpu.roll(right_tile, 128 - step, 1)
    below = (low0, jnp.where(lane < step, low0, low1))
    above = (jnp.where(lane >= 128 - step, high1, high0), high1)
    return below, above


def make_faces(x, coef, faces, row, rows, step):
    fx, fy, fl, fr, weight, ease = faces
    at = pl.ds(row, rows)
    own = [coef[x, t, at, :] for t in range(2)]
    below, above = beside(*own, step)
    lane = lanes_of(rows)
    for t in range(2):
        c = own[t]
        low = jnp.where(lane < step, 0.0, below[0]) if t == 0 else below[1]
        high = jnp.where(lane >= 128 - step, 0.0, above[1]) if t == 1 else above[0]
        x_low = c + coef[x - 1, t, at, :]
        y_low = c + coef[x, t, pl.ds(row - 1, rows), :]
        z_low, z_high = c + low, c + high
        total = (
            x_low
            + (c + coef[x + 1, t, at, :])
            + y_low
            + (c + coef[x, t, pl.ds(row + 1, rows), :])
            + z_low
            + z_high
        )
        fx[x, t, at, :] = x_low
        fy[x, t, at, :] = y_low
        fl[x, t, at, :] = jnp.where(lane < step, 0.0, z_low) if t == 0 else z_low
        fr[x, t, at, :] = jnp.where(lane >= 128 - step, 0.0, z_high) if t == 1 else z_high
        weight[x, t, at, :] = total
        ease[x, t, at, :] = jnp.where(c > 0.0, RELAX / total, 0.0)


def last_face(x, coef, faces, row, rows):
    at = pl.ds(row, rows)
    for t in range(2):
        faces[0][x, t, at, :] = coef[x, t, at, :] + coef[x - 1, t, at, :]


def pull(x, field, faces, row, rows, step):
    fx, fy, fl, fr = faces[:4]
    at = pl.ds(row, rows)
    own = [field[x, t, at, :] for t in range(2)]
    below, above = beside(*own, step)
    sums = []
    for t in range(2):
        sums.append(
            fx[x, t, at, :] * field[x - 1, t, at, :]
            + fx[x + 1, t, at, :] * field[x + 1, t, at, :]
            + fy[x, t, at, :] * field[x, t, pl.ds(row - 1, rows), :]
            + fy[x, t, pl.ds(row + 1, rows), :] * field[x, t, pl.ds(row + 1, rows), :]
            + fl[x, t, at, :] * below[t]
            + fr[x, t, at, :] * above[t]
        )
    return sums, own


def sweep(x, field, out, faces, source, gain, row, rows, step):
    at = pl.ds(row, rows)
    sums, own = pull(x, field, faces, row, rows, step)
    for t in range(2):
        out[x, t, at, :] = 0.2 * own[t] + faces[5][x, t, at, :] * (gain * source[x, t, at, :] + sums[t])


def left_over(x, field, faces, source, half, row, rows, step):
    at = pl.ds(row, rows)
    sums, own = pull(x, field, faces, row, rows, step)
    return [source[x, t, at, :] - half * (faces[4][x, t, at, :] * own[t] - sums[t]) for t in range(2)]


def pair_sum(value, step):
    lane = lanes_of(value.shape[0])
    other = jnp.where((lane // step) % 2 == 0, pltpu.roll(value, 128 - step, 1), pltpu.roll(value, step, 1))
    return value + other


def exact_dot(a, b):
    return jnp.dot(a, b, precision=lax.Precision.HIGHEST, preferred_element_type=F32)


def braid(parts):
    kind = lanes_of(parts[0].shape[0]) % 4
    return jnp.where(kind < 2, jnp.where(kind == 0, parts[0], parts[1]), jnp.where(kind == 2, parts[2], parts[3]))


def unbraid(value):
    lane = lanes_of(value.shape[0])
    even, upper = lane % 2 == 0, lane % 4 >= 2
    pairs = (jnp.where(even, value, pltpu.roll(value, 1, 1)), jnp.where(even, pltpu.roll(value, 127, 1), value))
    return [
        jnp.where(upper, pltpu.roll(pair, 2, 1), pair) if half == 0 else jnp.where(upper, pair, pltpu.roll(pair, 126, 1))
        for half in range(2)
        for pair in pairs
    ]


def cycle(n_gx, n_gy, src, beta, tgt, out, *scratch):
    (C, S, FX, FY, FL, FR, W, E, V1, V2, V3,
     MC, MS, MFX, MFY, MFL, MFR, MW, ME, M1, M2, M2P, M3, M4,
     RS, RC, R2, SY, Y2, SX, EB, ES, GB, GS, FB, Q, SQ, PK, PF, FO,
     local, e1s, e1r, mcs, mcr, mss, msr, ebs, ebr, gs, gr, fs, fr, ys, yr, xs, xr, qs, qr, os_, or_, vs, vr, ebss, ebsr, gss, gsr, ts, tr, TS, TB, QP, known) = scratch
    i, j, g = lax.axis_index("gx"), lax.axis_index("gy"), lax.axis_index("gz")
    fine = (FX, FY, FL, FR, W, E)
    mid = (MFX, MFY, MFL, MFR, MW, ME)

    def near_x(d):
        return lax.rem(i + d + n_gx, n_gx)

    def near_y(d):
        return lax.rem(j + d + n_gy, n_gy)

    def send(source, target, send_sem, recv_sem, where):
        pltpu.make_async_remote_copy(
            src_ref=source, dst_ref=target, send_sem=send_sem, recv_sem=recv_sem,
            device_id=where, device_id_type=MESH,
        ).start()

    def tell():
        for sign in (1, -1):
            pl.semaphore_signal(known.at[0], inc=1, device_id=(near_x(sign * 4), j, g), device_id_type=MESH)

    def wait(ref, sem):
        pltpu.make_async_copy(ref, ref, sem).wait()

    own_rows = pl.ds(pl.multiple_of(8 * g, 8), 24)
    own_at = pl.ds(pl.multiple_of(16 - 8 * g, 8), 24)
    pltpu.make_async_copy(beta.at[:, own_rows, :], C.at[pl.ds(4, 8), g, own_at, :], local.at[0]).start()
    pltpu.make_async_copy(src.at[:, own_rows, :], S.at[pl.ds(4, 8), g, own_at, :], local.at[1]).start()

    barrier = pltpu.get_barrier_semaphore()
    side = 2 * g - 1
    up, down = j < n_gy - 1, j > 0
    has_side = jnp.where(g == 0, j, n_gy - 1 - j) > 0

    def greet(where):
        pl.semaphore_signal(barrier, inc=1, device_id=where, device_id_type=MESH)

    @pl.when(has_side)
    def _():
        for dx in (-1, 0, 1):
            for core in range(2):
                greet((near_x(dx), near_y(side), core))

    for dx in (4, 3, 2, 1):
        for sign in (1, -1):
            for core in range(2 if dx == 1 else 1):
                greet((near_x(sign * dx), j, core if dx == 1 else g))
    greet((i, j, 1 - g))
    pl.semaphore_wait(barrier, 11 + 3 * (up.astype(jnp.int32) + down.astype(jnp.int32)))
    tell()

    fields = ((beta, C, 3), (src, S, 2))
    for core, there, theirs, ours in ((0, up, 8, 24), (1, down, 32, 0)):

        @pl.when(there)
        def _():
            far_y = near_y(1 - 2 * core)
            for index, (field, target, deep) in enumerate(fields):
                for dx in (1, -1):
                    part = pl.ds(8 - deep, deep) if dx == 1 else pl.ds(0, deep)
                    place = pl.ds(4 - deep, deep) if dx == 1 else pl.ds(12, deep)
                    send(field.at[part, pl.ds(ours, 8), :], target.at[place, g, pl.ds(theirs, 8), :],
                         e1s.at[index, 4 + core], e1r.at[index, 3], (near_x(dx), far_y, core))
            for index, (field, target, _) in enumerate(fields):
                send(field.at[:, pl.ds(ours, 8), :], target.at[pl.ds(4, 8), g, pl.ds(theirs, 8), :],
                     e1s.at[index, 2 + core], e1r.at[index, 2], (i, far_y, core))

    for index, (field, target, deep) in enumerate(fields):
        for dx in (1, -1):
            part = pl.ds(8 - deep, deep) if dx == 1 else pl.ds(0, deep)
            place = pl.ds(4 - deep, deep) if dx == 1 else pl.ds(12, deep)
            for core in range(2):
                send(field.at[part, pl.ds(8 * core, 24), :], target.at[place, g, pl.ds(16 - 8 * core, 24), :],
                     e1s.at[index, 0], e1r.at[index, 0], (near_x(dx), j, core))
    for index, (field, target, _) in enumerate(fields):
        send(field.at[:, pl.ds(pl.multiple_of(8 - 8 * g, 8), 24), :],
             target.at[pl.ds(4, 8), g, pl.ds(pl.multiple_of(8 + 8 * g, 8), 24), :],
             e1s.at[index, 1], e1r.at[index, 1], (i, j, 1 - g))
    def outside(edge, row):
        @pl.when(edge)
        def _():
            for field in (C, S):
                field[:, :, pl.ds(row, 8), :] = jnp.zeros((16, 2, 8, 128), F32)

    outside((j == 0) & (g == 0), 8)
    outside((j == n_gy - 1) & (g == 1), 32)

    def cells(layers, rows, tiles=2):
        return C.at[pl.ds(0, layers), pl.ds(0, tiles), pl.ds(0, rows), :]

    wait(beta.at[:, pl.ds(0, 24), :], local.at[0])
    wait(cells(8, 24, 1), e1r.at[0, 1])

    @pl.when(has_side)
    def _():
        wait(cells(8, 8), e1r.at[0, 2])

    def mid_coefficient(m, _):
        for t in range(2):
            RC[m, t] = C[4 + 2 * m, t, pl.ds(8, 32), :] + C[5 + 2 * m, t, pl.ds(8, 32), :]
            two = RC[m, t, pl.ds(0, 16, stride=2), :] + RC[m, t, pl.ds(1, 16, stride=2), :]
            MC[m + 3, t, pl.ds(8, 16), :] = 0.125 * pair_sum(two, 1)

    layers(0, 4, mid_coefficient)
    mid_rows = pl.ds(8, 16)
    send(MC.at[pl.ds(4, 3), :, mid_rows, :], MC.at[pl.ds(0, 3), :, mid_rows, :], mcs, mcr, (near_x(1), j, g))
    send(MC.at[pl.ds(3, 3), :, mid_rows, :], MC.at[pl.ds(7, 3), :, mid_rows, :], mcs, mcr, (near_x(-1), j, g))

    wait(src.at[:, pl.ds(0, 24), :], local.at[1])
    wait(cells(8, 24, 1), e1r.at[1, 1])

    @pl.when(has_side)
    def _():
        wait(cells(8, 8), e1r.at[1, 2])


    def fine_first(x, _):
        make_faces(x, C, fine, 8, 32, 1)
        for t in range(2):
            V1[x, t, pl.ds(8, 32), :] = E[x, t, pl.ds(8, 32), :] * (2.0 * S[x, t, pl.ds(8, 32), :])

    def fine_second(x, _):
        sweep(x, V1, V2, fine, S, 2.0, 8, 32, 1)

    layers(5, 11, fine_first)
    layers(6, 10, fine_second)

    pl.semaphore_wait(known.at[0], 2)

    @pl.when(has_side)
    def _():
        pl.semaphore_signal(known.at[1], inc=1, device_id=(i, near_y(side), 1 - g), device_id_type=MESH)

    wait(cells(6, 24), e1r.at[0, 0])

    @pl.when(has_side)
    def _():
        wait(cells(6, 8), e1r.at[0, 3])


    @pl.when(i == 0)
    def _():
        C[pl.ds(1, 3)] = jnp.zeros((3, *C.shape[1:]), F32)

    @pl.when(i == n_gx - 1)
    def _():
        C[pl.ds(12, 3)] = jnp.zeros((3, *C.shape[1:]), F32)

    wait(cells(4, 24), e1r.at[1, 0])

    @pl.when(has_side)
    def _():
        wait(cells(4, 8), e1r.at[1, 3])

    layers(2, 5, fine_first)
    layers(11, 14, fine_first)
    last_face(14, C, fine, 8, 32)
    layers(3, 6, fine_second)
    layers(10, 13, fine_second)
    fine_rows = pl.ds(8, 32)

    def fine_residual(m, _):
        lower = left_over(4 + 2 * m, V2, fine, S, 0.5, 8, 32, 1)
        upper = left_over(5 + 2 * m, V2, fine, S, 0.5, 8, 32, 1)
        for t in range(2):
            RS[m, t] = lower[t] + upper[t]
            two = RS[m, t, pl.ds(0, 16, stride=2), :] + RS[m, t, pl.ds(1, 16, stride=2), :]
            MS[m + 3, t, mid_rows, :] = 0.125 * pair_sum(two, 1)

    layers(0, 4, fine_residual)
    send(MS.at[pl.ds(5, 2), :, mid_rows, :], MS.at[pl.ds(1, 2), :, mid_rows, :], mss, msr, (near_x(1), j, g))
    send(MS.at[pl.ds(3, 2), :, mid_rows, :], MS.at[pl.ds(7, 2), :, mid_rows, :], mss, msr, (near_x(-1), j, g))

    def coarsest(field, scale):
        parts = []
        for layer in range(2):
            for t in range(2):
                R2[layer, t] = field(2 * layer, t) + field(2 * layer + 1, t)
                two = R2[layer, t, pl.ds(4, 4, stride=2), :] + R2[layer, t, pl.ds(5, 4, stride=2), :]
                parts.append(scale * pair_sum(two, 2))
        return braid(parts)

    own_target = jnp.full((4, 128), tgt[0, 0, 0].astype(F32), F32)
    ES[pl.ds(0, 4), :] = coarsest(lambda m, t: MC[3 + m, t, mid_rows, :], 0.125)
    ES[pl.ds(4, 4), :] = own_target
    EB[2 * NEAR + g] = ES[...]
    for d in (4, 3, 2, 1):
        for sign in (1, -1):
            for core in range(2):
                send(ES, EB.at[2 * (NEAR - sign * d) + g], ebs, ebr, (near_x(sign * d), j, core))
    send(ES, EB.at[2 * NEAR + g], ebss, ebsr, (i, j, 1 - g))

    wait(MC.at[pl.ds(0, 6), :, mid_rows, :], mcr)

    @pl.when(i == 0)
    def _():
        MC[pl.ds(0, 3)] = jnp.zeros((3, *MC.shape[1:]), F32)

    @pl.when(i == n_gx - 1)
    def _():
        MC[pl.ds(7, 3)] = jnp.zeros((3, *MC.shape[1:]), F32)

    def mid_first(x, _):
        make_faces(x, MC, mid, 8, 16, 2)

    layers(1, 9, mid_first)
    last_face(9, MC, mid, 8, 16)
    wait(MS.at[pl.ds(0, 4), :, mid_rows, :], msr)

    def mid_start(x, _):
        for t in range(2):
            M1[x, t, mid_rows, :] = ME[x, t, mid_rows, :] * (8.0 * MS[x, t, mid_rows, :])

    layers(1, 9, mid_start)

    def mid_second(x, _):
        sweep(x, M1, M2, mid, MS, 8.0, 8, 16, 2)

    layers(2, 8, mid_second)
    mid_res = [left_over(3 + m, M2, mid, MS, 0.125, 8, 16, 2) for m in range(4)]
    low_src = coarsest(lambda m, t: mid_res[m][t], 0.125)

    GS[...] = low_src
    GB[2 * NEAR + g] = low_src
    send(GS, GB.at[2 * NEAR + g], gss, gsr, (i, j, 1 - g))
    for d in (4, 3, 2, 1):
        for sign in (1, -1):
            for core in range(2):
                send(GS, GB.at[2 * (NEAR - sign * d) + g], gs, gr, (near_x(sign * d), j, core))
    wait(GB.at[0], gsr)

    wait(EB.at[0], ebsr)
    halves = [EB[2 * NEAR + core][4:5] for core in range(2)]
    TS[pl.ds(0, 1), :] = jnp.sum(low_src + GB[2 * NEAR + 1 - g], axis=0, keepdims=True)
    TS[pl.ds(1, 1), :] = jnp.where(lanes_of(1) % 2 == 0, halves[0], halves[1])

    @pl.when(has_side)
    def _():
        pl.semaphore_wait(known.at[1], 1)

    far_y = near_y(side)
    for d in sorted(range(NEAR + 1, n_gx - NEAR), key=lambda d: -min(d, n_gx - d)):
        slot = n_gx - d - NEAR - 1

        @pl.when(has_side)
        def _():
            send(TS, TB.at[slot], ts, tr, (near_x(d), far_y, 1 - g))

        send(TS, FB.at[slot], fs, fr, (near_x(d), j, g))

    for m in range(6):
        for t in range(2):
            SY[m, t] = M2[2 + m, t, pl.ds(12, 8), :]

    @pl.when(has_side)
    def _():
        send(SY, Y2.at[1 - g], ys.at[1], yr.at[1], (i, near_y(side), 1 - g))

    send(SY, Y2.at[g], ys.at[0], yr.at[0], (i, j, 1 - g))
    send(M2.at[pl.ds(4, 2), :, mid_rows, :], M2P.at[pl.ds(0, 2), :, mid_rows, :], xs, xr, (near_x(1), j, g))
    send(M2.at[pl.ds(4, 2), :, mid_rows, :], M2P.at[pl.ds(8, 2), :, mid_rows, :], xs, xr, (near_x(-1), j, g))

    send(V2.at[10, :, fine_rows, :], V2.at[2, :, fine_rows, :], vs, vr.at[0], (near_x(1), j, g))
    send(V2.at[5, :, fine_rows, :], V2.at[13, :, fine_rows, :], vs, vr.at[1], (near_x(-1), j, g))

    wait(EB.at[pl.ds(0, 16)], ebr)
    lane = lanes_of(8)
    row = lax.broadcasted_iota(jnp.int32, (8, 128), 0)
    layer, tile, cell = (lane % 4) // 2, lane % 2, lane // 4
    boxes = 2 * NEAR + 1
    zero = jnp.zeros((8, 128), F32)
    coefs, marks = [], []
    for b in range(boxes):
        first, second = EB[2 * b], EB[2 * b + 1]
        coefs.append(jnp.concatenate([first[:4], second[:4]], axis=0))
        marks.append(jnp.where(tile == 0, jnp.broadcast_to(first[4:5], (8, 128)), jnp.broadcast_to(second[4:5], (8, 128))))
    joined = []
    for b in range(boxes - 1):
        touch = lax.rem(i + b - NEAR + n_gx, n_gx) != n_gx - 1
        joined.append(jnp.where((marks[b] == marks[b + 1]) & touch, 1.0, 0.0))

    def along_x(values):
        down = [pltpu.roll(v, 2, 1) for v in values]
        up = [pltpu.roll(v, 126, 1) for v in values]
        below, above = [], []
        for b in range(boxes):
            before = up[b - 1] * joined[b - 1] if b else zero
            after = down[b + 1] * joined[b] if b < boxes - 1 else zero
            below.append(jnp.where(layer == 0, before, down[b]))
            above.append(jnp.where(layer == 0, up[b], after))
        return below, above

    def along_yz(v):
        return (pltpu.roll(v, 1, 0), pltpu.roll(v, 7, 0), pltpu.roll(v, 4, 1), pltpu.roll(v, 124, 1))

    keeps = (row > 0, row < 7, cell > 0, cell < 31)
    c_below, c_above = along_x(coefs)
    low_faces, low_ease = [], []
    for b in range(boxes):
        c = coefs[b]
        around = [jnp.where(keep, v, 0.0) for keep, v in zip(keeps, along_yz(c))]
        faces = [c + c_below[b], c + c_above[b]] + [c + v for v in around]
        total = faces[0] + faces[1] + faces[2] + faces[3] + faces[4] + faces[5]
        low_faces.append(faces[:2] + [jnp.where(keep, f, 0.0) for keep, f in zip(keeps, faces[2:])])
        low_ease.append(RELAX / total)

    def solve(low, rhs, sweeps):
        for number in range(sweeps):
            below, above = along_x(low)
            fresh = []
            for b in range(boxes):
                around = [below[b], above[b], *along_yz(low[b])]
                total = low_faces[b][0] * around[0]
                for face, value in zip(low_faces[b][1:], around[1:]):
                    total = total + face * value
                if rhs is not None:
                    total = total + 32.0 * rhs[b]
                fresh.append(0.2 * low[b] + low_ease[b] * total)
            low = fresh
        return low[NEAR - 1:NEAR + 2]

    from_mean = solve([jnp.full((8, 128), 4.0, F32)] * boxes, None, BOTTOM)
    wait(GB.at[pl.ds(0, 16)], gr)
    rhs = [jnp.concatenate([GB[2 * b], GB[2 * b + 1]], axis=0) for b in range(boxes)]
    from_source = solve([low_ease[b] * (32.0 * rhs[b]) for b in range(boxes)], rhs, BOTTOM - 1)
    sums = [jnp.sum(v, axis=0, keepdims=True) for v in rhs]
    for b in range(3):
        SQ[b] = from_source[b]
        SQ[3 + b] = from_mean[b]
    for b in range(boxes):
        SQ[6 + b // 8, pl.ds(b % 8, 1), :] = sums[b]
        SQ[8 + b // 8, pl.ds(b % 8, 1), :] = marks[b][:1]

    @pl.when(has_side)
    def _():
        send(SQ, QP, qs, qr, (i, near_y(side), 1 - g))

    for m in range(6):
        for t in range(2):
            M2P[2 + m, t, mid_rows, :] = M2[2 + m, t, mid_rows, :]
    wait(Y2.at[0], yr.at[0])

    @pl.when(has_side)
    def _():
        wait(Y2.at[0], yr.at[1])

    for m in range(6):
        for t in range(2):
            M2P[2 + m, t, pl.ds(9, 1), :] = Y2[0, m, t, pl.ds(5, 1), :]
            M2P[2 + m, t, pl.ds(22, 1), :] = Y2[1, m, t, pl.ds(2, 1), :]
    names = [m[:1] for m in marks]
    src_lane = lax.broadcasted_iota(jnp.int32, (128, 128), 0)
    dst_lane = lax.broadcasted_iota(jnp.int32, (128, 128), 1)
    same_tile = jnp.where(src_lane % 2 == dst_lane % 2, 1.0, 0.0).astype(F32)

    wait(FB, fr)
    for d in range(n_gx - boxes):
        sums.append(FB[d][:1])
        names.append(FB[d][1:])
    @pl.when(has_side)
    def _():
        wait(TB, tr)
        wait(SQ, qr)

    for b in range(boxes):
        sums.append(QP[6 + b // 8, pl.ds(b % 8, 1), :])
        names.append(QP[8 + b // 8, pl.ds(b % 8, 1), :])
    for d in range(n_gx - boxes):
        sums.append(TB[d][:1])
        names.append(TB[d][1:])
    sums = exact_dot(jnp.concatenate(sums, axis=0), same_tile)
    names = jnp.concatenate(names, axis=0)

    def means(first):
        row_sums, row_names = sums[first:first + n_gx], names[first:first + n_gx]
        for place in (NEAR - 1, NEAR, NEAR + 1):
            same = row_names == row_names[place:place + 1]
            total = jnp.sum(jnp.where(same, row_sums, 0.0), axis=0, keepdims=True)
            number = jnp.sum(jnp.where(same, 512.0, 0.0), axis=0, keepdims=True)
            yield total / jnp.maximum(number, 1.0)

    side_at = pl.ds(pl.multiple_of(16 * g, 8), 8)
    for b, mean in enumerate(means(0)):
        Q[b, pl.ds(8, 8), :] = from_source[b] + mean * from_mean[b]
    for b, mean in enumerate(means(n_gx)):
        Q[b, side_at, :] = QP[b] + mean * QP[3 + b]

    wait(M2P.at[pl.ds(0, 4), :, mid_rows, :], xr)

    for b in range(3):
        fix = jnp.where(g == 0, Q[b, pl.ds(6, 8), :], Q[b, pl.ds(10, 8), :])
        for part, wide in enumerate(unbraid(fix)):
            PK[2 * b + part // 2, part % 2, pl.ds(0, 8, stride=2), :] = wide
            PK[2 * b + part // 2, part % 2, pl.ds(1, 8, stride=2), :] = wide

    def corrected(x, _):
        for t in range(2):
            better = M2P[x, t, mid_rows, :] + PK[(x + 1) // 2, t]
            M3[x, t, mid_rows, :] = jnp.where(MC[x, t, mid_rows, :] > 0.0, better, 0.0)

    layers(0, 10, corrected)

    def mid_third(x, _):
        sweep(x, M3, M4, mid, MS, 8.0, 8, 16, 2)

    layers(1, 9, mid_third)
    wait(V2.at[0, :, fine_rows, :], vr.at[0])
    wait(V2.at[0, :, fine_rows, :], vr.at[1])

    def mid_fourth(x, _):
        sweep(x, M4, M1, mid, MS, 8.0, 8, 16, 2)
        for t in range(2):
            PF[x - 2, t, pl.ds(0, 16, stride=2), :] = M1[x, t, mid_rows, :]
            PF[x - 2, t, pl.ds(1, 16, stride=2), :] = M1[x, t, mid_rows, :]
            for half in range(2):
                V3[2 * x - 2 + half, t, fine_rows, :] = V2[2 * x - 2 + half, t, fine_rows, :] + PF[x - 2, t]

    layers(2, 8, mid_fourth)

    def fine_third(x, _):
        sweep(x, V3, V1, fine, S, 2.0, 15, 18, 1)

    layers(3, 13, fine_third)

    def fine_fourth(x, _):
        at = pl.ds(16, 16)
        sums, own = pull(x, V1, fine, 16, 16, 1)
        for t in range(2):
            FO[x - 4, t] = 0.2 * own[t] + E[x, t, at, :] * (2.0 * S[x, t, at, :] + sums[t])

    layers(4, 12, fine_fourth)

    out_rows = pl.ds(pl.multiple_of(16 * g, 8), 16)
    send(FO.at[:, 1 - g], out.at[:, out_rows, :], os_, or_, (i, j, 1 - g))
    keep = pltpu.make_async_copy(FO.at[:, g], out.at[:, out_rows, :], local.at[2])
    keep.start()

    for index, deep in ((0, 3), (1, 2)):
        wait(cells(2 * deep, 24), e1s.at[index, 0])
        wait(cells(8, 24, 1), e1s.at[index, 1])
    for core, there in ((0, up), (1, down)):

        @pl.when(there)
        def _():
            for index, deep in ((0, 3), (1, 2)):
                wait(cells(8, 8, 1), e1s.at[index, 2 + core])
                wait(cells(2 * deep, 8, 1), e1s.at[index, 4 + core])

    wait(V2.at[pl.ds(0, 2), :, fine_rows, :], vs)
    wait(MC.at[pl.ds(0, 6), :, mid_rows, :], mcs)
    wait(MS.at[pl.ds(0, 4), :, mid_rows, :], mss)
    wait(EB.at[pl.ds(0, 16)], ebs)
    wait(EB.at[0], ebss)
    wait(GB.at[pl.ds(0, 16)], gs)
    wait(GB.at[0], gss)
    wait(FB, fs)
    wait(Y2.at[0], ys.at[0])
    wait(M2P.at[pl.ds(0, 4), :, mid_rows, :], xs)

    @pl.when(has_side)
    def _():
        wait(Y2.at[0], ys.at[1])
        wait(SQ, qs)
        wait(TB, ts)

    keep.wait()
    wait(FO.at[:, 0], os_)
    wait(out.at[:, pl.ds(0, 16), :], or_)


def solution(mesh):
    n_gx, n_gy = mesh.shape["gx"], mesh.shape["gy"]

    def kernel(*refs):
        cycle(n_gx, n_gy, *refs)

    def per_device(source, beta_cells, target):
        fine = pltpu.VMEM((16, 2, 48, 128), F32)
        mid = pltpu.VMEM((10, 2, 32, 128), F32)
        far = n_gx - 2 * NEAR - 1
        dma = pltpu.SemaphoreType.DMA
        return pl.pallas_call(
            kernel,
            out_shape=jax.ShapeDtypeStruct(source.shape, F32),
            in_specs=[
                pl.BlockSpec(memory_space=pltpu.HBM),
                pl.BlockSpec(memory_space=pltpu.HBM),
                pl.BlockSpec(memory_space=pltpu.SMEM),
            ],
            out_specs=pl.BlockSpec(memory_space=pl.ANY),
            scratch_shapes=[
                *[fine] * 11,
                *[mid] * 13,
                pltpu.VMEM((4, 2, 32, 128), F32),
                pltpu.VMEM((4, 2, 32, 128), F32),
                pltpu.VMEM((2, 2, 16, 128), F32),
                pltpu.VMEM((6, 2, 8, 128), F32),
                pltpu.VMEM((2, 6, 2, 8, 128), F32),
                pltpu.VMEM((8, 128), F32),
                pltpu.VMEM((4 * NEAR + 2, 8, 128), F32),
                pltpu.VMEM((8, 128), F32),
                pltpu.VMEM((4 * NEAR + 2, 4, 128), F32),
                pltpu.VMEM((4, 128), F32),
                pltpu.VMEM((far, 2, 128), F32),
                pltpu.VMEM((3, 24, 128), F32),
                pltpu.VMEM((10, 8, 128), F32),
                pltpu.VMEM((6, 2, 16, 128), F32),
                pltpu.VMEM((6, 2, 32, 128), F32),
                pltpu.VMEM((8, 2, 16, 128), F32),
                dma((3,)),
                dma((2, 6)),
                dma((2, 4)),
                *[dma] * 10,
                dma((2,)),
                dma((2,)),
                *[dma] * 7,
                dma((2,)),
                *[dma] * 6,
                pltpu.VMEM((2, 128), F32),
                pltpu.VMEM((far, 2, 128), F32),
                pltpu.VMEM((10, 8, 128), F32),
                pltpu.SemaphoreType.REGULAR((2,)),
            ],
            compiler_params=pltpu.CompilerParams(
                collective_id=0, has_side_effects=True, vmem_limit_bytes=32 * 2**20
            ),
            name="cycle",
        )(source, beta_cells, target)

    spec = P("gx", "gy", "gz")
    return jax.shard_map(
        per_device, mesh=mesh, in_specs=(spec, spec, spec), out_specs=spec, check_vma=False
    )
```

```python
import jax
import jax.numpy as jnp
from jax import lax
from jax.experimental import pallas as pl
from jax.experimental.pallas import tpu as pltpu
from jax.sharding import PartitionSpec as P


BOTTOM = 6
RELAX = 0.8
F32 = jnp.float32
MESH = pl.DeviceIdType.MESH
NEAR = 4


def layers(low, high, work):
    for x in range(low, high):
        work(x, 0)


def lanes_of(rows):
    return lax.broadcasted_iota(jnp.int32, (rows, 128), 1)


def beside(left_tile, right_tile, step):
    lane = lanes_of(left_tile.shape[0])
    low0, low1 = pltpu.roll(left_tile, step, 1), pltpu.roll(right_tile, step, 1)
    high0, high1 = pltpu.roll(left_tile, 128 - step, 1), pltpu.roll(right_tile, 128 - step, 1)
    below = (low0, jnp.where(lane < step, low0, low1))
    above = (jnp.where(lane >= 128 - step, high1, high0), high1)
    return below, above


def make_faces(x, coef, faces, row, rows, step):
    fx, fy, fl, fr, weight, ease = faces
    at = pl.ds(row, rows)
    own = [coef[x, t, at, :] for t in range(2)]
    below, above = beside(*own, step)
    lane = lanes_of(rows)
    for t in range(2):
        c = own[t]
        low = jnp.where(lane < step, 0.0, below[0]) if t == 0 else below[1]
        high = jnp.where(lane >= 128 - step, 0.0, above[1]) if t == 1 else above[0]
        x_low = c + coef[x - 1, t, at, :]
        y_low = c + coef[x, t, pl.ds(row - 1, rows), :]
        z_low, z_high = c + low, c + high
        total = (
            x_low
            + (c + coef[x + 1, t, at, :])
            + y_low
            + (c + coef[x, t, pl.ds(row + 1, rows), :])
            + z_low
            + z_high
        )
        fx[x, t, at, :] = x_low
        fy[x, t, at, :] = y_low
        fl[x, t, at, :] = jnp.where(lane < step, 0.0, z_low) if t == 0 else z_low
        fr[x, t, at, :] = jnp.where(lane >= 128 - step, 0.0, z_high) if t == 1 else z_high
        weight[x, t, at, :] = total
        ease[x, t, at, :] = jnp.where(c > 0.0, RELAX / total, 0.0)


def last_face(x, coef, faces, row, rows):
    at = pl.ds(row, rows)
    for t in range(2):
        faces[0][x, t, at, :] = coef[x, t, at, :] + coef[x - 1, t, at, :]


def pull(x, field, faces, row, rows, step):
    fx, fy, fl, fr = faces[:4]
    at = pl.ds(row, rows)
    own = [field[x, t, at, :] for t in range(2)]
    below, above = beside(*own, step)
    sums = []
    for t in range(2):
        sums.append(
            fx[x, t, at, :] * field[x - 1, t, at, :]
            + fx[x + 1, t, at, :] * field[x + 1, t, at, :]
            + fy[x, t, at, :] * field[x, t, pl.ds(row - 1, rows), :]
            + fy[x, t, pl.ds(row + 1, rows), :] * field[x, t, pl.ds(row + 1, rows), :]
            + fl[x, t, at, :] * below[t]
            + fr[x, t, at, :] * above[t]
        )
    return sums, own


def sweep(x, field, out, faces, source, gain, row, rows, step):
    at = pl.ds(row, rows)
    sums, own = pull(x, field, faces, row, rows, step)
    for t in range(2):
        out[x, t, at, :] = 0.2 * own[t] + faces[5][x, t, at, :] * (gain * source[x, t, at, :] + sums[t])


def left_over(x, field, faces, source, half, row, rows, step):
    at = pl.ds(row, rows)
    sums, own = pull(x, field, faces, row, rows, step)
    return [source[x, t, at, :] - half * (faces[4][x, t, at, :] * own[t] - sums[t]) for t in range(2)]


def pair_sum(value, step):
    lane = lanes_of(value.shape[0])
    other = jnp.where((lane // step) % 2 == 0, pltpu.roll(value, 128 - step, 1), pltpu.roll(value, step, 1))
    return value + other


def exact_dot(a, b):
    return jnp.dot(a, b, precision=lax.Precision.HIGHEST, preferred_element_type=F32)


def braid(parts):
    kind = lanes_of(parts[0].shape[0]) % 4
    return jnp.where(kind < 2, jnp.where(kind == 0, parts[0], parts[1]), jnp.where(kind == 2, parts[2], parts[3]))


def unbraid(value):
    lane = lanes_of(value.shape[0])
    even, upper = lane % 2 == 0, lane % 4 >= 2
    pairs = (jnp.where(even, value, pltpu.roll(value, 1, 1)), jnp.where(even, pltpu.roll(value, 127, 1), value))
    return [
        jnp.where(upper, pltpu.roll(pair, 2, 1), pair) if half == 0 else jnp.where(upper, pair, pltpu.roll(pair, 126, 1))
        for half in range(2)
        for pair in pairs
    ]


def cycle(n_gx, n_gy, src, beta, tgt, out, *scratch):
    (C, S, FX, FY, FL, FR, W, E, V1, V2, V3,
     MC, MS, MFX, MFY, MFL, MFR, MW, ME, M1, M2, M2P, M3, M4,
     RS, RC, R2, SY, Y2, SX, EB, ES, GB, GS, FB, Q, SQ, PK, PF, FO,
     local, e1s, e1r, mcs, mcr, mss, msr, ebs, ebr, gs, gr, fs, fr, ys, yr, xs, xr, qs, qr, os_, or_, vs, vr, ebss, ebsr, gss, gsr, ts, tr, TS, TB, QP, known) = scratch
    i, j, g = lax.axis_index("gx"), lax.axis_index("gy"), lax.axis_index("gz")
    fine = (FX, FY, FL, FR, W, E)
    mid = (MFX, MFY, MFL, MFR, MW, ME)

    def near_x(d):
        return lax.rem(i + d + n_gx, n_gx)

    def near_y(d):
        return lax.rem(j + d + n_gy, n_gy)

    def send(source, target, send_sem, recv_sem, where):
        pltpu.make_async_remote_copy(
            src_ref=source, dst_ref=target, send_sem=send_sem, recv_sem=recv_sem,
            device_id=where, device_id_type=MESH,
        ).start()

    def tell():
        for sign in (1, -1):
            pl.semaphore_signal(known.at[0], inc=1, device_id=(near_x(sign * 4), j, g), device_id_type=MESH)

    def wait(ref, sem):
        pltpu.make_async_copy(ref, ref, sem).wait()

    own_rows = pl.ds(pl.multiple_of(8 * g, 8), 24)
    own_at = pl.ds(pl.multiple_of(16 - 8 * g, 8), 24)
    pltpu.make_async_copy(beta.at[:, own_rows, :], C.at[pl.ds(4, 8), g, own_at, :], local.at[0]).start()
    pltpu.make_async_copy(src.at[:, own_rows, :], S.at[pl.ds(4, 8), g, own_at, :], local.at[1]).start()

    barrier = pltpu.get_barrier_semaphore()
    side = 2 * g - 1
    up, down = j < n_gy - 1, j > 0
    has_side = jnp.where(g == 0, j, n_gy - 1 - j) > 0

    def greet(where):
        pl.semaphore_signal(barrier, inc=1, device_id=where, device_id_type=MESH)

    @pl.when(has_side)
    def _():
        for dx in (-1, 0, 1):
            for core in range(2):
                greet((near_x(dx), near_y(side), core))

    for dx in (4, 3, 2, 1):
        for sign in (1, -1):
            for core in range(2 if dx == 1 else 1):
                greet((near_x(sign * dx), j, core if dx == 1 else g))
    greet((i, j, 1 - g))
    pl.semaphore_wait(barrier, 11 + 3 * (up.astype(jnp.int32) + down.astype(jnp.int32)))
    tell()

    fields = ((beta, C, 3), (src, S, 2))
    for core, there, theirs, ours in ((0, up, 8, 24), (1, down, 32, 0)):

        @pl.when(there)
        def _():
            far_y = near_y(1 - 2 * core)
            for index, (field, target, deep) in enumerate(fields):
                for dx in (1, -1):
                    part = pl.ds(8 - deep, deep) if dx == 1 else pl.ds(0, deep)
                    place = pl.ds(4 - deep, deep) if dx == 1 else pl.ds(12, deep)
                    send(field.at[part, pl.ds(ours, 8), :], target.at[place, g, pl.ds(theirs, 8), :],
                         e1s.at[index, 4 + core], e1r.at[index, 3], (near_x(dx), far_y, core))
            for index, (field, target, _) in enumerate(fields):
                send(field.at[:, pl.ds(ours, 8), :], target.at[pl.ds(4, 8), g, pl.ds(theirs, 8), :],
                     e1s.at[index, 2 + core], e1r.at[index, 2], (i, far_y, core))

    for index, (field, target, deep) in enumerate(fields):
        for dx in (1, -1):
            part = pl.ds(8 - deep, deep) if dx == 1 else pl.ds(0, deep)
            place = pl.ds(4 - deep, deep) if dx == 1 else pl.ds(12, deep)
            for core in range(2):
                send(field.at[part, pl.ds(8 * core, 24), :], target.at[place, g, pl.ds(16 - 8 * core, 24), :],
                     e1s.at[index, 0], e1r.at[index, 0], (near_x(dx), j, core))
    for index, (field, target, _) in enumerate(fields):
        send(field.at[:, pl.ds(pl.multiple_of(8 - 8 * g, 8), 24), :],
             target.at[pl.ds(4, 8), g, pl.ds(pl.multiple_of(8 + 8 * g, 8), 24), :],
             e1s.at[index, 1], e1r.at[index, 1], (i, j, 1 - g))
    def outside(edge, row):
        @pl.when(edge)
        def _():
            for field in (C, S):
                field[:, :, pl.ds(row, 8), :] = jnp.zeros((16, 2, 8, 128), F32)

    outside((j == 0) & (g == 0), 8)
    outside((j == n_gy - 1) & (g == 1), 32)

    def cells(layers, rows, tiles=2):
        return C.at[pl.ds(0, layers), pl.ds(0, tiles), pl.ds(0, rows), :]

    wait(beta.at[:, pl.ds(0, 24), :], local.at[0])
    wait(cells(8, 24, 1), e1r.at[0, 1])

    @pl.when(has_side)
    def _():
        wait(cells(8, 8), e1r.at[0, 2])

    def mid_coefficient(m, _):
        for t in range(2):
            RC[m, t] = C[4 + 2 * m, t, pl.ds(8, 32), :] + C[5 + 2 * m, t, pl.ds(8, 32), :]
            two = RC[m, t, pl.ds(0, 16, stride=2), :] + RC[m, t, pl.ds(1, 16, stride=2), :]
            MC[m + 3, t, pl.ds(8, 16), :] = 0.125 * pair_sum(two, 1)

    layers(0, 4, mid_coefficient)
    mid_rows = pl.ds(8, 16)
    send(MC.at[pl.ds(4, 3), :, mid_rows, :], MC.at[pl.ds(0, 3), :, mid_rows, :], mcs, mcr, (near_x(1), j, g))
    send(MC.at[pl.ds(3, 3), :, mid_rows, :], MC.at[pl.ds(7, 3), :, mid_rows, :], mcs, mcr, (near_x(-1), j, g))

    wait(src.at[:, pl.ds(0, 24), :], local.at[1])
    wait(cells(8, 24, 1), e1r.at[1, 1])

    @pl.when(has_side)
    def _():
        wait(cells(8, 8), e1r.at[1, 2])


    def fine_first(x, _):
        make_faces(x, C, fine, 8, 32, 1)
        for t in range(2):
            V1[x, t, pl.ds(8, 32), :] = E[x, t, pl.ds(8, 32), :] * (2.0 * S[x, t, pl.ds(8, 32), :])

    def fine_second(x, _):
        sweep(x, V1, V2, fine, S, 2.0, 8, 32, 1)

    layers(5, 11, fine_first)
    layers(6, 10, fine_second)

    pl.semaphore_wait(known.at[0], 2)

    @pl.when(has_side)
    def _():
        pl.semaphore_signal(known.at[1], inc=1, device_id=(i, near_y(side), 1 - g), device_id_type=MESH)

    wait(cells(6, 24), e1r.at[0, 0])

    @pl.when(has_side)
    def _():
        wait(cells(6, 8), e1r.at[0, 3])


    @pl.when(i == 0)
    def _():
        C[pl.ds(1, 3)] = jnp.zeros((3, *C.shape[1:]), F32)

    @pl.when(i == n_gx - 1)
    def _():
        C[pl.ds(12, 3)] = jnp.zeros((3, *C.shape[1:]), F32)

    wait(cells(4, 24), e1r.at[1, 0])

    @pl.when(has_side)
    def _():
        wait(cells(4, 8), e1r.at[1, 3])

    layers(2, 5, fine_first)
    layers(11, 14, fine_first)
    last_face(14, C, fine, 8, 32)
    layers(3, 6, fine_second)
    layers(10, 13, fine_second)
    fine_rows = pl.ds(8, 32)

    def fine_residual(m, _):
        lower = left_over(4 + 2 * m, V2, fine, S, 0.5, 8, 32, 1)
        upper = left_over(5 + 2 * m, V2, fine, S, 0.5, 8, 32, 1)
        for t in range(2):
            RS[m, t] = lower[t] + upper[t]
            two = RS[m, t, pl.ds(0, 16, stride=2), :] + RS[m, t, pl.ds(1, 16, stride=2), :]
            MS[m + 3, t, mid_rows, :] = 0.125 * pair_sum(two, 1)

    layers(0, 4, fine_residual)
    send(MS.at[pl.ds(5, 2), :, mid_rows, :], MS.at[pl.ds(1, 2), :, mid_rows, :], mss, msr, (near_x(1), j, g))
    send(MS.at[pl.ds(3, 2), :, mid_rows, :], MS.at[pl.ds(7, 2), :, mid_rows, :], mss, msr, (near_x(-1), j, g))

    def coarsest(field, scale):
        parts = []
        for layer in range(2):
            for t in range(2):
                R2[layer, t] = field(2 * layer, t) + field(2 * layer + 1, t)
                two = R2[layer, t, pl.ds(4, 4, stride=2), :] + R2[layer, t, pl.ds(5, 4, stride=2), :]
                parts.append(scale * pair_sum(two, 2))
        return braid(parts)

    own_target = jnp.full((4, 128), tgt[0, 0, 0].astype(F32), F32)
    ES[pl.ds(0, 4), :] = coarsest(lambda m, t: MC[3 + m, t, mid_rows, :], 0.125)
    ES[pl.ds(4, 4), :] = own_target
    EB[2 * NEAR + g] = ES[...]
    for d in (4, 3, 2, 1):
        for sign in (1, -1):
            for core in range(2):
                send(ES, EB.at[2 * (NEAR - sign * d) + g], ebs, ebr, (near_x(sign * d), j, core))
    send(ES, EB.at[2 * NEAR + g], ebss, ebsr, (i, j, 1 - g))

    wait(MC.at[pl.ds(0, 6), :, mid_rows, :], mcr)

    @pl.when(i == 0)
    def _():
        MC[pl.ds(0, 3)] = jnp.zeros((3, *MC.shape[1:]), F32)

    @pl.when(i == n_gx - 1)
    def _():
        MC[pl.ds(7, 3)] = jnp.zeros((3, *MC.shape[1:]), F32)

    def mid_first(x, _):
        make_faces(x, MC, mid, 8, 16, 2)

    layers(1, 9, mid_first)
    last_face(9, MC, mid, 8, 16)
    wait(MS.at[pl.ds(0, 4), :, mid_rows, :], msr)

    def mid_start(x, _):
        for t in range(2):
            M1[x, t, mid_rows, :] = ME[x, t, mid_rows, :] * (8.0 * MS[x, t, mid_rows, :])

    layers(1, 9, mid_start)

    def mid_second(x, _):
        sweep(x, M1, M2, mid, MS, 8.0, 8, 16, 2)

    layers(2, 8, mid_second)
    mid_res = [left_over(3 + m, M2, mid, MS, 0.125, 8, 16, 2) for m in range(4)]
    low_src = coarsest(lambda m, t: mid_res[m][t], 0.125)

    GS[...] = low_src
    GB[2 * NEAR + g] = low_src
    send(GS, GB.at[2 * NEAR + g], gss, gsr, (i, j, 1 - g))
    for d in (4, 3, 2, 1):
        for sign in (1, -1):
            for core in range(2):
                send(GS, GB.at[2 * (NEAR - sign * d) + g], gs, gr, (near_x(sign * d), j, core))
    wait(GB.at[0], gsr)

    wait(EB.at[0], ebsr)
    halves = [EB[2 * NEAR + core][4:5] for core in range(2)]
    TS[pl.ds(0, 1), :] = jnp.sum(low_src + GB[2 * NEAR + 1 - g], axis=0, keepdims=True)
    TS[pl.ds(1, 1), :] = jnp.where(lanes_of(1) % 2 == 0, halves[0], halves[1])

    @pl.when(has_side)
    def _():
        pl.semaphore_wait(known.at[1], 1)

    far_y = near_y(side)
    for d in sorted(range(NEAR + 1, n_gx - NEAR), key=lambda d: -min(d, n_gx - d)):
        slot = n_gx - d - NEAR - 1

        @pl.when(has_side)
        def _():
            send(TS, TB.at[slot], ts, tr, (near_x(d), far_y, 1 - g))

        send(TS, FB.at[slot], fs, fr, (near_x(d), j, g))

    for m in range(6):
        for t in range(2):
            SY[m, t] = M2[2 + m, t, pl.ds(12, 8), :]

    @pl.when(has_side)
    def _():
        send(SY, Y2.at[1 - g], ys.at[1], yr.at[1], (i, near_y(side), 1 - g))

    send(SY, Y2.at[g], ys.at[0], yr.at[0], (i, j, 1 - g))
    send(M2.at[pl.ds(4, 2), :, mid_rows, :], M2P.at[pl.ds(0, 2), :, mid_rows, :], xs, xr, (near_x(1), j, g))
    send(M2.at[pl.ds(4, 2), :, mid_rows, :], M2P.at[pl.ds(8, 2), :, mid_rows, :], xs, xr, (near_x(-1), j, g))

    wait(EB.at[pl.ds(0, 16)], ebr)
    lane = lanes_of(8)
    row = lax.broadcasted_iota(jnp.int32, (8, 128), 0)
    layer, tile, cell = (lane % 4) // 2, lane % 2, lane // 4
    boxes = 2 * NEAR + 1
    zero = jnp.zeros((8, 128), F32)
    coefs, marks = [], []
    for b in range(boxes):
        first, second = EB[2 * b], EB[2 * b + 1]
        coefs.append(jnp.concatenate([first[:4], second[:4]], axis=0))
        marks.append(jnp.where(tile == 0, jnp.broadcast_to(first[4:5], (8, 128)), jnp.broadcast_to(second[4:5], (8, 128))))
    joined = []
    for b in range(boxes - 1):
        touch = lax.rem(i + b - NEAR + n_gx, n_gx) != n_gx - 1
        joined.append(jnp.where((marks[b] == marks[b + 1]) & touch, 1.0, 0.0))

    def along_x(values):
        down = [pltpu.roll(v, 2, 1) for v in values]
        up = [pltpu.roll(v, 126, 1) for v in values]
        below, above = [], []
        for b in range(boxes):
            before = up[b - 1] * joined[b - 1] if b else zero
            after = down[b + 1] * joined[b] if b < boxes - 1 else zero
            below.append(jnp.where(layer == 0, before, down[b]))
            above.append(jnp.where(layer == 0, up[b], after))
        return below, above

    def along_yz(v):
        return (pltpu.roll(v, 1, 0), pltpu.roll(v, 7, 0), pltpu.roll(v, 4, 1), pltpu.roll(v, 124, 1))

    keeps = (row > 0, row < 7, cell > 0, cell < 31)
    c_below, c_above = along_x(coefs)
    low_faces, low_ease = [], []
    for b in range(boxes):
        c = coefs[b]
        around = [jnp.where(keep, v, 0.0) for keep, v in zip(keeps, along_yz(c))]
        faces = [c + c_below[b], c + c_above[b]] + [c + v for v in around]
        total = faces[0] + faces[1] + faces[2] + faces[3] + faces[4] + faces[5]
        low_faces.append(faces[:2] + [jnp.where(keep, f, 0.0) for keep, f in zip(keeps, faces[2:])])
        low_ease.append(RELAX / total)

    def solve(low, rhs, sweeps):
        for number in range(sweeps):
            below, above = along_x(low)
            fresh = []
            for b in range(boxes):
                around = [below[b], above[b], *along_yz(low[b])]
                total = low_faces[b][0] * around[0]
                for face, value in zip(low_faces[b][1:], around[1:]):
                    total = total + face * value
                if rhs is not None:
                    total = total + 32.0 * rhs[b]
                fresh.append(0.2 * low[b] + low_ease[b] * total)
            low = fresh
        return low[NEAR - 1:NEAR + 2]

    from_mean = solve([jnp.full((8, 128), 4.0, F32)] * boxes, None, BOTTOM)
    wait(GB.at[pl.ds(0, 16)], gr)
    rhs = [jnp.concatenate([GB[2 * b], GB[2 * b + 1]], axis=0) for b in range(boxes)]
    from_source = solve([low_ease[b] * (32.0 * rhs[b]) for b in range(boxes)], rhs, BOTTOM - 1)
    sums = [jnp.sum(v, axis=0, keepdims=True) for v in rhs]
    for b in range(3):
        SQ[b] = from_source[b]
        SQ[3 + b] = from_mean[b]
    for b in range(boxes):
        SQ[6 + b // 8, pl.ds(b % 8, 1), :] = sums[b]
        SQ[8 + b // 8, pl.ds(b % 8, 1), :] = marks[b][:1]

    @pl.when(has_side)
    def _():
        send(SQ, QP, qs, qr, (i, near_y(side), 1 - g))

    send(V2.at[10, :, fine_rows, :], V2.at[2, :, fine_rows, :], vs, vr.at[0], (near_x(1), j, g))
    send(V2.at[5, :, fine_rows, :], V2.at[13, :, fine_rows, :], vs, vr.at[1], (near_x(-1), j, g))

    for m in range(6):
        for t in range(2):
            M2P[2 + m, t, mid_rows, :] = M2[2 + m, t, mid_rows, :]
    wait(Y2.at[0], yr.at[0])

    @pl.when(has_side)
    def _():
        wait(Y2.at[0], yr.at[1])

    for m in range(6):
        for t in range(2):
            M2P[2 + m, t, pl.ds(9, 1), :] = Y2[0, m, t, pl.ds(5, 1), :]
            M2P[2 + m, t, pl.ds(22, 1), :] = Y2[1, m, t, pl.ds(2, 1), :]
    names = [m[:1] for m in marks]
    src_lane = lax.broadcasted_iota(jnp.int32, (128, 128), 0)
    dst_lane = lax.broadcasted_iota(jnp.int32, (128, 128), 1)
    same_tile = jnp.where(src_lane % 2 == dst_lane % 2, 1.0, 0.0).astype(F32)

    wait(FB, fr)
    for d in range(n_gx - boxes):
        sums.append(FB[d][:1])
        names.append(FB[d][1:])
    @pl.when(has_side)
    def _():
        wait(TB, tr)
        wait(SQ, qr)

    for b in range(boxes):
        sums.append(QP[6 + b // 8, pl.ds(b % 8, 1), :])
        names.append(QP[8 + b // 8, pl.ds(b % 8, 1), :])
    for d in range(n_gx - boxes):
        sums.append(TB[d][:1])
        names.append(TB[d][1:])
    sums = exact_dot(jnp.concatenate(sums, axis=0), same_tile)
    names = jnp.concatenate(names, axis=0)

    def means(first):
        row_sums, row_names = sums[first:first + n_gx], names[first:first + n_gx]
        for place in (NEAR - 1, NEAR, NEAR + 1):
            same = row_names == row_names[place:place + 1]
            total = jnp.sum(jnp.where(same, row_sums, 0.0), axis=0, keepdims=True)
            number = jnp.sum(jnp.where(same, 512.0, 0.0), axis=0, keepdims=True)
            yield total / jnp.maximum(number, 1.0)

    side_at = pl.ds(pl.multiple_of(16 * g, 8), 8)
    for b, mean in enumerate(means(0)):
        Q[b, pl.ds(8, 8), :] = from_source[b] + mean * from_mean[b]
    for b, mean in enumerate(means(n_gx)):
        Q[b, side_at, :] = QP[b] + mean * QP[3 + b]

    wait(M2P.at[pl.ds(0, 4), :, mid_rows, :], xr)

    for b in range(3):
        fix = jnp.where(g == 0, Q[b, pl.ds(6, 8), :], Q[b, pl.ds(10, 8), :])
        for part, wide in enumerate(unbraid(fix)):
            PK[2 * b + part // 2, part % 2, pl.ds(0, 8, stride=2), :] = wide
            PK[2 * b + part // 2, part % 2, pl.ds(1, 8, stride=2), :] = wide

    def corrected(x, _):
        for t in range(2):
            better = M2P[x, t, mid_rows, :] + PK[(x + 1) // 2, t]
            M3[x, t, mid_rows, :] = jnp.where(MC[x, t, mid_rows, :] > 0.0, better, 0.0)

    layers(0, 10, corrected)

    def mid_third(x, _):
        sweep(x, M3, M4, mid, MS, 8.0, 8, 16, 2)

    layers(1, 9, mid_third)
    wait(V2.at[0, :, fine_rows, :], vr.at[0])
    wait(V2.at[0, :, fine_rows, :], vr.at[1])

    def mid_fourth(x, _):
        sweep(x, M4, M1, mid, MS, 8.0, 8, 16, 2)
        for t in range(2):
            PF[x - 2, t, pl.ds(0, 16, stride=2), :] = M1[x, t, mid_rows, :]
            PF[x - 2, t, pl.ds(1, 16, stride=2), :] = M1[x, t, mid_rows, :]
            for half in range(2):
                V3[2 * x - 2 + half, t, fine_rows, :] = V2[2 * x - 2 + half, t, fine_rows, :] + PF[x - 2, t]

    layers(2, 8, mid_fourth)

    def fine_third(x, _):
        sweep(x, V3, V1, fine, S, 2.0, 15, 18, 1)

    layers(3, 13, fine_third)

    def fine_fourth(x, _):
        at = pl.ds(16, 16)
        sums, own = pull(x, V1, fine, 16, 16, 1)
        for t in range(2):
            FO[x - 4, t] = 0.2 * own[t] + E[x, t, at, :] * (2.0 * S[x, t, at, :] + sums[t])

    layers(4, 12, fine_fourth)

    out_rows = pl.ds(pl.multiple_of(16 * g, 8), 16)
    send(FO.at[:, 1 - g], out.at[:, out_rows, :], os_, or_, (i, j, 1 - g))
    keep = pltpu.make_async_copy(FO.at[:, g], out.at[:, out_rows, :], local.at[2])
    keep.start()

    for index, deep in ((0, 3), (1, 2)):
        wait(cells(2 * deep, 24), e1s.at[index, 0])
        wait(cells(8, 24, 1), e1s.at[index, 1])
    for core, there in ((0, up), (1, down)):

        @pl.when(there)
        def _():
            for index, deep in ((0, 3), (1, 2)):
                wait(cells(8, 8, 1), e1s.at[index, 2 + core])
                wait(cells(2 * deep, 8, 1), e1s.at[index, 4 + core])

    wait(V2.at[pl.ds(0, 2), :, fine_rows, :], vs)
    wait(MC.at[pl.ds(0, 6), :, mid_rows, :], mcs)
    wait(MS.at[pl.ds(0, 4), :, mid_rows, :], mss)
    wait(EB.at[pl.ds(0, 16)], ebs)
    wait(EB.at[0], ebss)
    wait(GB.at[pl.ds(0, 16)], gs)
    wait(GB.at[0], gss)
    wait(FB, fs)
    wait(Y2.at[0], ys.at[0])
    wait(M2P.at[pl.ds(0, 4), :, mid_rows, :], xs)

    @pl.when(has_side)
    def _():
        wait(Y2.at[0], ys.at[1])
        wait(SQ, qs)
        wait(TB, ts)

    keep.wait()
    wait(FO.at[:, 0], os_)
    wait(out.at[:, pl.ds(0, 16), :], or_)


def solution(mesh):
    n_gx, n_gy = mesh.shape["gx"], mesh.shape["gy"]

    def kernel(*refs):
        cycle(n_gx, n_gy, *refs)

    def per_device(source, beta_cells, target):
        fine = pltpu.VMEM((16, 2, 48, 128), F32)
        mid = pltpu.VMEM((10, 2, 32, 128), F32)
        far = n_gx - 2 * NEAR - 1
        dma = pltpu.SemaphoreType.DMA
        return pl.pallas_call(
            kernel,
            out_shape=jax.ShapeDtypeStruct(source.shape, F32),
            in_specs=[
                pl.BlockSpec(memory_space=pltpu.HBM),
                pl.BlockSpec(memory_space=pltpu.HBM),
                pl.BlockSpec(memory_space=pltpu.SMEM),
            ],
            out_specs=pl.BlockSpec(memory_space=pl.ANY),
            scratch_shapes=[
                *[fine] * 11,
                *[mid] * 13,
                pltpu.VMEM((4, 2, 32, 128), F32),
                pltpu.VMEM((4, 2, 32, 128), F32),
                pltpu.VMEM((2, 2, 16, 128), F32),
                pltpu.VMEM((6, 2, 8, 128), F32),
                pltpu.VMEM((2, 6, 2, 8, 128), F32),
                pltpu.VMEM((8, 128), F32),
                pltpu.VMEM((4 * NEAR + 2, 8, 128), F32),
                pltpu.VMEM((8, 128), F32),
                pltpu.VMEM((4 * NEAR + 2, 4, 128), F32),
                pltpu.VMEM((4, 128), F32),
                pltpu.VMEM((far, 2, 128), F32),
                pltpu.VMEM((3, 24, 128), F32),
                pltpu.VMEM((10, 8, 128), F32),
                pltpu.VMEM((6, 2, 16, 128), F32),
                pltpu.VMEM((6, 2, 32, 128), F32),
                pltpu.VMEM((8, 2, 16, 128), F32),
                dma((3,)),
                dma((2, 6)),
                dma((2, 4)),
                *[dma] * 10,
                dma((2,)),
                dma((2,)),
                *[dma] * 7,
                dma((2,)),
                *[dma] * 6,
                pltpu.VMEM((2, 128), F32),
                pltpu.VMEM((far, 2, 128), F32),
                pltpu.VMEM((10, 8, 128), F32),
                pltpu.SemaphoreType.REGULAR((2,)),
            ],
            compiler_params=pltpu.CompilerParams(
                collective_id=0, has_side_effects=True, vmem_limit_bytes=32 * 2**20
            ),
            name="cycle",
        )(source, beta_cells, target)

    spec = P("gx", "gy", "gz")
    return jax.shard_map(
        per_device, mesh=mesh, in_specs=(spec, spec, spec), out_specs=spec, check_vma=False
    )
```
